32 devices in a mesh: seq: 8 (over z, x), blk: 4 (over y, core).
Axes of the slice: x: 2, y: 2, z: 4, core: 2. Of those that a mesh axis runs over, the one named last changes fastest.
Arguments:
- tokens: bfloat16 [16, 256, 768], P('seq', 'blk'), may hold values from -6 to 6
- ln1_gain: bfloat16 [768], replicated, may hold values from 0.099609375 to 1.8984375
- ln1_bias: bfloat16 [768], replicated, may hold values from -1.75 to 1.75
- query_key_value_weight: bfloat16 [768, 2304], replicated, may hold values from -0.21875 to 0.21875
- bias_qv: bfloat16 [1536], replicated, may hold values from -3 to 3
- output_weight: bfloat16 [768, 768], replicated, may hold values from -0.875 to 0.875
- output_bias: bfloat16 [768], replicated, may hold values from -1.75 to 1.75
- ln2_gain: bfloat16 [768], replicated, may hold values from 0.099609375 to 1.8984375
- ln2_bias: bfloat16 [768], replicated, may hold values from -1.75 to 1.75
- up_weight: bfloat16 [768, 3072], replicated, may hold values from -0.21875 to 0.21875
- up_bias: bfloat16 [3072], replicated, may hold values from -3 to 3
- down_weight: bfloat16 [3072, 768], replicated, may hold values from -0.109375 to 0.109375
- down_bias: bfloat16 [768], replicated, may hold values from -1.75 to 1.75
- segment_ids: int32 [16, 256], P('seq'), may hold values from 0 to 7, as said below
- block_output_gradient: bfloat16 [16, 256, 768], P('seq', 'blk'), may hold values from -6 to 6
Outputs:
- block_out: bfloat16 [16, 256, 768], P('seq', 'blk')
- in_grad: bfloat16 [16, 256, 768], P('seq', 'blk')
- grad_ln1_gain: float32 [768], P('seq')
- grad_ln1_bias: float32 [768], P('seq')
- grad_w_qkv: float32 [768, 2304], P('seq')
- grad_bias_qv: float32 [1536], P('seq')
- grad_w_out: float32 [768, 768], P('seq')
- grad_bias_out: float32 [768], P('seq')
- grad_ln2_gain: float32 [768], P('seq')
- grad_ln2_bias: float32 [768], P('seq')
- grad_w_up: float32 [768, 3072], P('seq')
- grad_bias_up: float32 [3072], P('seq')
- grad_w_down: float32 [3072, 768], P('seq')
- grad_bias_down: float32 [768], P('seq')
The draws below stay inside these ranges and needn't reach their ends.
Inputs may be any that keep to these rules, and one draw needn't show every extreme that they name: `segment_ids`: each sequence's crop numbers start at 0 at its first patch and never fall; a patch attends to the patches of its own crop in its own sequence. Among each index of seq's 2 sequences, one has a crop that runs from patch 3 * (8) to patch 256 - 256 // 8 - 1.
All inputs are finite; a program needn't handle non-finite values.
Results may differ from the reference program's by a relative error of at most 0.015.
Values may be sent and summed in bfloat16 or wider, within the bound.
No kernel may reach another device: no remote copies, remote signals or barrier semaphores. Data moves between devices by JAX's collectives and lax.ppermute only.
A program may use at most 128 MiB of HBM per device.

```python
import math
import jax
import jax.numpy as jnp
from jax import lax

D = 768
HEADS = 12
HEAD_DIM = 64
FF = 3072
LEN = 256
SEQ_DEV = 2
SEQS = 16


def draw_segment_ids(key, part):
    key = jax.random.fold_in(key, 7)
    key_cut, key_pick, key_head, key_tail = jax.random.split(key, 4)
    flags = (jax.random.randint(key_cut, (SEQS, LEN), 0, 24) == 0).astype(jnp.int32)
    position = jnp.arange(LEN, dtype=jnp.int32)[None, :]
    flags = jnp.where(position == 0, 0, flags)
    picked = jax.random.randint(key_pick, (SEQS // SEQ_DEV,), 0, SEQ_DEV)
    chosen = jnp.arange(SEQS, dtype=jnp.int32) % SEQ_DEV == jnp.repeat(picked, SEQ_DEV)
    margin_cells = LEN // 8
    crop_start = 3 * (margin_cells // 4)
    tail_start = LEN - margin_cells
    head_marks = jax.random.randint(key_head, (SEQS, 2), 1, crop_start)
    tail_marks = jax.random.randint(key_tail, (SEQS, 2), tail_start + 1, LEN)
    head_cuts = (position == head_marks[:, 0:1]) | (position == head_marks[:, 1:2]) | (position == crop_start)
    tail_cuts = (position == tail_start) | (position == tail_marks[:, 0:1]) | (position == tail_marks[:, 1:2])
    chosen_flags = (head_cuts | tail_cuts).astype(jnp.int32)
    flags = jnp.where(chosen[:, None], chosen_flags, flags)
    return jnp.minimum(jnp.cumsum(flags, axis=1), 7).astype(jnp.int32)


def block_levels(stream_key, dims, pieces, smallest, high):
    factor_of, own = 1.0, jax.random.fold_in(stream_key, 6)
    for axis_at, parts in pieces:
        heights = jnp.exp(jax.random.uniform(jax.random.fold_in(own, axis_at), (parts,), jnp.float32, smallest / len(pieces), high / len(pieces)))
        factor_of = factor_of * jnp.repeat(heights, dims[axis_at] // parts).reshape([-1 if axis == axis_at else 1 for axis in range(len(dims))])
    return factor_of


def centred(key, shape, deviation, limit, shards=(), kind=jnp.bfloat16):
    drawn = jax.random.normal(key, shape, jnp.float32) * deviation
    if len(shards) > 0:
        drawn = block_levels(key, shape, shards, -0.22, 0.18) * drawn
    return jnp.clip(drawn, min=-limit, max=limit).astype(kind)


def setup_inputs(seed: int = 0) -> dict:
    arg_keys = jax.random.split(jax.random.key(seed), 16)
    tokens = centred(arg_keys[0], (SEQS, LEN, D), 1.0, 6.0, ((0, 8), (1, 4)))
    ln1_gain = jnp.clip(1.0 + 0.18 * jax.random.normal(arg_keys[1], (D,), jnp.float32), 0.099609375, 1.8984375).astype(jnp.bfloat16)
    ln1_bias = centred(arg_keys[2], (D,), 0.3, 1.75)
    query_key_value_weight = centred(arg_keys[3], (D, 3 * D), D ** -0.5, 0.21875)
    bias_qv = centred(arg_keys[4], (2 * D,), 0.5, 3.0)
    output_weight = centred(arg_keys[5], (D, D), (D // 16) ** -0.5, 0.875)
    output_bias = centred(arg_keys[6], (D,), 0.3, 1.75)
    ln2_gain = jnp.clip(1.0 + 0.18 * jax.random.normal(arg_keys[7], (D,), jnp.float32), 0.099609375, 1.8984375).astype(jnp.bfloat16)
    ln2_bias = centred(arg_keys[8], (D,), 0.3, 1.75)
    up_weight = centred(arg_keys[9], (D, FF), D ** -0.5, 0.21875)
    up_bias = centred(arg_keys[10], (FF,), 0.5, 3.0)
    down_weight = centred(arg_keys[11], (FF, D), FF ** -0.5, 0.109375)
    down_bias = centred(arg_keys[12], (D,), 0.3, 1.75)
    segment_ids = draw_segment_ids(jax.random.fold_in(arg_keys[15], 71), 0)
    block_output_gradient = centred(arg_keys[14], (SEQS, LEN, D), 1.0, 6.0, ((0, 8), (1, 4)))
    return {"tokens": tokens, "ln1_gain": ln1_gain, "ln1_bias": ln1_bias, "query_key_value_weight": query_key_value_weight, "bias_qv": bias_qv, "output_weight": output_weight, "output_bias": output_bias, "ln2_gain": ln2_gain, "ln2_bias": ln2_bias, "up_weight": up_weight, "up_bias": up_bias, "down_weight": down_weight, "down_bias": down_bias, "segment_ids": segment_ids, "block_output_gradient": block_output_gradient}


@jax.custom_vjp
def low(v):
    return lax.optimization_barrier(v.astype(jnp.bfloat16)).astype(jnp.float32)

@jax.custom_vjp
def reduced_backward(v):
    return v

def low_keep(v):
    return (low(v), None)

def low_pass(kept, grad):
    return (grad,)

def back_keep(v):
    return (v, None)

def back_low(kept, grad):
    return (low(grad),)
low.defvjp(low_keep, low_pass)
reduced_backward.defvjp(back_keep, back_low)
epsilon = 1e-06
highest_precision = lax.Precision.HIGHEST

def normalize(values, gain_vec, shift_vec):
    row_mean = lax.optimization_barrier(jnp.mean(values, axis=-1, keepdims=True))
    centered = values - row_mean
    row_var = lax.optimization_barrier(jnp.mean(centered * centered, axis=-1, keepdims=True))
    return centered * lax.rsqrt(row_var + epsilon) * gain_vec + shift_vec

def layer(inputs, ln1_gain, ln1_bias, query_key_value_weight, bias_qv, output_weight, output_bias, ln2_gain, ln2_bias, up_weight, up_bias, down_weight, down_bias, crop_ids):
    group_count, seq_length, model_width = inputs.shape
    score_scale = 1.0 / math.sqrt(HEAD_DIM)
    first_normed_input = low(normalize(inputs, ln1_gain, ln1_bias))
    projected_output = jnp.einsum('gft,tx->gfx', first_normed_input, query_key_value_weight, precision=highest_precision)
    queries = reduced_backward(low(projected_output[..., :model_width] + bias_qv[:model_width]))
    keys_local = reduced_backward(low(projected_output[..., model_width:2 * model_width]))
    values_local = reduced_backward(low(projected_output[..., 2 * model_width:] + bias_qv[model_width:]))
    head_shape = (group_count, seq_length, HEADS, HEAD_DIM)
    raw_scores = jnp.einsum('sqhe,skhe->shqk', queries.reshape(head_shape), keys_local.reshape(head_shape), precision=highest_precision)
    scores = reduced_backward(raw_scores * score_scale)
    same_crop = crop_ids[:, :, None] == crop_ids[:, None, :]
    scores = jnp.where(same_crop[:, None], scores, -1000000000.0)
    probs = low(jax.nn.softmax(scores, axis=-1))
    attended_values = jnp.einsum('shqk,skhe->sqhe', probs, values_local.reshape(head_shape), precision=highest_precision)
    attended_values = reduced_backward(low(attended_values.reshape(group_count, seq_length, model_width)))
    residual_branch = reduced_backward(jnp.einsum('gft,tx->gfx', attended_values, output_weight, precision=highest_precision) + output_bias)
    hidden_state = inputs + residual_branch
    second_normed_input = low(normalize(hidden_state, ln2_gain, ln2_bias))
    up_projection = reduced_backward(jnp.einsum('bpm,mv->bpv', second_normed_input, up_weight, precision=highest_precision) + up_bias)
    active_mask = low(jax.nn.gelu(up_projection))
    return hidden_state + (jnp.einsum('nuo,ow->nuw', active_mask, down_weight, precision=highest_precision) + down_bias)

def reference(tokens, ln1_gain, ln1_bias, query_key_value_weight, bias_qv, output_weight, output_bias, ln2_gain, ln2_bias, up_weight, up_bias, down_weight, down_bias, segment_ids, block_output_gradient):
    params = tuple((param.astype(jnp.float32) for param in (ln1_gain, ln1_bias, query_key_value_weight, bias_qv, output_weight, output_bias, ln2_gain, ln2_bias, up_weight, up_bias, down_weight, down_bias)))
    group_size = math.gcd(SEQS, 16)
    block_count = SEQS // group_size

    def one_block(running, block_index):
        row_start = (block_index * group_size).astype(jnp.int32)
        block_in = lax.dynamic_slice_in_dim(tokens, row_start, group_size, 0).astype(jnp.float32)
        crop_ids = lax.dynamic_slice_in_dim(segment_ids, row_start, group_size, 0)
        cotangent = lax.dynamic_slice_in_dim(block_output_gradient, row_start, group_size, 0).astype(jnp.float32)

        def forward_pass(block_values, *weights):
            return layer(block_values, *weights, crop_ids)
        result, pullback = jax.vjp(forward_pass, block_in, *params)
        gradients = pullback(cotangent)
        running = tuple((acc_sum + new_sum for acc_sum, new_sum in zip(running, gradients[1:])))
        return (running, (result.astype(jnp.bfloat16), gradients[0].astype(jnp.bfloat16)))
    zero_sums = tuple((jnp.zeros_like(param) for param in params))
    totals, (outputs, in_grads) = lax.scan(one_block, zero_sums, jnp.arange(block_count, dtype=jnp.int32))
    outputs = outputs.reshape(SEQS, LEN, D)
    in_grads = in_grads.reshape(SEQS, LEN, D)
    return (outputs, in_grads, totals[0], totals[1], totals[2], totals[3], totals[4], totals[5], totals[6], totals[7], totals[8], totals[9], totals[10], totals[11])
```

```python
import jax
import jax.numpy as jnp
from jax import lax
from jax.experimental import pallas as pl
from jax.experimental.pallas import tpu as pltpu
from jax.sharding import PartitionSpec as P

HEADS = 12
EPS = 1e-06
SLOTS = 8
F32 = jnp.float32
BF16 = jnp.bfloat16
GELU_C = 0.7978845608028654
GELU_A = 0.044715
PARAMS = pltpu.CompilerParams(vmem_limit_bytes=56 * 1024 * 1024)
GRID_PARAMS = pltpu.CompilerParams(
    vmem_limit_bytes=56 * 1024 * 1024, dimension_semantics=("arbitrary",)
)


def nn(a, b):
    return lax.dot_general(a, b, (((1,), (0,)), ((), ())), preferred_element_type=F32)


def nt(a, b):
    return lax.dot_general(a, b, (((1,), (1,)), ((), ())), preferred_element_type=F32)


def tn(a, b):
    return lax.dot_general(a, b, (((0,), (0,)), ((), ())), preferred_element_type=F32)


def standardize(x):
    centered = x - jnp.mean(x, axis=-1, keepdims=True)
    rstd = lax.rsqrt(jnp.mean(centered * centered, axis=-1, keepdims=True) + EPS)
    return centered * rstd, rstd


def norm_back(xhat, rstd, g):
    return rstd * (
        g
        - jnp.mean(g, axis=-1, keepdims=True)
        - xhat * jnp.mean(g * xhat, axis=-1, keepdims=True)
    )


def half_masks():
    lane = lax.broadcasted_iota(jnp.int32, (1, 128), 1)
    low = jnp.where(lane < 64, 1.0, 0.0)
    return low.astype(BF16), (1.0 - low).astype(BF16)


def crop_mask(seg_row):
    wide = jnp.broadcast_to(seg_row, (256, 256))
    return jnp.where(wide == wide.T, 1.0, 0.0)


def softmax_rows(scores, same):
    scores = jnp.where(same > 0.0, scores, -1e9)
    e = jnp.exp(scores - jnp.max(scores, axis=-1, keepdims=True))
    return e * (1.0 / jnp.sum(e, axis=-1, keepdims=True))


def forward_kernel(
    seg, t0, t1, t2, t3, pv, wqkv_hbm, wout_hbm,
    first_o, q_o, k_o, v_o, att_o, hid_o, sec_o,
    wqkv, wout, same, sem,
):
    load_qkv = pltpu.make_async_copy(wqkv_hbm, wqkv, sem.at[0])
    load_out = pltpu.make_async_copy(wout_hbm, wout, sem.at[1])
    load_qkv.start()
    load_out.start()
    for s in range(2):
        for p, t in enumerate((t0, t1, t2, t3)):
            xhat, _ = standardize(t[s].astype(F32))
            first_o[pl.ds(s * 256 + p * 64, 64), :] = (xhat * pv[0:1, :] + pv[1:2, :]).astype(BF16)
        same[s] = crop_mask(seg[s : s + 1, :])
    load_qkv.wait()
    for half in range(2):
        cols = pl.ds(half * 384, 384)
        q_o[:, cols] = (
            nn(first_o[...], wqkv[:, half * 384 : half * 384 + 384]) + pv[2:3, cols]
        ).astype(BF16) * BF16(0.125)
        k_o[:, cols] = nn(
            first_o[...], wqkv[:, 768 + half * 384 : 768 + half * 384 + 384]
        ).astype(BF16)
        v_o[:, cols] = (
            nn(first_o[...], wqkv[:, 1536 + half * 384 : 1536 + half * 384 + 384]) + pv[3:4, cols]
        ).astype(BF16)
    low, high = half_masks()

    def one_sequence(s, _):
        rows = pl.ds(pl.multiple_of(s * 256, 256), 256)
        for j in range(HEADS // 2):
            cols = pl.ds(j * 128, 128)
            q, k, v = q_o[rows, cols], k_o[rows, cols], v_o[rows, cols]
            out = None
            for keep in (low, high):
                probs = softmax_rows(nt(q * keep, k), same[s]).astype(BF16)
                part = nn(probs, v * keep)
                out = part if out is None else out + part
            att_o[rows, cols] = out.astype(BF16)
        return 0

    lax.fori_loop(0, 2, one_sequence, 0)
    load_out.wait()
    for s in range(2):
        for p, t in enumerate((t0, t1, t2, t3)):
            rows = pl.ds(s * 256 + p * 64, 64)
            hid = t[s].astype(F32) + (nn(att_o[rows, :], wout[...]) + pv[4:5, :])
            hid_o[rows, :] = hid
            xhat, _ = standardize(hid)
            sec_o[rows, :] = (xhat * pv[5:6, :] + pv[6:7, :]).astype(BF16)


def forward(seg, pieces, pv, wqkv, wout):
    bf = jax.ShapeDtypeStruct((512, 768), BF16)
    vmem = pl.BlockSpec(memory_space=pltpu.VMEM)
    hbm = pl.BlockSpec(memory_space=pl.ANY)
    return pl.pallas_call(
        forward_kernel,
        out_shape=(bf, bf, bf, bf, bf, jax.ShapeDtypeStruct((512, 768), F32), bf),
        in_specs=[vmem] * 6 + [hbm] * 2,
        out_specs=[vmem] * 7,
        scratch_shapes=[
            pltpu.VMEM((768, 2304), BF16),
            pltpu.VMEM((768, 768), BF16),
            pltpu.VMEM((2, 256, 256), F32),
            pltpu.SemaphoreType.DMA((2,)),
        ],
        compiler_params=PARAMS,
        name="forward",
    )(seg, *pieces, pv, wqkv, wout)


def own_rows(ref):
    return jnp.concatenate([ref[0:64, :], ref[256:320, :]], axis=0)


def gather_dy(pieces, dy):
    for s in range(2):
        for p, t in enumerate(pieces):
            dy[pl.ds(s * 256 + p * 64, 64), :] = t[s]


def pick_rows(transposed, chosen, core):
    for s in range(SLOTS):
        chosen[pl.ds(s * 48, 48), :] = transposed[pl.ds(pl.multiple_of(s * 96 + core * 48, 16), 48), :]


def put_slots(x_bit, product, keep, send, offset):
    tiles = product.shape[1] // 128
    for s in range(SLOTS):
        for t in range(tiles):
            value = product[s * 48 : s * 48 + 48, t * 128 : t * 128 + 128]
            rows = pl.ds(offset + t * 48, 48)

            @pl.when(x_bit == s % 2)
            def _():
                keep[s // 2, rows, :] = value

            @pl.when(x_bit != s % 2)
            def _():
                send[s // 2, rows, :] = value


def feed_step(ids, i, sec, dy, wup, bup, wdown, act_t, down_keep, down_send, act_own):
    y_bit, core, x_bit = ids[0], ids[1], ids[2]
    up = nn(sec[...], wup[...]) + bup[...]
    da = nt(dy[...], wdown[...])
    square = up * up
    tanh = jnp.tanh(GELU_C * up * (1.0 + GELU_A * square))
    cdf = 0.5 * (1.0 + tanh)
    act = (up * cdf).astype(BF16)
    slope = cdf + (0.5 * GELU_C) * up * (1.0 - tanh * tanh) * (1.0 + (3.0 * GELU_A) * square)
    dup = (da * slope).astype(BF16)
    act_t[...] = act.T
    dy_half = dy[:, pl.ds(pl.multiple_of(y_bit * 384, 128), 384)]
    mine = act_t[pl.ds(pl.multiple_of(core * 192, 64), 192), :]
    product = nn(mine, dy_half).astype(BF16)

    @pl.when(x_bit == lax.rem(i, 2))
    def _():
        for t in range(3):
            down_keep[0, pl.ds(t * 192, 192), :] = product[:, t * 128 : t * 128 + 128]

    @pl.when(x_bit != lax.rem(i, 2))
    def _():
        for t in range(3):
            down_send[0, pl.ds(t * 192, 192), :] = product[:, t * 128 : t * 128 + 128]

    act_own[0:64, :] = act[0:64, :]
    act_own[64:128, :] = act[256:320, :]
    bias = jnp.sum(dup[0:64, :].astype(F32), axis=0, keepdims=True) + jnp.sum(
        dup[256:320, :].astype(F32), axis=0, keepdims=True
    )
    return dup, bias


def feed_a_kernel(
    ids, sec, d0, d1, d2, d3, wup, bup, wdown,
    up_keep, up_send, down_keep, down_send, dsec, out_own, bias_o,
    dy, act_t, act_own, sec_t, chosen,
):
    i = pl.program_id(0)

    @pl.when(i == 0)
    def _():
        gather_dy((d0, d1, d2, d3), dy)
        sec_t[...] = sec[...].T
        pick_rows(sec_t, chosen, ids[1])
        dsec[...] = jnp.zeros_like(dsec)
        out_own[...] = jnp.zeros_like(out_own)

    dup, bias = feed_step(ids, i, sec, dy, wup, bup, wdown, act_t, down_keep, down_send, act_own)
    bias_o[...] = bias
    product = nn(chosen[...], dup).astype(BF16)
    put_slots(ids[2], product, up_keep, up_send, 0)
    dsec[...] += nt(dup, wup[...])
    out_own[...] += nn(act_own[...], wdown[...])


def feed_b_kernel(
    ids, sec, d0, d1, d2, d3, wup, bup, wdown, keep_in, send_in, dsec_in, own_in, hid, pv,
    down_keep, down_send, bias_o, dh_o, dhid_own, block_o, sums_o,
    dy, act_t, act_own, dsec, out_own,
):
    i = pl.program_id(0)

    @pl.when(i == 0)
    def _():
        gather_dy((d0, d1, d2, d3), dy)
        dsec[...] = dsec_in[...]
        out_own[...] = own_in[...]

    dup, bias = feed_step(ids, i, sec, dy, wup, bup, wdown, act_t, down_keep, down_send, act_own)
    bias_o[...] = bias
    dsec[...] += nt(dup, wup[...])
    out_own[...] += nn(act_own[...], wdown[...])

    @pl.when(i == 3)
    def _():
        for s in range(2):
            block_o[s] = (
                hid[pl.ds(s * 256, 64), :] + (out_own[pl.ds(s * 64, 64), :] + pv[7:8, :])
            ).astype(BF16)
        sums = [jnp.zeros((1, 768), F32)] * 4
        for s in range(2):
            for p in range(4):
                rows = pl.ds(s * 256 + p * 64, 64)
                xhat, rstd = standardize(hid[rows, :])
                dy_rows = dy[rows, :].astype(F32)
                grad = dsec[rows, :]
                dhid = dy_rows + norm_back(xhat, rstd, grad * pv[5:6, :])
                low = dhid.astype(BF16)
                dh_o[rows, :] = low
                if p == 0:
                    dhid_own[pl.ds(s * 64, 64), :] = dhid
                    parts = (grad * xhat, grad, low.astype(F32), dy_rows)
                    sums = [a + jnp.sum(b, axis=0, keepdims=True) for a, b in zip(sums, parts)]
        for r in range(4):
            sums_o[r : r + 1, :] = sums[r]
        sums_o[4:8, :] = jnp.zeros((4, 768), F32)


def whole_spec(shape):
    return pl.BlockSpec(shape, lambda i, ids: (0,) * len(shape))


def weight_specs(flip):
    def chunk(i, ids):
        y_bit = 1 - ids[0] if flip else ids[0]
        return y_bit * 4 + i

    return [
        pl.BlockSpec((768, 384), lambda i, ids: (0, chunk(i, ids))),
        pl.BlockSpec((1, 384), lambda i, ids: (0, chunk(i, ids))),
        pl.BlockSpec((384, 768), lambda i, ids: (chunk(i, ids), 0)),
    ]


def down_spec(flip):
    def place(i, ids):
        y_bit = 1 - ids[0] if flip else ids[0]
        return (y_bit * 2 + i // 2, 0, 0)

    return pl.BlockSpec((1, 576, 128), place)


def feed_a(ids, sec, dys, wup, bup, wdown):
    part = jax.ShapeDtypeStruct((4, 576, 128), BF16)
    slot_spec = pl.BlockSpec((4, 144, 128), lambda i, ids: (0, i, 0))
    return pl.pallas_call(
        feed_a_kernel,
        grid_spec=pltpu.PrefetchScalarGridSpec(
            num_scalar_prefetch=1,
            grid=(4,),
            in_specs=[whole_spec((512, 768))] + [whole_spec((2, 64, 768))] * 4 + weight_specs(False),
            out_specs=[
                slot_spec, slot_spec, down_spec(False), down_spec(False),
                whole_spec((512, 768)), whole_spec((128, 768)),
                pl.BlockSpec((1, 384), lambda i, ids: (0, i)),
            ],
            scratch_shapes=[
                pltpu.VMEM((512, 768), BF16),
                pltpu.VMEM((384, 512), BF16),
                pltpu.VMEM((128, 384), BF16),
                pltpu.VMEM((768, 512), BF16),
                pltpu.VMEM((384, 512), BF16),
            ],
        ),
        out_shape=(
            part, part, part, part,
            jax.ShapeDtypeStruct((512, 768), F32),
            jax.ShapeDtypeStruct((128, 768), F32),
            jax.ShapeDtypeStruct((1, 1536), F32),
        ),
        compiler_params=GRID_PARAMS,
        name="feed_a",
    )(ids, sec, *dys, wup, bup, wdown)


def feed_b(ids, sec, dys, wup, bup, wdown, keep_in, send_in, dsec_in, own_in, hid, pv):
    part = jax.ShapeDtypeStruct((4, 576, 128), BF16)
    anywhere = pl.BlockSpec(memory_space=pl.ANY)
    return pl.pallas_call(
        feed_b_kernel,
        grid_spec=pltpu.PrefetchScalarGridSpec(
            num_scalar_prefetch=1,
            grid=(4,),
            in_specs=[whole_spec((512, 768))]
            + [whole_spec((2, 64, 768))] * 4
            + weight_specs(True)
            + [
                anywhere, anywhere,
                whole_spec((512, 768)), whole_spec((128, 768)), whole_spec((512, 768)), whole_spec((8, 768)),
            ],
            out_specs=[
                down_spec(True), down_spec(True),
                pl.BlockSpec((1, 384), lambda i, ids: (0, i)),
                whole_spec((512, 768)), whole_spec((128, 768)), whole_spec((2, 64, 768)), whole_spec((8, 768)),
            ],
            scratch_shapes=[
                pltpu.VMEM((512, 768), BF16),
                pltpu.VMEM((384, 512), BF16),
                pltpu.VMEM((128, 384), BF16),
                pltpu.VMEM((512, 768), F32),
                pltpu.VMEM((128, 768), F32),
            ],
        ),
        out_shape=(
            part, part,
            jax.ShapeDtypeStruct((1, 1536), F32),
            jax.ShapeDtypeStruct((512, 768), BF16),
            jax.ShapeDtypeStruct((128, 768), F32),
            jax.ShapeDtypeStruct((2, 64, 768), BF16),
            jax.ShapeDtypeStruct((8, 768), F32),
        ),
        input_output_aliases={9: 0, 10: 1},
        compiler_params=GRID_PARAMS,
        name="feed_b",
    )(ids, sec, *dys, wup, bup, wdown, keep_in, send_in, dsec_in, own_in, hid, pv)


def attention_back_kernel(ids, seg, dh, wout, q_r, k_r, v_r, dproj_o, sums_o, same, datt):
    same[...] = crop_mask(seg[pl.ds(ids[1], 1), :])
    datt[...] = nt(dh[...], wout[...]).astype(BF16)
    low, high = half_masks()
    for j in range(HEADS // 4):
        cols = pl.ds(j * 128, 128)
        q, k, v, da = q_r[:, cols], k_r[:, cols], v_r[:, cols], datt[:, cols]
        dq = dk = dv = None
        for keep in (low, high):
            qh, kh, dah = q * keep, k * keep, da * keep
            probs = softmax_rows(nt(qh, k), same[...])
            dprobs = nt(dah, v)
            delta = jnp.sum(probs * dprobs, axis=-1, keepdims=True)
            ds = (probs * (dprobs - delta)).astype(BF16)
            parts = nn(ds, kh), tn(ds, qh), tn(probs.astype(BF16), dah)
            if dq is None:
                dq, dk, dv = parts
            else:
                dq, dk, dv = dq + parts[0], dk + parts[1], dv + parts[2]
        dq = (dq * 0.125).astype(BF16)
        dv = dv.astype(BF16)
        dproj_o[:, cols] = dq
        dproj_o[:, pl.ds(384 + j * 128, 128)] = dk.astype(BF16)
        dproj_o[:, pl.ds(768 + j * 128, 128)] = dv
        sums_o[0:1, cols] = jnp.sum(dq.astype(F32), axis=0, keepdims=True)
        sums_o[1:2, cols] = jnp.sum(dv.astype(F32), axis=0, keepdims=True)
    sums_o[2:8, :] = jnp.zeros((6, 384), F32)


def attention_back(ids, seg, dh, wout, q, k, v):
    mine = pl.BlockSpec((256, 384), lambda i, ids: (ids[1], ids[0]))
    return pl.pallas_call(
        attention_back_kernel,
        grid_spec=pltpu.PrefetchScalarGridSpec(
            num_scalar_prefetch=1,
            grid=(1,),
            in_specs=[
                whole_spec((2, 256)),
                pl.BlockSpec((256, 768), lambda i, ids: (ids[1], 0)),
                pl.BlockSpec((384, 768), lambda i, ids: (ids[0], 0)),
                mine, mine, mine,
            ],
            out_specs=[whole_spec((256, 1152)), whole_spec((8, 384))],
            scratch_shapes=[pltpu.VMEM((256, 256), F32), pltpu.VMEM((256, 384), BF16)],
        ),
        out_shape=(jax.ShapeDtypeStruct((256, 1152), BF16), jax.ShapeDtypeStruct((8, 384), F32)),
        compiler_params=GRID_PARAMS,
        name="attention_back",
    )(ids, seg, dh, wout, q, k, v)


def attention_weights_kernel(
    ids, own, other, first, att, dh, wq, wk, wv, t0, t2, vec,
    keep, send, dfirst_own, dfirst_send,
    dproj, turned, chosen, picked,
):
    core, x_bit = ids[1], ids[2]
    dproj[core] = own[...]
    for p in range(4):
        dproj[1 - core, pl.ds(p * 64, 64), :] = other[pl.ds((p ^ 1) * 64, 64), :]
    gain = jnp.zeros((1, 768), F32)
    shift = jnp.zeros((1, 768), F32)
    for s in range(2):
        for p, t in ((0, t0), (2, t2)):
            rows = dproj[s, pl.ds(p * 64, 64), :]
            part = nt(rows[:, 0:384], wq[...]) + nt(rows[:, 384:768], wk[...]) + nt(rows[:, 768:1152], wv[...])
            if p == 0:
                dfirst_own[s] = part
            else:
                dfirst_send[s] = part.astype(BF16)
            xhat, _ = standardize(t[s].astype(F32))
            gain += jnp.sum(part * xhat, axis=0, keepdims=True)
            shift += jnp.sum(part, axis=0, keepdims=True)
    turned[...] = first[...].T
    pick_rows(turned, chosen, core)
    product = nn(chosen[:, 0:256], dproj[0]) + nn(chosen[:, 256:512], dproj[1])
    put_slots(x_bit, product.astype(BF16), keep, send, 0)
    turned[...] = att[...].T
    pick_rows(turned, chosen, core)
    put_slots(x_bit, nn(chosen[...], dh[...]).astype(BF16), keep, send, 432)
    picked[...] = vec[...]
    for s in range(SLOTS):
        picked[s, 0:1, 0:96] = gain[:, s * 96 : s * 96 + 96]
        picked[s, 1:2, 0:96] = shift[:, s * 96 : s * 96 + 96]
    for s in range(SLOTS):
        value = picked[s].astype(BF16)

        @pl.when(x_bit == s % 2)
        def _():
            keep[s // 2, pl.ds(576, 16), :] = value

        @pl.when(x_bit != s % 2)
        def _():
            send[s // 2, pl.ds(576, 16), :] = value


def attention_weights(ids, own, other, first, att, dh, wqkv, t0, t2, vec):
    part = jax.ShapeDtypeStruct((4, 592, 128), BF16)
    heads = [pl.BlockSpec((768, 384), lambda i, ids, n=n: (0, 2 * n + ids[0])) for n in range(3)]
    return pl.pallas_call(
        attention_weights_kernel,
        grid_spec=pltpu.PrefetchScalarGridSpec(
            num_scalar_prefetch=1,
            grid=(1,),
            in_specs=[
                whole_spec((256, 1152)), whole_spec((256, 1152)),
                whole_spec((512, 768)), whole_spec((512, 768)),
                pl.BlockSpec((512, 384), lambda i, ids: (0, ids[0])),
                *heads,
                whole_spec((2, 64, 768)), whole_spec((2, 64, 768)),
                whole_spec((8, 16, 128)),
            ],
            out_specs=[
                whole_spec((4, 592, 128)), whole_spec((4, 592, 128)),
                whole_spec((2, 64, 768)), whole_spec((2, 64, 768)),
            ],
            scratch_shapes=[
                pltpu.VMEM((2, 256, 1152), BF16),
                pltpu.VMEM((768, 512), BF16),
                pltpu.VMEM((384, 512), BF16),
                pltpu.VMEM((8, 16, 128), F32),
            ],
        ),
        out_shape=(
            part, part,
            jax.ShapeDtypeStruct((2, 64, 768), F32),
            jax.ShapeDtypeStruct((2, 64, 768), BF16),
        ),
        compiler_params=GRID_PARAMS,
        name="attention_weights",
    )(ids, own, other, first, att, dh, wqkv, wqkv, wqkv, t0, t2, vec)


def input_grad_kernel(tokens, dfirst, received, dhid, pv, out):
    for s in range(2):
        xhat, rstd = standardize(tokens[s].astype(F32))
        grad = dfirst[s] + received[s].astype(F32)
        out[s] = (dhid[pl.ds(s * 64, 64), :] + norm_back(xhat, rstd, grad * pv[0:1, :])).astype(BF16)


def assemble_kernel(ids, *refs):
    ups, downs, atts = refs[0:4], refs[4:8], refs[8:12]
    up_o, down_o, out_o, qkv_o, vec_o = refs[12:]
    b = ids[3]
    total = jnp.zeros((16, 128), F32)
    for k in range(4):
        source = b ^ k
        y_bit, core = source // 2, lax.rem(source, 2)
        r48 = pl.ds(pl.multiple_of(core * 48, 16), 48)
        r192 = pl.ds(pl.multiple_of(core * 192, 64), 192)

        def cols(start, t):
            return pl.ds(pl.multiple_of(start + t * 128, 128), 128)

        for t in range(12):
            up_o[r48, cols(y_bit * 1536, t)] = ups[k][pl.ds(t * 48, 48), :].astype(F32)
        for t in range(3):
            down_o[r192, cols(y_bit * 384, t)] = downs[k][pl.ds(t * 192, 192), :].astype(F32)
            out_o[r48, cols(y_bit * 384, t)] = atts[k][pl.ds(432 + t * 48, 48), :].astype(F32)
        for t in range(9):
            qkv_o[r48, cols(y_bit * 384 + 768 * (t // 3), t % 3)] = atts[k][pl.ds(t * 48, 48), :].astype(F32)
        total += atts[k][pl.ds(576, 16), :].astype(F32)
    vec_o[...] = total


def assemble(ids, ups, downs, atts):
    vmem = pl.BlockSpec(memory_space=pltpu.VMEM)
    return pl.pallas_call(
        assemble_kernel,
        in_specs=[pl.BlockSpec(memory_space=pltpu.SMEM)] + [vmem] * 12,
        out_specs=[vmem] * 5,
        out_shape=(
            jax.ShapeDtypeStruct((96, 3072), F32),
            jax.ShapeDtypeStruct((384, 768), F32),
            jax.ShapeDtypeStruct((96, 768), F32),
            jax.ShapeDtypeStruct((96, 2304), F32),
            jax.ShapeDtypeStruct((16, 128), F32),
        ),
        compiler_params=PARAMS,
        name="assemble",
    )(ids, *ups, *downs, *atts)


def build(seq_size, blk_size):
    inner = seq_size // SLOTS

    def swap(x, axis, size, step):
        return lax.ppermute(x, axis, [(i, i ^ step) for i in range(size)])

    def core_swap(x):
        return swap(x, "blk", blk_size, 1)

    def y_swap(x):
        return swap(x, "blk", blk_size, 2)

    def seq_swap(x, step):
        return swap(x, "seq", seq_size, step * inner)

    def gather(x):
        across = y_swap(x)
        return x, core_swap(x), across, core_swap(across)

    def summed(keep, send, bits):
        got = seq_swap(send, 1)
        shape = keep.shape
        split = (2, 2) + shape[1:]
        both = keep.astype(F32).reshape(split), got.astype(F32).reshape(split)

        def take(a, i, axis):
            return lax.dynamic_index_in_dim(a, i, axis, keepdims=False)

        stay = sum(take(a, bits[1], 1) for a in both)
        leave = sum(take(a, 1 - bits[1], 1) for a in both).astype(BF16)
        got = seq_swap(leave, 2).astype(F32)
        leave = (take(stay, 1 - bits[2], 0) + take(got, 1 - bits[2], 0)).astype(BF16)
        stay = take(stay, bits[2], 0) + take(got, bits[2], 0)
        return (stay + seq_swap(leave, 4).astype(F32)).astype(BF16)

    def on_device(
        tokens, ln1_gain, ln1_bias, wqkv, bias_qv, wout, output_bias, ln2_gain, ln2_bias,
        wup, up_bias, wdown, down_bias, segment_ids, dy,
    ):
        b = lax.axis_index("blk")
        slot = lax.axis_index("seq") // inner
        bits = [(slot >> n) & 1 for n in range(3)]
        ids = jnp.stack([b // 2, b % 2, bits[0], b]).astype(jnp.int32)
        t_pieces = gather(tokens)
        d_pieces = gather(dy)
        pv = jnp.stack(
            [ln1_gain, ln1_bias, bias_qv[:768], bias_qv[768:], output_bias, ln2_gain, ln2_bias, down_bias]
        ).astype(F32)
        bup = up_bias.astype(F32).reshape(1, -1)
        seg = jnp.concatenate(
            [lax.dynamic_slice_in_dim(segment_ids, (b ^ p) * 64, 64, 1) for p in range(4)], axis=1
        )
        first, q, k, v, att, hid, sec = forward(seg, t_pieces, pv, wqkv, wout)
        up_keep, up_send, down_keep, down_send, dsec, own, bias_a = feed_a(
            ids, sec, d_pieces, wup, bup, wdown
        )
        up_sum = summed(up_keep, up_send, bits)
        down_keep, down_send, bias_b, dh, dhid_own, block_out, sums = feed_b(
            ids, sec, d_pieces, wup, bup, wdown, down_keep, down_send, dsec, own, hid, pv
        )
        down_sum = summed(down_keep, down_send, bits)
        dproj, head_sums = attention_back(ids, seg, dh, wout, q, k, v)
        dproj_other = core_swap(dproj)

        def rows(vector, per_slot):
            return vector.reshape(SLOTS, per_slot, 96)

        def placed(part, y_bit, size):
            return lax.dynamic_update_slice(jnp.zeros((2 * size,), F32), part, (y_bit * size,))

        qv = jnp.concatenate([placed(head_sums[0], b // 2, 384), placed(head_sums[1], b // 2, 384)])
        gelu_bias = jnp.where(
            b // 2 == 0,
            jnp.concatenate([bias_a[0], bias_b[0]]),
            jnp.concatenate([bias_b[0], bias_a[0]]),
        )
        vec = jnp.concatenate(
            [
                jnp.zeros((SLOTS, 2, 96), F32),
                rows(qv, 2), rows(sums[2], 1), rows(sums[0], 1), rows(sums[1], 1),
                rows(gelu_bias, 4), rows(sums[3], 1),
            ],
            axis=1,
        )
        vec = jnp.pad(vec, ((0, 0), (0, 4), (0, 32)))
        att_keep, att_send, dfirst_own, dfirst_send = attention_weights(
            ids, dproj, dproj_other, first, att, dh, wqkv, tokens, t_pieces[2], vec
        )
        att_sum = summed(att_keep, att_send, bits)
        dfirst_got = y_swap(dfirst_send)
        in_grad = pl.pallas_call(
            input_grad_kernel,
            out_shape=jax.ShapeDtypeStruct((2, 64, 768), BF16),
            compiler_params=PARAMS,
            name="input_grad",
        )(tokens, dfirst_own, dfirst_got, dhid_own, pv)
        up_o, down_o, out_o, qkv_o, vec_o = assemble(
            ids, gather(up_sum), gather(down_sum), gather(att_sum)
        )

        def flat(start, count):
            return vec_o[start : start + count, :96].reshape(-1)

        outs = [
            flat(0, 1), flat(1, 1), qkv_o, flat(2, 2), out_o, flat(4, 1), flat(5, 1), flat(6, 1),
            up_o, flat(7, 4), down_o, flat(11, 1),
        ]
        if inner > 1:
            groups = [list(range(g * inner, g * inner + inner)) for g in range(SLOTS)]
            outs = [
                lax.psum_scatter(o, "seq", scatter_dimension=0, axis_index_groups=groups, tiled=True)
                for o in outs
            ]
        return (block_out, in_grad, *outs)

    return on_device


def solution(mesh):
    data, vector, matrix = P("seq", "blk", None), P("seq"), P("seq", None)
    return jax.shard_map(
        build(mesh.shape["seq"], mesh.shape["blk"]),
        mesh=mesh,
        in_specs=(data,) + (P(),) * 12 + (matrix, data),
        out_specs=(
            data, data, vector, vector, matrix, vector, matrix, vector, vector, vector,
            matrix, vector, matrix, vector,
        ),
        check_vma=False,
    )
```

```python
import jax
import jax.numpy as jnp
from jax import lax
from jax.experimental import pallas as pl
from jax.experimental.pallas import tpu as pltpu
from jax.sharding import PartitionSpec as P

HEADS = 12
EPS = 1e-06
SLOTS = 8
F32 = jnp.float32
BF16 = jnp.bfloat16
GELU_C = 0.7978845608028654
GELU_A = 0.044715
VMEM = pl.BlockSpec(memory_space=pltpu.VMEM)
HBM = pl.BlockSpec(memory_space=pltpu.HBM)


def nn(a, b):
    return lax.dot_general(a, b, (((1,), (0,)), ((), ())), preferred_element_type=F32)


def nt(a, b):
    return lax.dot_general(a, b, (((1,), (1,)), ((), ())), preferred_element_type=F32)


def tn(a, b):
    return lax.dot_general(a, b, (((0,), (0,)), ((), ())), preferred_element_type=F32)


def standardize(x):
    centered = x - jnp.mean(x, axis=-1, keepdims=True)
    rstd = lax.rsqrt(jnp.mean(centered * centered, axis=-1, keepdims=True) + EPS)
    return centered * rstd, rstd


def norm_back(xhat, rstd, g):
    return rstd * (
        g
        - jnp.mean(g, axis=-1, keepdims=True)
        - xhat * jnp.mean(g * xhat, axis=-1, keepdims=True)
    )


def row(ref):
    return ref[...].astype(F32).reshape(1, -1)


def half_masks():
    lane = lax.broadcasted_iota(jnp.int32, (1, 128), 1)
    low = jnp.where(lane < 64, 1.0, 0.0)
    return low.astype(BF16), (1.0 - low).astype(BF16)


def flip(bit, k):
    return lax.rem(bit + k, 2)


def softmax_rows(scores, same):
    scores = jnp.where(same > 0.0, scores, -1e9)
    e = jnp.exp(scores - jnp.max(scores, axis=-1, keepdims=True))
    return e * (1.0 / jnp.sum(e, axis=-1, keepdims=True))


def column_sum(x):
    return jnp.sum(x.astype(F32), axis=0, keepdims=True)


def call(kernel, outs, ins, args, scratch=(), limit=24, us=2.0):
    return pl.pallas_call(
        kernel,
        out_shape=tuple(jax.ShapeDtypeStruct(s, d) for s, d in outs),
        in_specs=ins,
        out_specs=tuple(VMEM for _ in outs),
        scratch_shapes=list(scratch),
        compiler_params=pltpu.CompilerParams(vmem_limit_bytes=limit * 1024 * 1024),
        cost_estimate=pl.CostEstimate(
            flops=int(us * 1e9), bytes_accessed=int(us * 1e5), transcendentals=0
        ),
        name=kernel.__name__,
    )(*args)


class Place:
    def __init__(self, inner):
        b = lax.axis_index("blk")
        slot = lax.axis_index("seq") // inner
        self.y, self.core = b // 2, lax.rem(b, 2)
        self.x, self.z_low, self.z_high = lax.rem(slot, 2), lax.rem(slot // 2, 2), slot // 4


def crop_mask(place, seg):
    ids = jnp.broadcast_to(seg[pl.ds(place.core, 1), :], (256, 256))
    first, second = ids[:, 0:128], ids[:, 128:256]
    tiles = jnp.where(place.y == 1, second, first), jnp.where(place.y == 1, first, second)
    tiles = [jnp.where(place.core == 1, pltpu.roll(t, 64, 1), t) for t in tiles]
    wide = jnp.concatenate(tiles, axis=1)
    return jnp.where(wide == wide.T, 1.0, 0.0)


def pick_rows(transposed, chosen, part, x_bit):
    for k in range(2):
        for z in range(4):
            start = pl.multiple_of((2 * z + flip(x_bit, k)) * 96 + part * 48, 16)
            chosen[pl.ds((4 * k + z) * 48, 48), :] = transposed[pl.ds(start, 48), :]


def put_slots(product, keep, send, offset):
    for t in range(product.shape[1] // 128):
        for z in range(4):
            tile = product[:, t * 128 : t * 128 + 128]
            keep[z, pl.ds(offset + t * 48, 48), :] = tile[z * 48 : z * 48 + 48]
            send[z, pl.ds(offset + t * 48, 48), :] = tile[192 + z * 48 : 240 + z * 48]


def gather_rows(pieces, out):
    for s in range(2):
        for p, piece in enumerate(pieces):
            out[pl.ds(s * 256 + p * 64, 64), :] = piece[s]


def both_cores(core, own, other, out):
    for p in range(4):
        out[core, pl.ds(p * 64, 64), :] = own[pl.ds(p * 64, 64), :]
        out[1 - core, pl.ds(p * 64, 64), :] = other[pl.ds((p ^ 1) * 64, 64), :]


def build_kernels(inner):
    def attention(seg, t0, t1, t2, t3, gain, shift, bias, wqkv_hbm, att_o, mine_o, first, q_s, k_s, v_s, wqkv, same, sem):
        place = Place(inner)
        loads = [
            pltpu.make_async_copy(wqkv_hbm.at[:, pl.ds(n * 768, 768)], wqkv.at[n], sem.at[n])
            for n in range(3)
        ]
        for load in loads:
            load.start()
        g, b = row(gain), row(shift)
        for p, t in enumerate((t0, t1, t2, t3)):
            xhat, _ = standardize(t[place.core].astype(F32))
            first[pl.ds(p * 64, 64), :] = (xhat * g + b).astype(BF16)
        same[...] = crop_mask(place, seg)
        biases = row(bias)
        loads[0].wait()
        q_s[...] = (nn(first[...], wqkv[0]) + biases[:, 0:768]).astype(BF16) * BF16(0.125)
        loads[1].wait()
        k_s[...] = nn(first[...], wqkv[1]).astype(BF16)
        loads[2].wait()
        v_s[...] = (nn(first[...], wqkv[2]) + biases[:, 768:1536]).astype(BF16)
        low, high = half_masks()
        for j in range(HEADS // 2):
            cols = pl.ds(j * 128, 128)
            q, k, v = q_s[:, cols], k_s[:, cols], v_s[:, cols]
            out = None
            for keep in (low, high):
                probs = softmax_rows(nt(q * keep, k), same[...]).astype(BF16)
                part = nn(probs, v * keep)
                out = part if out is None else out + part
            att_o[:, cols] = out.astype(BF16)
        half = pl.ds(pl.multiple_of(place.y * 384, 128), 384)
        for n, source in enumerate((q_s, k_s, v_s)):
            mine_o[:, pl.ds(n * 384, 384)] = source[:, half]

    def feed(
        att_own, att_other, t0, t1, t2, t3, out_bias, gain, shift, up_bias, d0, d1, d2, d3,
        wout_hbm, wup_hbm, wdown_hbm,
        sec_o, dup_o, act_o, send_o, dsec_o, part_o, hid_core_o, hid_own_o, dy_o,
        att, hid, wout, wup, wdown, sem,
    ):
        place = Place(inner)
        load_out = pltpu.make_async_copy(wout_hbm, wout, sem.at[0])
        load_out.start()
        loads = []
        for j in range(4):
            units = pl.ds(pl.multiple_of((2 * j + place.core) * 384, 128), 384)
            loads.append(
                (
                    pltpu.make_async_copy(wup_hbm.at[:, units], wup.at[:, pl.ds(j * 384, 384)], sem.at[1 + j]),
                    pltpu.make_async_copy(wdown_hbm.at[units, :], wdown.at[pl.ds(j * 384, 384), :], sem.at[5 + j]),
                )
            )
        for pair in loads:
            for load in pair:
                load.start()
        both_cores(place.core, att_own, att_other, att)
        gather_rows((d0, d1, d2, d3), dy_o)
        g, b, ob = row(gain), row(shift), row(out_bias)
        load_out.wait()
        for s in range(2):
            added = nn(att[s], wout[...]) + ob
            for p, t in enumerate((t0, t1, t2, t3)):
                h = t[s].astype(F32) + added[p * 64 : p * 64 + 64]
                hid[s, pl.ds(p * 64, 64), :] = h
                xhat, _ = standardize(h)
                sec_o[pl.ds(s * 256 + p * 64, 64), :] = (xhat * g + b).astype(BF16)
            hid_own_o[pl.ds(s * 64, 64), :] = hid[s, 0:64, :]
        hid_core_o[...] = hid[place.core]
        for j in range(4):
            for load in loads[j]:
                load.wait()
            cols = pl.ds(j * 384, 384)
            units = pl.ds(pl.multiple_of((2 * j + place.core) * 384, 128), 384)
            ub = up_bias[:, units].astype(F32)
            for s in range(2):
                rows = pl.ds(s * 256, 256)
                up = nn(sec_o[rows, :], wup[:, cols]) + ub
                da = nt(dy_o[rows, :], wdown[cols, :])
                square = up * up
                tanh = jnp.tanh(GELU_C * up * (1.0 + GELU_A * square))
                cdf = 0.5 * (1.0 + tanh)
                act_o[rows, cols] = (up * cdf).astype(BF16)
                slope = cdf + (0.5 * GELU_C) * up * (1.0 - tanh * tanh) * (1.0 + (3.0 * GELU_A) * square)
                dup_o[rows, cols] = (da * slope).astype(BF16)
        dsec_o[...] = nt(dup_o[pl.ds(pl.multiple_of(place.core * 256, 256), 256), :], wup[...])
        away = nt(dup_o[pl.ds(pl.multiple_of((1 - place.core) * 256, 256), 256), :], wup[...])
        for p in range(4):
            send_o[pl.ds(p * 64, 64), :] = away[(p ^ 1) * 64 : (p ^ 1) * 64 + 64].astype(BF16)
        for s in range(2):
            part = nn(act_o[pl.ds(s * 256, 128), :], wdown[...])
            part_o[pl.ds(s * 64, 64), :] = part[0:64]
            send_o[pl.ds(256 + s * 64, 64), :] = part[64:128].astype(BF16)

    def feed_weights(sec, dup, act, dy, up_keep, up_send, down_keep, down_send, bias_o, turned, chosen):
        place = Place(inner)
        turned[...] = sec[...].T
        pick_rows(turned, chosen, place.y, place.x)
        dy_half = dy[:, pl.ds(pl.multiple_of(place.y * 384, 128), 384)]
        for j in range(4):
            cols = pl.ds(j * 384, 384)
            put_slots(nn(chosen[...], dup[:, cols]).astype(BF16), up_keep, up_send, j * 144)
            bias_o[:, cols] = column_sum(dup[0:128, cols]) + column_sum(dup[256:384, cols])
        for k, out in enumerate((down_keep, down_send)):
            for z in range(2):
                j = 2 * z + flip(place.z_low, k)
                units = pl.ds(pl.multiple_of(j * 384, 128), 384)
                product = tn(act[:, units], dy_half).astype(BF16)
                for t in range(3):
                    out[z, pl.ds(t * 384, 384), :] = product[:, t * 128 : t * 128 + 128]

    def attention_back(
        dsec_in, got, part, hid_core, hid_own, d0, d1, d2, d3, gain, down_bias, seg, mine, wout_hbm,
        block_o, ex_o, dhid_o, sums_o, heads_o,
        wout, dh, datt, same, sem,
    ):
        place = Place(inner)
        load = pltpu.make_async_copy(
            wout_hbm.at[pl.ds(pl.multiple_of(place.y * 384, 128), 384), :], wout, sem.at[0]
        )
        load.start()
        same[...] = crop_mask(place, seg)
        g = row(gain)
        sums = [jnp.zeros((1, 768), F32)] * 3
        for p, d in enumerate((d0, d1, d2, d3)):
            rows = pl.ds(p * 64, 64)
            xhat, rstd = standardize(hid_core[rows, :])
            grad = dsec_in[rows, :] + got[rows, :].astype(F32)
            dhid = d[place.core].astype(F32) + norm_back(xhat, rstd, grad * g)
            low = dhid.astype(BF16)
            dh[rows, :] = low
            if p < 2:
                sums = [a + column_sum(v) for a, v in zip(sums, (low, grad * xhat, grad))]
            if p == 0:
                dhid_o[...] = dhid
            if p == 1:
                ex_o[pl.ds(256, 32), 0:768] = low[0:32]
                ex_o[pl.ds(256, 32), 768:1536] = low[32:64]
        for r in range(3):
            sums_o[r : r + 1, :] = sums[r]
        sums_o[3:4, :] = column_sum(d0[0]) + column_sum(d0[1])
        sums_o[4:8, :] = jnp.zeros((4, 768), F32)
        ex_o[0:256, 1152:1536] = dh[:, pl.ds(pl.multiple_of(place.y * 384, 128), 384)]
        load.wait()
        datt[...] = nt(dh[...], wout[...]).astype(BF16)
        low, high = half_masks()
        for j in range(HEADS // 4):
            cols = pl.ds(j * 128, 128)
            q, k, v = (mine[:, pl.ds(n * 384 + j * 128, 128)] for n in range(3))
            da = datt[:, cols]
            dq = dk = dv = None
            for keep in (low, high):
                qh, kh, dah = q * keep, k * keep, da * keep
                probs = softmax_rows(nt(qh, k), same[...])
                dprobs = nt(dah, v)
                delta = jnp.sum(probs * dprobs, axis=-1, keepdims=True)
                ds = (probs * (dprobs - delta)).astype(BF16)
                parts = nn(ds, kh), tn(ds, qh), tn(probs.astype(BF16), dah)
                if dq is None:
                    dq, dk, dv = parts
                else:
                    dq, dk, dv = dq + parts[0], dk + parts[1], dv + parts[2]
            dq = (dq * 0.125).astype(BF16)
            dv = dv.astype(BF16)
            ex_o[0:256, pl.ds(j * 128, 128)] = dq
            ex_o[0:256, pl.ds(384 + j * 128, 128)] = dk.astype(BF16)
            ex_o[0:256, pl.ds(768 + j * 128, 128)] = dv
            heads_o[0:1, cols] = column_sum(dq)
            heads_o[1:2, cols] = column_sum(dv)
        heads_o[2:8, :] = jnp.zeros((6, 384), F32)
        bias = row(down_bias)
        for s in range(2):
            rows = pl.ds(s * 64, 64)
            arrived = got[pl.ds(256 + s * 64, 64), :].astype(F32)
            block_o[s] = (hid_own[rows, :] + (part[rows, :] + arrived + bias)).astype(BF16)

    def attention_weights(
        own, other, att_own, att_other, t0, t1, t2, t3, gain, shift, sums, heads, up_sums, wqkv_hbm,
        keep, send, dfirst_own, dfirst_send,
        ex, first, att, turned, chosen, vec, wqkv, sem,
    ):
        place = Place(inner)
        loads = []
        for n in range(3):
            cols = pl.ds(pl.multiple_of(n * 768 + place.y * 384, 128), 384)
            loads.append(pltpu.make_async_copy(wqkv_hbm.at[:, cols], wqkv.at[n], sem.at[n]))
        for load in loads:
            load.start()
        both_cores(place.core, own.at[pl.ds(0, 256)], other.at[pl.ds(0, 256)], ex)
        both_cores(place.core, att_own, att_other, att)
        for load in loads:
            load.wait()
        g, b = row(gain), row(shift)
        dgain = jnp.zeros((1, 768), F32)
        dshift = jnp.zeros((1, 768), F32)
        for s in range(2):
            for p, t in enumerate((t0, t1, t2, t3)):
                rows = pl.ds(p * 64, 64)
                xhat, _ = standardize(t[s].astype(F32))
                first[s, rows, :] = (xhat * g + b).astype(BF16)
                if p % 2 == 0:
                    part = nt(ex[s, rows, 0:384], wqkv[0])
                    part += nt(ex[s, rows, 384:768], wqkv[1])
                    part += nt(ex[s, rows, 768:1152], wqkv[2])
                    dgain += column_sum(part * xhat)
                    dshift += column_sum(part)
                    if p == 0:
                        dfirst_own[s] = part
                    else:
                        dfirst_send[s] = part.astype(BF16)
        for s in range(2):
            turned[:, pl.ds(s * 256, 256)] = first[s].T
        pick_rows(turned, chosen, place.core, place.x)
        product = nn(chosen[:, 0:256], ex[0, :, 0:1152]) + nn(chosen[:, 256:512], ex[1, :, 0:1152])
        put_slots(product.astype(BF16), keep, send, 0)
        for s in range(2):
            turned[:, pl.ds(s * 256, 256)] = att[s].T
        pick_rows(turned, chosen, place.core, place.x)
        product = nn(chosen[:, 0:256], ex[0, :, 1152:1536]) + nn(chosen[:, 256:512], ex[1, :, 1152:1536])
        put_slots(product.astype(BF16), keep, send, 432)
        vec[...] = jnp.zeros_like(vec)
        for s in range(SLOTS):
            k, z = flip(place.x, s % 2), s // 2
            lanes = slice(s * 96, s * 96 + 96)
            vec[k, z, 0:1, 0:96] = dgain[:, lanes]
            vec[k, z, 1:2, 0:96] = dshift[:, lanes]
            vec[k, z, 4:5, 0:96] = sums[0:1, lanes]
            vec[k, z, 5:6, 0:96] = sums[1:2, lanes]
            vec[k, z, 6:7, 0:96] = sums[2:3, lanes]
            vec[k, z, 11:12, 0:96] = sums[3:4, lanes]
        for h in range(2):
            for n in range(2):
                for r in range(2):
                    start = h * 192 + r * 96
                    vec[flip(place.x, h), 2 * n + place.y, 2 + r : 3 + r, 0:96] = heads[
                        n : n + 1, start : start + 96
                    ]
        for z in range(4):
            for r in range(4):
                start = z * 384 + r * 96
                vec[flip(place.x, place.core), z, 7 + r : 8 + r, 0:96] = up_sums[:, start : start + 96]
        for z in range(4):
            keep[z, pl.ds(576, 16), :] = vec[0, z].astype(BF16)
            send[z, pl.ds(576, 16), :] = vec[1, z].astype(BF16)

    def input_grad(tokens, dfirst, received, dhid, other, gain, out):
        place = Place(inner)
        g = row(gain)

        def write(s, residual):
            xhat, rstd = standardize(tokens[s].astype(F32))
            grad = dfirst[s] + received[s].astype(F32)
            out[s] = (residual + norm_back(xhat, rstd, grad * g)).astype(BF16)

        write(place.core, dhid[...])
        away = jnp.concatenate([other[256:288, 0:768], other[256:288, 768:1536]], axis=0)
        write(1 - place.core, away.astype(F32))

    def halve_z_low(keep, got, stay, leave):
        halve(Place(inner).z_low, keep, got, stay, leave)

    def halve_z_high(keep, got, stay, leave):
        halve(Place(inner).z_high, keep, got, stay, leave)

    def halve(bit, keep, got, stay, leave):
        for i in range(stay.shape[0]):
            for out, k in ((leave, 1), (stay, 0)):
                at = 2 * i + flip(bit, k)
                out[i] = (keep[at].astype(F32) + got[at].astype(F32)).astype(BF16)

    def add(a, b, out):
        out[...] = (a[...].astype(F32) + b[...].astype(F32)).astype(BF16)

    def assemble_up(p0, p1, p2, p3, out):
        place = Place(inner)
        for k, piece in enumerate((p0, p1, p2, p3)):
            y, core = flip(place.y, k // 2), flip(place.core, k % 2)
            rows = pl.ds(pl.multiple_of(y * 48, 16), 48)
            for j in range(4):
                for t in range(3):
                    cols = pl.ds(pl.multiple_of((2 * j + core) * 384 + t * 128, 128), 128)
                    out[rows, cols] = piece[0, pl.ds((3 * j + t) * 48, 48), :].astype(F32)

    def assemble_down(mine, across, partner, partner_across, out):
        place = Place(inner)

        def write(own, other):
            for k, piece in enumerate((own, other)):
                for t in range(3):
                    cols = pl.ds(pl.multiple_of(flip(place.y, k) * 384 + t * 128, 128), 128)
                    out[:, cols] = piece[0, pl.ds(t * 384, 384), :].astype(F32)

        @pl.when(place.core == place.x)
        def _():
            write(mine, across)

        @pl.when(place.core != place.x)
        def _():
            write(partner, partner_across)

    def assemble_rest(p0, p1, p2, p3, out_o, qkv_o, gain1, shift1, qv, out_b, gain2, shift2, up_b, down_b):
        place = Place(inner)
        total = jnp.zeros((16, 128), F32)
        for k, piece in enumerate((p0, p1, p2, p3)):
            y, core = flip(place.y, k // 2), flip(place.core, k % 2)
            rows = pl.ds(pl.multiple_of(core * 48, 16), 48)
            for t in range(3):
                cols = pl.ds(pl.multiple_of(y * 384 + t * 128, 128), 128)
                out_o[rows, cols] = piece[0, pl.ds(432 + t * 48, 48), :].astype(F32)
                for n in range(3):
                    cols = pl.ds(pl.multiple_of(n * 768 + y * 384 + t * 128, 128), 128)
                    qkv_o[rows, cols] = piece[0, pl.ds((3 * n + t) * 48, 48), :].astype(F32)
            total += piece[0, pl.ds(576, 16), :].astype(F32)

        def lay(out, start, count):
            parts = [total[start + r : start + r + 1, 0:96] for r in range(count)]
            out[...] = jnp.concatenate(parts, axis=1).reshape(count * 96)

        for out, start, count in (
            (gain1, 0, 1), (shift1, 1, 1), (qv, 2, 2), (out_b, 4, 1), (gain2, 5, 1), (shift2, 6, 1),
            (up_b, 7, 4), (down_b, 11, 1),
        ):
            lay(out, start, count)

    return locals()


def build(seq_size, blk_size):
    inner = seq_size // SLOTS
    kernels = build_kernels(inner)

    def swap(x, axis, size, step):
        return lax.ppermute(x, axis, [(i, i ^ step) for i in range(size)])

    def core_swap(x):
        return swap(x, "blk", blk_size, 1)

    def y_swap(x):
        return swap(x, "blk", blk_size, 2)

    def seq_swap(x, step):
        return swap(x, "seq", seq_size, step * inner)

    def some(x, moved):
        pairs = []
        for s in range(seq_size):
            for b in range(blk_size):
                to = moved(s, b)
                if to is not None:
                    pairs.append((s * blk_size + b, to[0] * blk_size + to[1]))
        return lax.ppermute(x, ("seq", "blk"), pairs)

    def aligned(s, b):
        return (s // inner) % 2 == b % 2

    def gather(x):
        across = y_swap(x)
        return x, core_swap(x), across, core_swap(across)

    def halve(name, keep, got, us):
        n, rows, lanes = keep.shape
        shape = ((n // 2, rows, lanes), BF16)
        return call(kernels[name], (shape, shape), [VMEM] * 2, (keep, got), us=us)

    def add(a, b):
        return call(kernels["add"], ((a.shape, BF16),), [VMEM] * 2, (a, b), us=1.0)[0]

    def on_device(
        tokens, ln1_gain, ln1_bias, wqkv, bias_qv, wout, output_bias, ln2_gain, ln2_bias,
        wup, up_bias, wdown, down_bias, segment_ids, dy,
    ):
        t_pieces = gather(tokens)
        d_pieces = gather(dy)
        up_row = up_bias.reshape(1, -1)
        att, mine = call(
            kernels["attention"],
            (((256, 768), BF16), ((256, 1152), BF16)),
            [VMEM] * 8 + [HBM],
            (segment_ids, *t_pieces, ln1_gain, ln1_bias, bias_qv, wqkv),
            [pltpu.VMEM((256, 768), BF16)] * 4
            + [pltpu.VMEM((3, 768, 768), BF16), pltpu.VMEM((256, 256), F32), pltpu.SemaphoreType.DMA((3,))],
            us=6.0,
        )
        att_other = core_swap(att)
        sec, dup, act, partial, dsec, part, hid_core, hid_own, dy_rows = call(
            kernels["feed"],
            (
                ((512, 768), BF16), ((512, 1536), BF16), ((512, 1536), BF16), ((384, 768), BF16),
                ((256, 768), F32), ((128, 768), F32), ((256, 768), F32), ((128, 768), F32), ((512, 768), BF16),
            ),
            [VMEM] * 14 + [HBM] * 3,
            (
                att, att_other, *t_pieces, output_bias, ln2_gain, ln2_bias, up_row, *d_pieces,
                wout, wup, wdown,
            ),
            [
                pltpu.VMEM((2, 256, 768), BF16), pltpu.VMEM((2, 256, 768), F32),
                pltpu.VMEM((768, 768), BF16), pltpu.VMEM((768, 1536), BF16), pltpu.VMEM((1536, 768), BF16),
                pltpu.SemaphoreType.DMA((9,)),
            ],
            us=9.0,
        )
        arrived = core_swap(partial)
        chunk, half = ((4, 576, 128), BF16), ((2, 1152, 128), BF16)
        up_keep, up_send, down_keep, down_send, up_sums = call(
            kernels["feed_weights"],
            (chunk, chunk, half, half, ((1, 1536), F32)),
            [VMEM] * 4,
            (sec, dup, act, dy_rows),
            [pltpu.VMEM((768, 512), BF16), pltpu.VMEM((384, 512), BF16)],
            us=3.0,
        )
        stay, leave = halve("halve_z_low", up_keep, seq_swap(up_send, 1), 1.0)
        stay, leave = halve("halve_z_high", stay, seq_swap(leave, 2), 1.0)
        up_sum = add(stay, seq_swap(leave, 4))
        stay, leave = halve("halve_z_high", down_keep, seq_swap(down_send, 2), 1.0)
        down_part = add(stay, seq_swap(leave, 4))
        down_sum = add(
            down_part,
            some(down_part, lambda s, b: None if aligned(s, b) else (s ^ inner, b)),
        )
        block_out, ex, dhid, sums, heads = call(
            kernels["attention_back"],
            (
                ((2, 64, 768), BF16), ((288, 1536), BF16), ((64, 768), F32), ((8, 768), F32), ((8, 384), F32),
            ),
            [VMEM] * 13 + [HBM],
            (
                dsec, arrived, part, hid_core, hid_own, *d_pieces, ln2_gain, down_bias, segment_ids, mine, wout,
            ),
            [
                pltpu.VMEM((384, 768), BF16), pltpu.VMEM((256, 768), BF16), pltpu.VMEM((256, 384), BF16),
                pltpu.VMEM((256, 256), F32), pltpu.SemaphoreType.DMA((1,)),
            ],
            us=4.0,
        )
        ex_other = core_swap(ex)
        rest = ((4, 592, 128), BF16)
        rest_keep, rest_send, dfirst_own, dfirst_send = call(
            kernels["attention_weights"],
            (rest, rest, ((2, 64, 768), F32), ((2, 64, 768), BF16)),
            [VMEM] * 13 + [HBM],
            (ex, ex_other, att, att_other, *t_pieces, ln1_gain, ln1_bias, sums, heads, up_sums, wqkv),
            [
                pltpu.VMEM((2, 256, 1536), BF16), pltpu.VMEM((2, 256, 768), BF16), pltpu.VMEM((2, 256, 768), BF16),
                pltpu.VMEM((768, 512), BF16), pltpu.VMEM((384, 512), BF16), pltpu.VMEM((2, 4, 16, 128), F32),
                pltpu.VMEM((3, 768, 384), BF16), pltpu.SemaphoreType.DMA((3,)),
            ],
            us=4.0,
        )
        stay, leave = halve("halve_z_low", rest_keep, seq_swap(rest_send, 1), 1.0)
        stay, leave = halve("halve_z_high", stay, seq_swap(leave, 2), 1.0)
        rest_sum = add(stay, seq_swap(leave, 4))
        (in_grad,) = call(
            kernels["input_grad"],
            (((2, 64, 768), BF16),),
            [VMEM] * 6,
            (tokens, dfirst_own, y_swap(dfirst_send), dhid, ex_other, ln1_gain),
            us=1.0,
        )
        (up_o,) = call(kernels["assemble_up"], (((96, 3072), F32),), [VMEM] * 4, gather(up_sum), us=1.0)
        across = some(down_sum, lambda s, b: (s, b ^ 2) if aligned(s, b) else None)
        to_core = lambda s, b: (s, b ^ 1) if aligned(s, b) else None
        (down_o,) = call(
            kernels["assemble_down"],
            (((384, 768), F32),),
            [VMEM] * 4,
            (down_sum, across, some(down_sum, to_core), some(across, to_core)),
            us=1.0,
        )
        small = [96, 96, 192, 96, 96, 96, 384, 96]
        out_o, qkv_o, *vectors = call(
            kernels["assemble_rest"],
            (((96, 768), F32), ((96, 2304), F32)) + tuple(((n,), F32) for n in small),
            [VMEM] * 4,
            gather(rest_sum),
            us=1.0,
        )
        gain1, shift1, qv, out_b, gain2, shift2, up_b, down_b = vectors
        outs = [gain1, shift1, qkv_o, qv, out_o, out_b, gain2, shift2, up_o, up_b, down_o, down_b]
        if inner > 1:
            groups = [list(range(g * inner, g * inner + inner)) for g in range(SLOTS)]
            outs = [
                lax.psum_scatter(o, "seq", scatter_dimension=0, axis_index_groups=groups, tiled=True)
                for o in outs
            ]
        return (block_out, in_grad, *outs)

    return on_device


def solution(mesh):
    data, vector, matrix = P("seq", "blk", None), P("seq"), P("seq", None)
    return jax.shard_map(
        build(mesh.shape["seq"], mesh.shape["blk"]),
        mesh=mesh,
        in_specs=(data,) + (P(),) * 12 + (matrix, data),
        out_specs=(
            data, data, vector, vector, matrix, vector, matrix, vector, vector, vector,
            matrix, vector, matrix, vector,
        ),
        check_vma=False,
    )
```

```python
import jax
import jax.numpy as jnp
from jax import lax
from jax.experimental import pallas as pl
from jax.experimental.pallas import tpu as pltpu
from jax.sharding import PartitionSpec as P

HEADS = 12
EPS = 1e-06
SLOTS = 8
F32 = jnp.float32
BF16 = jnp.bfloat16
GELU_C = 0.7978845608028654
GELU_A = 0.044715
US = 0.01
FILL = 20.0
VMEM = pl.BlockSpec(memory_space=pltpu.VMEM)
HBM = pl.BlockSpec(memory_space=pltpu.HBM)
ANY = pl.BlockSpec(memory_space=pl.ANY)


def nn(a, b):
    return lax.dot_general(a, b, (((1,), (0,)), ((), ())), preferred_element_type=F32)


def nt(a, b):
    return lax.dot_general(a, b, (((1,), (1,)), ((), ())), preferred_element_type=F32)


def tn(a, b):
    return lax.dot_general(a, b, (((0,), (0,)), ((), ())), preferred_element_type=F32)


def standardize(x):
    centered = x - jnp.mean(x, axis=-1, keepdims=True)
    rstd = lax.rsqrt(jnp.mean(centered * centered, axis=-1, keepdims=True) + EPS)
    return centered * rstd, rstd


def norm_back(xhat, rstd, g):
    return rstd * (
        g
        - jnp.mean(g, axis=-1, keepdims=True)
        - xhat * jnp.mean(g * xhat, axis=-1, keepdims=True)
    )


def row(ref):
    return ref[...].astype(F32).reshape(1, -1)


def half_masks():
    lane = lax.broadcasted_iota(jnp.int32, (1, 128), 1)
    low = jnp.where(lane < 64, 1.0, 0.0)
    return low.astype(BF16), (1.0 - low).astype(BF16)


def flip(bit, k):
    return lax.rem(bit + k, 2)


def softmax_rows(scores, same):
    scores = jnp.where(same > 0.0, scores, -1e9)
    e = jnp.exp(scores - jnp.max(scores, axis=-1, keepdims=True))
    return e * (1.0 / jnp.sum(e, axis=-1, keepdims=True))


def column_sum(x):
    return jnp.sum(x.astype(F32), axis=0, keepdims=True)


def call(kernel, outs, ins, args, scratch=(), limit=24, us=2.0):
    return pl.pallas_call(
        kernel,
        out_shape=tuple(jax.ShapeDtypeStruct(s, d) for s, d in outs),
        in_specs=ins,
        out_specs=tuple(VMEM for _ in outs),
        scratch_shapes=list(scratch),
        compiler_params=pltpu.CompilerParams(vmem_limit_bytes=limit * 1024 * 1024),
        cost_estimate=pl.CostEstimate(
            flops=int(us * 1e9), bytes_accessed=int(us * 1e5), transcendentals=0
        ),
        name=kernel.__name__,
    )(*args)


def in_hbm(*arrays):
    return tuple(pltpu.with_memory_space_constraint(a, pltpu.HBM) for a in arrays)


class Place:
    def __init__(self, inner):
        b = lax.axis_index("blk")
        slot = lax.axis_index("seq") // inner
        self.y, self.core = b // 2, lax.rem(b, 2)
        self.x, self.z_low, self.z_high = lax.rem(slot, 2), lax.rem(slot // 2, 2), slot // 4


def crop_mask(place, seg):
    ids = jnp.broadcast_to(seg[pl.ds(place.core, 1), :], (256, 256))
    first, second = ids[:, 0:128], ids[:, 128:256]
    tiles = jnp.where(place.y == 1, second, first), jnp.where(place.y == 1, first, second)
    tiles = [jnp.where(place.core == 1, pltpu.roll(t, 64, 1), t) for t in tiles]
    wide = jnp.concatenate(tiles, axis=1)
    return jnp.where(wide == wide.T, 1.0, 0.0)


def pick_rows(transposed, chosen, part, x_bit):
    for k in range(2):
        for z in range(4):
            start = pl.multiple_of((2 * z + flip(x_bit, k)) * 96 + part * 48, 16)
            chosen[pl.ds((4 * k + z) * 48, 48), :] = transposed[pl.ds(start, 48), :]


def put_slots(product, keep, send, offset):
    for t in range(product.shape[1] // 128):
        for z in range(4):
            tile = product[:, t * 128 : t * 128 + 128]
            keep[z, pl.ds(offset + t * 48, 48), :] = tile[z * 48 : z * 48 + 48]
            send[z, pl.ds(offset + t * 48, 48), :] = tile[192 + z * 48 : 240 + z * 48]


def gather_rows(pieces, out):
    for s in range(2):
        for p, piece in enumerate(pieces):
            out[pl.ds(s * 256 + p * 64, 64), :] = piece[s]


def both_cores(core, own, other, out):
    for p in range(4):
        out[core, pl.ds(p * 64, 64), :] = own[pl.ds(p * 64, 64), :]
        out[1 - core, pl.ds(p * 64, 64), :] = other[pl.ds((p ^ 1) * 64, 64), :]


def build_kernels(inner):
    def near(
        t1, tokens_hbm, seg_hbm, g1_hbm, s1_hbm, qv_hbm, ob_hbm, g2_hbm, s2_hbm, db_hbm, ub_hbm,
        wqkv_hbm, wout_hbm, wup_hbm, wdown_hbm,
        near_o, same_o, vec_o, up_bias_o, t0, wqkv, wout, wup, wdown,
        first, seg, g1, s1, qv, ob, g2, s2, db, ub, sem,
    ):
        place = Place(inner)
        pairs = [
            (g1_hbm, g1), (s1_hbm, s1), (qv_hbm, qv), (ob_hbm, ob), (g2_hbm, g2), (s2_hbm, s2),
            (db_hbm, db), (ub_hbm, ub), (seg_hbm, seg), (tokens_hbm, t0),
        ]
        small = len(pairs)
        pairs += [(wqkv_hbm.at[:, pl.ds(n * 768, 768)], wqkv.at[:, pl.ds(n * 768, 768)]) for n in range(3)]
        pairs.append((wout_hbm, wout))
        for j in range(4):
            units = pl.ds(pl.multiple_of((2 * j + place.core) * 384, 128), 384)
            mine = pl.ds(j * 384, 384)
            pairs += [(wup_hbm.at[:, units], wup.at[:, mine]), (wdown_hbm.at[units, :], wdown.at[mine, :])]
        loads = [pltpu.make_async_copy(a, b, sem.at[i]) for i, (a, b) in enumerate(pairs)]
        for load in loads:
            load.start()
        for load in loads[:small]:
            load.wait()
        both = row(qv)
        for r, value in enumerate(
            (row(g1), row(s1), both[:, 0:768], both[:, 768:1536], row(ob), row(g2), row(s2), row(db))
        ):
            vec_o[r : r + 1, :] = value
        flat = row(ub)
        for j in range(4):
            start = 2 * j * 384
            up_bias_o[:, pl.ds(j * 384, 384)] = jnp.where(
                place.core == 1, flat[:, start + 384 : start + 768], flat[:, start : start + 384]
            )
        same_o[...] = crop_mask(place, seg)
        for p, t in enumerate((t0, t1)):
            xhat, _ = standardize(t[place.core].astype(F32))
            first[pl.ds(p * 64, 64), :] = (xhat * vec_o[0:1, :] + vec_o[1:2, :]).astype(BF16)
        for n in range(3):
            loads[small + n].wait()
            project(n, first[...], wqkv, vec_o, near_o)
        for load in loads[small + 3 :]:
            load.wait()

    def project(n, first, wqkv, vec, out):
        cols = pl.ds(n * 768, 768)
        value = nn(first, wqkv[:, cols])
        if n != 1:
            value = value + vec[2 + n // 2 : 3 + n // 2, :]
        value = value.astype(BF16)
        out[:, cols] = value * BF16(0.125) if n == 0 else value

    def attention(near_in, same, vec, t2, t3, wqkv, att_o, mine_o, first, far, qkv):
        place = Place(inner)
        for p, t in enumerate((t2, t3)):
            xhat, _ = standardize(t[place.core].astype(F32))
            first[pl.ds(p * 64, 64), :] = (xhat * vec[0:1, :] + vec[1:2, :]).astype(BF16)
        for n in range(3):
            project(n, first[...], wqkv, vec, far)
        qkv[0:128, :] = near_in[...]
        qkv[128:256, :] = far[...]
        low, high = half_masks()
        for j in range(HEADS // 2):
            q, k, v = (qkv[:, pl.ds(n * 768 + j * 128, 128)] for n in range(3))
            out = None
            for keep in (low, high):
                probs = softmax_rows(nt(q * keep, k), same[...]).astype(BF16)
                part = nn(probs, v * keep)
                out = part if out is None else out + part
            att_o[:, pl.ds(j * 128, 128)] = out.astype(BF16)
        for n in range(3):
            half = pl.ds(pl.multiple_of(n * 768 + place.y * 384, 128), 384)
            mine_o[:, pl.ds(n * 384, 384)] = qkv[:, half]

    def feed(
        att_own, att_other, t0, t1, t2, t3, vec, up_bias, d0, d1, d2, d3, wout, wup, wdown,
        sec_o, dup_o, act_o, send_o, dsec_o, hid_core_o, hid_own_o, dy_o,
        att, hid,
    ):
        place = Place(inner)
        both_cores(place.core, att_own, att_other, att)
        gather_rows((d0, d1, d2, d3), dy_o)
        g, b, ob = vec[5:6, :], vec[6:7, :], vec[4:5, :]
        for s in range(2):
            added = nn(att[s], wout[...]) + ob
            for p, t in enumerate((t0, t1, t2, t3)):
                h = t[s].astype(F32) + added[p * 64 : p * 64 + 64]
                hid[s, pl.ds(p * 64, 64), :] = h
                xhat, _ = standardize(h)
                sec_o[pl.ds(s * 256 + p * 64, 64), :] = (xhat * g + b).astype(BF16)
            hid_own_o[pl.ds(s * 64, 64), :] = hid[s, 0:64, :]
        hid_core_o[...] = hid[place.core]
        for j in range(4):
            cols = pl.ds(j * 384, 384)
            for s in range(2):
                rows = pl.ds(s * 256, 256)
                up = nn(sec_o[rows, :], wup[:, cols]) + up_bias[:, cols]
                da = nt(dy_o[rows, :], wdown[cols, :])
                square = up * up
                tanh = jnp.tanh(up * (GELU_C + (GELU_C * GELU_A) * square))
                cdf = 0.5 + 0.5 * tanh
                act_o[rows, cols] = (up * cdf).astype(BF16)
                slope = cdf + (1.0 - tanh * tanh) * (
                    up * ((0.5 * GELU_C) + (1.5 * GELU_C * GELU_A) * square)
                )
                dup_o[rows, cols] = (da * slope).astype(BF16)
        away = nt(dup_o[pl.ds(pl.multiple_of((1 - place.core) * 256, 256), 256), :], wup[...])
        for p in range(4):
            send_o[pl.ds(p * 64, 64), :] = away[(p ^ 1) * 64 : (p ^ 1) * 64 + 64].astype(BF16)
        dsec_o[...] = nt(dup_o[pl.ds(pl.multiple_of(place.core * 256, 256), 256), :], wup[...])

    def feed_weights(sec, dup, act, dy, up_keep, up_send, down_keep, down_send, bias_o, turned, chosen):
        place = Place(inner)
        turned[...] = sec[...].T
        pick_rows(turned, chosen, place.y, place.x)
        for j in range(4):
            cols = pl.ds(j * 384, 384)
            put_slots(nn(chosen[...], dup[:, cols]).astype(BF16), up_keep, up_send, j * 144)
            bias_o[:, cols] = column_sum(dup[0:128, cols]) + column_sum(dup[256:384, cols])
        dy_half = dy[:, pl.ds(pl.multiple_of(place.y * 384, 128), 384)]
        for k, out in enumerate((down_keep, down_send)):
            for z in range(2):
                j = 2 * z + flip(place.z_low, k)
                units = pl.ds(pl.multiple_of(j * 384, 128), 384)
                product = tn(act[:, units], dy_half).astype(BF16)
                for t in range(3):
                    out[z, pl.ds(t * 384, 384), :] = product[:, t * 128 : t * 128 + 128]

    def attention_back(
        dsec_in, got, hid_core, d0, d1, d2, d3, vec, same, mine, wout, up_sums,
        exa_o, exb_o, dhid_o, sums_o, heads_o,
        dh, datt,
    ):
        place = Place(inner)
        g = vec[5:6, :]
        sums = [jnp.zeros((1, 768), F32)] * 3
        for p, d in enumerate((d0, d1, d2, d3)):
            rows = pl.ds(p * 64, 64)
            xhat, rstd = standardize(hid_core[rows, :])
            grad = dsec_in[rows, :] + got[rows, :].astype(F32)
            dhid = d[place.core].astype(F32) + norm_back(xhat, rstd, grad * g)
            low = dhid.astype(BF16)
            dh[rows, :] = low
            if p < 2:
                sums = [a + column_sum(v) for a, v in zip(sums, (low, grad * xhat, grad))]
            if p == 0:
                dhid_o[...] = dhid
            if p == 1:
                exb_o[pl.ds(256, 64), :] = low
        for r in range(3):
            sums_o[r : r + 1, :] = sums[r]
        sums_o[3:4, :] = column_sum(d0[0]) + column_sum(d0[1])
        sums_o[4:8, :] = jnp.zeros((4, 768), F32)
        exb_o[0:256, 384:768] = dh[:, pl.ds(pl.multiple_of(place.y * 384, 128), 384)]
        datt[...] = nt(dh[...], wout[pl.ds(pl.multiple_of(place.y * 384, 128), 384), :]).astype(BF16)
        low, high = half_masks()
        for j in range(HEADS // 4):
            cols = pl.ds(j * 128, 128)
            q, k, v = (mine[:, pl.ds(n * 384 + j * 128, 128)] for n in range(3))
            da = datt[:, cols]
            dq = dk = dv = None
            for keep in (low, high):
                qh, kh, dah = q * keep, k * keep, da * keep
                probs = softmax_rows(nt(qh, k), same[...])
                dprobs = nt(dah, v)
                delta = jnp.sum(probs * dprobs, axis=-1, keepdims=True)
                ds = (probs * (dprobs - delta)).astype(BF16)
                parts = nn(ds, kh), tn(ds, qh), tn(probs.astype(BF16), dah)
                if dq is None:
                    dq, dk, dv = parts
                else:
                    dq, dk, dv = dq + parts[0], dk + parts[1], dv + parts[2]
            dq = (dq * 0.125).astype(BF16)
            dv = dv.astype(BF16)
            exa_o[:, cols] = dq
            exa_o[:, pl.ds(384 + j * 128, 128)] = dk.astype(BF16)
            exb_o[0:256, cols] = dv
            heads_o[0:1, cols] = column_sum(dq)
            heads_o[1:2, cols] = column_sum(dv)
        heads_o[2:8, :] = jnp.zeros((6, 384), F32)

    def turn(
        att_own, att_other, t0, t1, t2, t3, params, act, wdown, before,
        first_o, att_o, part_o, part_send,
        first, att, turned,
    ):
        place = Place(inner)
        both_cores(place.core, att_own, att_other, att)
        for s in range(2):
            for p, t in enumerate((t0, t1, t2, t3)):
                xhat, _ = standardize(t[s].astype(F32))
                first[s, pl.ds(p * 64, 64), :] = (xhat * params[0:1, :] + params[1:2, :]).astype(BF16)
        for source, chosen in ((first, first_o), (att, att_o)):
            for s in range(2):
                turned[:, pl.ds(s * 256, 256)] = source[s].T
            pick_rows(turned, chosen, place.core, place.x)
        for s in range(2):
            part = nn(act[pl.ds(s * 256, 128), :], wdown[...])
            part_o[s] = part[0:64]
            part_send[s] = part[64:128].astype(BF16)

    def attention_weights(
        owna, ownb, othera, otherb, first, att, t0, t2, params, sums, heads, up_sums, wqkv,
        keep, send, dfirst_own, dfirst_send,
        exa, exb, vec,
    ):
        place = Place(inner)
        weights = [wqkv[:, pl.ds(pl.multiple_of(n * 768 + place.y * 384, 128), 384)] for n in range(3)]
        both_cores(place.core, owna, othera, exa)
        both_cores(place.core, ownb, otherb, exb)
        for chosen, source, lanes, offset in (
            (first, exa, slice(0, 768), 0),
            (first, exb, slice(0, 384), 288),
            (att, exb, slice(384, 768), 432),
        ):
            product = nn(chosen[:, 0:256], source[0, :, lanes]) + nn(chosen[:, 256:512], source[1, :, lanes])
            put_slots(product.astype(BF16), keep, send, offset)
        dgain = jnp.zeros((1, 768), F32)
        dshift = jnp.zeros((1, 768), F32)
        for s in range(2):
            for p, t in ((0, t0), (2, t2)):
                rows = pl.ds(p * 64, 64)
                xhat, _ = standardize(t[s].astype(F32))
                part = nt(exa[s, rows, 0:384], weights[0])
                part += nt(exa[s, rows, 384:768], weights[1])
                part += nt(exb[s, rows, 0:384], weights[2])
                dgain += column_sum(part * xhat)
                dshift += column_sum(part)
                if p == 0:
                    dfirst_own[s] = part
                else:
                    dfirst_send[s] = part.astype(BF16)
        vec[...] = jnp.zeros_like(vec)
        for s in range(SLOTS):
            k, z = flip(place.x, s % 2), s // 2
            lanes = slice(s * 96, s * 96 + 96)
            vec[k, z, 0:1, 0:96] = dgain[:, lanes]
            vec[k, z, 1:2, 0:96] = dshift[:, lanes]
            vec[k, z, 4:5, 0:96] = sums[0:1, lanes]
            vec[k, z, 5:6, 0:96] = sums[1:2, lanes]
            vec[k, z, 6:7, 0:96] = sums[2:3, lanes]
            vec[k, z, 11:12, 0:96] = sums[3:4, lanes]
        for h in range(2):
            for n in range(2):
                for r in range(2):
                    start = h * 192 + r * 96
                    vec[flip(place.x, h), 2 * n + place.y, 2 + r : 3 + r, 0:96] = heads[
                        n : n + 1, start : start + 96
                    ]
        for z in range(4):
            for r in range(4):
                start = z * 384 + r * 96
                vec[flip(place.x, place.core), z, 7 + r : 8 + r, 0:96] = up_sums[:, start : start + 96]
        for z in range(4):
            keep[z, pl.ds(576, 16), :] = vec[0, z].astype(BF16)
            send[z, pl.ds(576, 16), :] = vec[1, z].astype(BF16)

    def input_grad(tokens, dfirst, received, dhid, other, vec, hid_own, part, part_got, out, block_o):
        place = Place(inner)

        def write(s, residual):
            xhat, rstd = standardize(tokens[s].astype(F32))
            grad = dfirst[s] + received[s].astype(F32)
            out[s] = (residual + norm_back(xhat, rstd, grad * vec[0:1, :])).astype(BF16)

        write(place.core, dhid[...])
        write(1 - place.core, other[256:320, :].astype(F32))
        for s in range(2):
            added = part[s] + part_got[s].astype(F32) + vec[7:8, :]
            block_o[s] = (hid_own[pl.ds(s * 64, 64), :] + added).astype(BF16)

    def halve_z_low(keep, got, before, stay, leave):
        halve(Place(inner).z_low, keep, got, stay, leave)

    def halve_z_high(keep, got, before, stay, leave):
        halve(Place(inner).z_high, keep, got, stay, leave)

    def halve(bit, keep, got, stay, leave):
        for i in range(stay.shape[0]):
            for out, k in ((leave, 1), (stay, 0)):
                at = 2 * i + flip(bit, k)
                out[i] = (keep[at].astype(F32) + got[at].astype(F32)).astype(BF16)

    def add(a, b, before, out):
        out[...] = (a[...].astype(F32) + b[...].astype(F32)).astype(BF16)

    def assemble_up(p0, p1, p2, p3, out):
        place = Place(inner)
        for k, piece in enumerate((p0, p1, p2, p3)):
            y, core = flip(place.y, k // 2), flip(place.core, k % 2)
            rows = pl.ds(pl.multiple_of(y * 48, 16), 48)
            for j in range(4):
                for t in range(3):
                    cols = pl.ds(pl.multiple_of((2 * j + core) * 384 + t * 128, 128), 128)
                    out[rows, cols] = piece[0, pl.ds((3 * j + t) * 48, 48), :].astype(F32)

    def assemble_down(mine, across, partner, partner_across, out):
        place = Place(inner)

        def write(own, other):
            for k, piece in enumerate((own, other)):
                for t in range(3):
                    cols = pl.ds(pl.multiple_of(flip(place.y, k) * 384 + t * 128, 128), 128)
                    out[:, cols] = piece[0, pl.ds(t * 384, 384), :].astype(F32)

        @pl.when(place.core == place.x)
        def _():
            write(mine, across)

        @pl.when(place.core != place.x)
        def _():
            write(partner, partner_across)

    def assemble_rest(p0, p1, p2, p3, out_o, qkv_o, gain1, shift1, qv, out_b, gain2, shift2, up_b, down_b):
        place = Place(inner)
        total = jnp.zeros((16, 128), F32)
        for k, piece in enumerate((p0, p1, p2, p3)):
            y, core = flip(place.y, k // 2), flip(place.core, k % 2)
            rows = pl.ds(pl.multiple_of(core * 48, 16), 48)
            for t in range(3):
                cols = pl.ds(pl.multiple_of(y * 384 + t * 128, 128), 128)
                out_o[rows, cols] = piece[0, pl.ds(432 + t * 48, 48), :].astype(F32)
                for n in range(3):
                    cols = pl.ds(pl.multiple_of(n * 768 + y * 384 + t * 128, 128), 128)
                    qkv_o[rows, cols] = piece[0, pl.ds((3 * n + t) * 48, 48), :].astype(F32)
            total += piece[0, pl.ds(576, 16), :].astype(F32)

        def lay(out, start, count):
            parts = [total[start + r : start + r + 1, 0:96] for r in range(count)]
            out[...] = jnp.concatenate(parts, axis=1).reshape(count * 96)

        for out, start, count in (
            (gain1, 0, 1), (shift1, 1, 1), (qv, 2, 2), (out_b, 4, 1), (gain2, 5, 1), (shift2, 6, 1),
            (up_b, 7, 4), (down_b, 11, 1),
        ):
            lay(out, start, count)

    return locals()


def build(seq_size, blk_size):
    inner = seq_size // SLOTS
    kernels = build_kernels(inner)

    def swap(x, axis, size, step):
        return lax.ppermute(x, axis, [(i, i ^ step) for i in range(size)])

    def core_swap(x):
        return swap(x, "blk", blk_size, 1)

    def y_swap(x):
        return swap(x, "blk", blk_size, 2)

    def seq_swap(x, step):
        return swap(x, "seq", seq_size, step * inner)

    def some(x, moved):
        pairs = []
        for s in range(seq_size):
            for b in range(blk_size):
                to = moved(s, b)
                if to is not None:
                    pairs.append((s * blk_size + b, to[0] * blk_size + to[1]))
        return lax.ppermute(x, ("seq", "blk"), pairs)

    def aligned(s, b):
        return (s // inner) % 2 == b % 2

    def gather(x):
        across = y_swap(x)
        return x, core_swap(x), across, core_swap(across)

    def halve(name, keep, got, before):
        n, rows, lanes = keep.shape
        shape = ((n // 2, rows, lanes), BF16)
        return call(kernels[name], (shape, shape), [VMEM, VMEM, ANY], (keep, got, before), us=US)

    def add(a, b, before):
        return call(kernels["add"], ((a.shape, BF16),), [VMEM, VMEM, ANY], (a, b, before), us=US)[0]

    def on_device(
        tokens, ln1_gain, ln1_bias, wqkv, bias_qv, wout, output_bias, ln2_gain, ln2_bias,
        wup, up_bias, wdown, down_bias, segment_ids, dy,
    ):
        t1 = core_swap(tokens)
        t2 = y_swap(tokens)
        hbm = in_hbm(
            tokens, segment_ids, ln1_gain, ln1_bias, bias_qv, output_bias, ln2_gain, ln2_bias, down_bias,
            up_bias, wqkv, wout, wup, wdown,
        )
        near_qkv, same, vec, up_row, t0, wqkv, wout, wup, wdown = call(
            kernels["near"],
            (
                ((128, 2304), BF16), ((256, 256), F32), ((8, 768), F32), ((1, 1536), F32), ((2, 64, 768), BF16),
                ((768, 2304), BF16), ((768, 768), BF16), ((768, 1536), BF16), ((1536, 768), BF16),
            ),
            [VMEM] + [HBM] * 14,
            (t1, *hbm),
            [pltpu.VMEM((128, 768), BF16), pltpu.VMEM((2, 256), jnp.int32)]
            + [pltpu.VMEM((n,), BF16) for n in (768, 768, 1536, 768, 768, 768, 768, 3072)]
            + [pltpu.SemaphoreType.DMA((22,))],
            us=3.0,
        )
        near_qkv, t2 = lax.optimization_barrier((near_qkv, t2))
        t3 = core_swap(t2)
        t_pieces = t0, t1, t2, t3
        d_pieces = gather(dy)
        att, mine = call(
            kernels["attention"],
            (((256, 768), BF16), ((256, 1152), BF16)),
            [VMEM] * 6,
            (near_qkv, same, vec, t2, t3, wqkv),
            [pltpu.VMEM((128, 768), BF16), pltpu.VMEM((128, 2304), BF16), pltpu.VMEM((256, 2304), BF16)],
            us=US,
        )
        att_other = core_swap(att)
        chunk, half = ((4, 576, 128), BF16), ((2, 1152, 128), BF16)
        own = (2, 64, 768)
        sec, dup, act, partial, dsec, hid_core, hid_own, dy_rows = call(
            kernels["feed"],
            (
                ((512, 768), BF16), ((512, 1536), BF16), ((512, 1536), BF16), ((256, 768), BF16),
                ((256, 768), F32), ((256, 768), F32), ((128, 768), F32), ((512, 768), BF16),
            ),
            [VMEM] * 15,
            (att, att_other, *t_pieces, vec, up_row, *d_pieces, wout, wup, wdown),
            [pltpu.VMEM((2, 256, 768), BF16), pltpu.VMEM((2, 256, 768), F32)],
            us=US,
        )
        arrived = core_swap(partial)
        up_keep, up_send, down_keep, down_send, up_sums = call(
            kernels["feed_weights"],
            (chunk, chunk, half, half, ((1, 1536), F32)),
            [VMEM] * 4,
            (sec, dup, act, dy_rows),
            [pltpu.VMEM((768, 512), BF16), pltpu.VMEM((384, 512), BF16)],
            us=FILL,
        )
        exa, exb, dhid, sums, heads = call(
            kernels["attention_back"],
            (((256, 768), BF16), ((320, 768), BF16), ((64, 768), F32), ((8, 768), F32), ((8, 384), F32)),
            [VMEM] * 12,
            (dsec, arrived, hid_core, *d_pieces, vec, same, mine, wout, up_sums),
            [pltpu.VMEM((256, 768), BF16), pltpu.VMEM((256, 384), BF16)],
            us=US,
        )
        exa_other, exb_other = core_swap(exa), core_swap(exb)
        rest = ((4, 592, 128), BF16)
        first_t, att_t, part, part_send = call(
            kernels["turn"],
            (((384, 512), BF16), ((384, 512), BF16), (own, F32), (own, BF16)),
            [VMEM] * 9 + [ANY],
            (att, att_other, *t_pieces, vec, act, wdown, sums),
            [pltpu.VMEM((2, 256, 768), BF16), pltpu.VMEM((2, 256, 768), BF16), pltpu.VMEM((768, 512), BF16)],
            us=FILL,
        )
        rest_keep, rest_send, dfirst_own, dfirst_send = call(
            kernels["attention_weights"],
            (rest, rest, (own, F32), (own, BF16)),
            [VMEM] * 13,
            (exa, exb, exa_other, exb_other, first_t, att_t, t0, t2, vec, sums, heads, up_sums, wqkv),
            [
                pltpu.VMEM((2, 256, 768), BF16), pltpu.VMEM((2, 256, 768), BF16),
                pltpu.VMEM((2, 4, 16, 128), F32),
            ],
            us=US,
        )
        down_stay, down_leave = halve("halve_z_high", down_keep, seq_swap(down_send, 2), rest_keep)
        up_stay, up_leave = halve("halve_z_low", up_keep, seq_swap(up_send, 1), down_stay)
        down_part = add(down_stay, seq_swap(down_leave, 4), up_stay)
        up_stay, up_leave = halve("halve_z_high", up_stay, seq_swap(up_leave, 2), down_part)
        rest_stay, rest_leave = halve("halve_z_low", rest_keep, seq_swap(rest_send, 1), up_stay)
        over_x = some(down_part, lambda s, b: None if aligned(s, b) else (s ^ inner, b))
        down_sum = add(down_part, over_x, rest_stay)
        up_sum = add(up_stay, seq_swap(up_leave, 4), down_sum)
        rest_stay, rest_leave = halve("halve_z_high", rest_stay, seq_swap(rest_leave, 2), up_sum)
        rest_sum = add(rest_stay, seq_swap(rest_leave, 4), up_sum)
        up_pieces = gather(up_sum)
        across = some(down_sum, lambda s, b: (s, b ^ 2) if aligned(s, b) else None)
        to_core = lambda s, b: (s, b ^ 1) if aligned(s, b) else None
        down_pieces = down_sum, across, some(down_sum, to_core), some(across, to_core)
        in_grad, block_out = call(
            kernels["input_grad"],
            ((own, BF16), (own, BF16)),
            [VMEM] * 9,
            (
                t0, dfirst_own, y_swap(dfirst_send), dhid, exb_other, vec, hid_own, part,
                core_swap(part_send),
            ),
            us=US,
        )
        (up_o,) = call(kernels["assemble_up"], (((96, 3072), F32),), [VMEM] * 4, up_pieces, us=US)
        (down_o,) = call(kernels["assemble_down"], (((384, 768), F32),), [VMEM] * 4, down_pieces, us=US)
        small = [96, 96, 192, 96, 96, 96, 384, 96]
        across = y_swap(rest_sum)
        hop, in_grad, up_o, down_o = lax.optimization_barrier((across, in_grad, up_o, down_o))
        out_o, qkv_o, *vectors = call(
            kernels["assemble_rest"],
            (((96, 768), F32), ((96, 2304), F32)) + tuple(((n,), F32) for n in small),
            [VMEM] * 4,
            (rest_sum, core_swap(rest_sum), hop, core_swap(hop)),
            us=US,
        )
        gain1, shift1, qv, out_b, gain2, shift2, up_b, down_b = vectors
        outs = [gain1, shift1, qkv_o, qv, out_o, out_b, gain2, shift2, up_o, up_b, down_o, down_b]
        if inner > 1:
            groups = [list(range(g * inner, g * inner + inner)) for g in range(SLOTS)]
            outs = [
                lax.psum_scatter(o, "seq", scatter_dimension=0, axis_index_groups=groups, tiled=True)
                for o in outs
            ]
        return (block_out, in_grad, *outs)

    return on_device


def solution(mesh):
    data, vector, matrix = P("seq", "blk", None), P("seq"), P("seq", None)
    return jax.shard_map(
        build(mesh.shape["seq"], mesh.shape["blk"]),
        mesh=mesh,
        in_specs=(data,) + (P(),) * 12 + (matrix, data),
        out_specs=(
            data, data, vector, vector, matrix, vector, matrix, vector, vector, vector,
            matrix, vector, matrix, vector,
        ),
        check_vma=False,
    )
```

```python
import jax
import jax.numpy as jnp
from jax import lax
from jax.experimental import pallas as pl
from jax.experimental.pallas import tpu as pltpu
from jax.sharding import PartitionSpec as P

HEADS = 12
EPS = 1e-06
SLOTS = 8
F32 = jnp.float32
BF16 = jnp.bfloat16
GELU_C = 0.7978845608028654
GELU_A = 0.044715
US = 0.01
FILL = 20.0
STEP = 0.2
VMEM = pl.BlockSpec(memory_space=pltpu.VMEM)
HBM = pl.BlockSpec(memory_space=pltpu.HBM)
ANY = pl.BlockSpec(memory_space=pl.ANY)


def nn(a, b):
    return lax.dot_general(a, b, (((1,), (0,)), ((), ())), preferred_element_type=F32)


def nt(a, b):
    return lax.dot_general(a, b, (((1,), (1,)), ((), ())), preferred_element_type=F32)


def tn(a, b):
    return lax.dot_general(a, b, (((0,), (0,)), ((), ())), preferred_element_type=F32)


def standardize(x):
    centered = x - jnp.mean(x, axis=-1, keepdims=True)
    rstd = lax.rsqrt(jnp.mean(centered * centered, axis=-1, keepdims=True) + EPS)
    return centered * rstd, rstd


def norm_back(xhat, rstd, g):
    return rstd * (
        g
        - jnp.mean(g, axis=-1, keepdims=True)
        - xhat * jnp.mean(g * xhat, axis=-1, keepdims=True)
    )


def row(ref):
    return ref[...].astype(F32).reshape(1, -1)


def half_masks():
    lane = lax.broadcasted_iota(jnp.int32, (1, 128), 1)
    low = jnp.where(lane < 64, 1.0, 0.0)
    return low.astype(BF16), (1.0 - low).astype(BF16)


def flip(bit, k):
    return lax.rem(bit + k, 2)


def softmax_parts(scores, mask):
    scores = scores + mask
    e = jnp.exp(scores - jnp.max(scores, axis=-1, keepdims=True))
    return e, 1.0 / jnp.sum(e, axis=-1, keepdims=True)


def column_sum(x):
    return jnp.sum(x.astype(F32), axis=0, keepdims=True)


def call(kernel, outs, ins, args, scratch=(), limit=24, us=2.0):
    return pl.pallas_call(
        kernel,
        out_shape=tuple(jax.ShapeDtypeStruct(s, d) for s, d in outs),
        in_specs=ins,
        out_specs=tuple(VMEM for _ in outs),
        scratch_shapes=list(scratch),
        compiler_params=pltpu.CompilerParams(vmem_limit_bytes=limit * 1024 * 1024),
        cost_estimate=pl.CostEstimate(
            flops=int(us * 1e9), bytes_accessed=int(us * 1e5), transcendentals=0
        ),
        name=kernel.__name__,
    )(*args)


def in_hbm(*arrays):
    return tuple(pltpu.with_memory_space_constraint(a, pltpu.HBM) for a in arrays)


class Place:
    def __init__(self, inner):
        b = lax.axis_index("blk")
        slot = lax.axis_index("seq") // inner
        self.y, self.core = b // 2, lax.rem(b, 2)
        self.x, self.z_low, self.z_high = lax.rem(slot, 2), lax.rem(slot // 2, 2), slot // 4


def crop_mask(place, seg):
    ids = jnp.broadcast_to(seg[pl.ds(place.core, 1), :], (256, 256))
    first, second = ids[:, 0:128], ids[:, 128:256]
    tiles = jnp.where(place.y == 1, second, first), jnp.where(place.y == 1, first, second)
    tiles = [jnp.where(place.core == 1, pltpu.roll(t, 64, 1), t) for t in tiles]
    wide = jnp.concatenate(tiles, axis=1)
    return jnp.where(wide == wide.T, 0.0, -1e9)


def pick_rows(transposed, chosen, part, x_bit):
    for k in range(2):
        for z in range(4):
            start = pl.multiple_of((2 * z + flip(x_bit, k)) * 96 + part * 48, 16)
            chosen[pl.ds((4 * k + z) * 48, 48), :] = transposed[pl.ds(start, 48), :]


def put_slots(product, keep, send, offset):
    for t in range(product.shape[1] // 128):
        for z in range(4):
            tile = product[:, t * 128 : t * 128 + 128]
            keep[z, pl.ds(offset + t * 48, 48), :] = tile[z * 48 : z * 48 + 48]
            send[z, pl.ds(offset + t * 48, 48), :] = tile[192 + z * 48 : 240 + z * 48]


def gather_rows(pieces, out):
    for s in range(2):
        for p, piece in enumerate(pieces):
            out[pl.ds(s * 256 + p * 64, 64), :] = piece[s]


def both_cores(core, own, other, out):
    for p in range(4):
        out[core, pl.ds(p * 64, 64), :] = own[pl.ds(p * 64, 64), :]
        out[1 - core, pl.ds(p * 64, 64), :] = other[pl.ds((p ^ 1) * 64, 64), :]


def build_kernels(inner):
    def near(
        t1, dy_hbm, tokens_hbm, seg_hbm, g1_hbm, s1_hbm, qv_hbm, ob_hbm, g2_hbm, s2_hbm, db_hbm, ub_hbm,
        wqkv_hbm, wout_hbm, wup_hbm, wdown_hbm,
        near_o, same_o, vec_o, up_bias_o, t0, d0, wqkv, wout, wup, wdown,
        first, seg, g1, s1, qv, ob, g2, s2, db, ub, sem,
    ):
        place = Place(inner)
        pairs = [
            (g1_hbm, g1), (s1_hbm, s1), (qv_hbm, qv), (ob_hbm, ob), (g2_hbm, g2), (s2_hbm, s2),
            (db_hbm, db), (ub_hbm, ub), (seg_hbm, seg), (tokens_hbm, t0), (dy_hbm, d0),
        ]
        small = len(pairs)
        pairs += [(wqkv_hbm.at[:, pl.ds(n * 768, 768)], wqkv.at[:, pl.ds(n * 768, 768)]) for n in range(3)]
        pairs.append((wout_hbm, wout))
        for j in range(4):
            units = pl.ds(pl.multiple_of((2 * j + place.core) * 384, 128), 384)
            mine = pl.ds(j * 384, 384)
            pairs += [(wup_hbm.at[:, units], wup.at[:, mine]), (wdown_hbm.at[units, :], wdown.at[mine, :])]
        loads = [pltpu.make_async_copy(a, b, sem.at[i]) for i, (a, b) in enumerate(pairs)]
        for load in loads:
            load.start()
        for load in loads[:small]:
            load.wait()
        both = row(qv)
        for r, value in enumerate(
            (row(g1), row(s1), both[:, 0:768], both[:, 768:1536], row(ob), row(g2), row(s2), row(db))
        ):
            vec_o[r : r + 1, :] = value
        flat = row(ub)
        for j in range(4):
            start = 2 * j * 384
            up_bias_o[:, pl.ds(j * 384, 384)] = jnp.where(
                place.core == 1, flat[:, start + 384 : start + 768], flat[:, start : start + 384]
            )
        same_o[...] = crop_mask(place, seg)
        for p, t in enumerate((t0, t1)):
            xhat, _ = standardize(t[place.core].astype(F32))
            first[pl.ds(p * 64, 64), :] = (xhat * vec_o[0:1, :] + vec_o[1:2, :]).astype(BF16)
        for n in range(3):
            loads[small + n].wait()
            project(n, first[...], wqkv, vec_o, near_o)
        for load in loads[small + 3 :]:
            load.wait()

    def project(n, first, wqkv, vec, out):
        cols = pl.ds(n * 768, 768)
        value = nn(first, wqkv[:, cols])
        if n != 1:
            value = value + vec[2 + n // 2 : 3 + n // 2, :]
        value = value.astype(BF16)
        out[:, cols] = value * BF16(0.125) if n == 0 else value

    def split_sequences(tokens, mine, away):
        core = Place(inner).core
        mine[...] = tokens[core]
        away[...] = tokens[1 - core]

    def attention(near_in, mask, vec, t2, t3, wqkv, before, atta_o, attb_o, mine_o, probs_o, first, far, qkv):
        place = Place(inner)
        for p, t in enumerate((t2[place.core], t3[...])):
            xhat, _ = standardize(t.astype(F32))
            first[pl.ds(p * 64, 64), :] = (xhat * vec[0:1, :] + vec[1:2, :]).astype(BF16)
        for n in range(3):
            project(n, first[...], wqkv, vec, far)
        qkv[0:128, :] = near_in[...]
        qkv[128:256, :] = far[...]
        low, high = half_masks()
        for half in range(2):
            for j in range(HEADS // 4):
                start = flip(place.y, half) * 384 + j * 128
                cols = [pl.ds(pl.multiple_of(n * 768 + start, 128), 128) for n in range(3)]
                q, k, v = (qkv[:, c] for c in cols)
                out = None
                for h, keep in enumerate((low, high)):
                    e, scale = softmax_parts(nt(q * keep, k), mask[...])
                    if half == 0:
                        probs = e * scale
                        probs_o[2 * j + h] = probs
                        part = nn(probs.astype(BF16), v * keep)
                    else:
                        part = nn(e.astype(BF16), v * keep) * scale
                    out = part if out is None else out + part
                (atta_o, attb_o)[half][:, pl.ds(j * 128, 128)] = out.astype(BF16)
                if half == 0:
                    for n, value in enumerate((q, k, v)):
                        mine_o[:, pl.ds(n * 384 + j * 128, 128)] = value

    def residual(
        atta, attb, othera, otherb, t0, t1, t2, t3_core, t3_away, vec, wout,
        att_own_o, att_other_o, sec_o, hid_core_o, hid_own_o, t3_o,
        att, hid,
    ):
        place = Place(inner)
        for out, halves in ((att_own_o, (atta, attb)), (att_other_o, (othera, otherb))):
            for n, part in enumerate(halves):
                cols = pl.ds(pl.multiple_of(flip(place.y, n) * 384, 128), 384)
                out[:, cols] = part[...]
        both_cores(place.core, att_own_o, att_other_o, att)
        t3_o[place.core] = t3_core[...]
        t3_o[1 - place.core] = t3_away[...]
        g, b, ob = vec[5:6, :], vec[6:7, :], vec[4:5, :]
        for s in range(2):
            added = nn(att[s], wout[...]) + ob
            for p, t in enumerate((t0, t1, t2, t3_o)):
                h = t[s].astype(F32) + added[p * 64 : p * 64 + 64]
                hid[s, pl.ds(p * 64, 64), :] = h
                xhat, _ = standardize(h)
                sec_o[pl.ds(s * 256 + p * 64, 64), :] = (xhat * g + b).astype(BF16)
            hid_own_o[pl.ds(s * 64, 64), :] = hid[s, 0:64, :]
        hid_core_o[...] = hid[place.core]

    def feed(sec_o, up_bias, d0, d1, d2, d3, wup, wdown, dup_o, act_o, send_o, dsec_o, dy_o):
        place = Place(inner)
        gather_rows((d0, d1, d2, d3), dy_o)
        for j in range(4):
            cols = pl.ds(j * 384, 384)
            for s in range(2):
                rows = pl.ds(s * 256, 256)
                up = nn(sec_o[rows, :], wup[:, cols]) + up_bias[:, cols]
                da = nt(dy_o[rows, :], wdown[cols, :])
                square = up * up
                tanh = jnp.tanh(up * (GELU_C + (GELU_C * GELU_A) * square))
                cdf = 0.5 + 0.5 * tanh
                act_o[rows, cols] = (up * cdf).astype(BF16)
                slope = cdf + (1.0 - tanh * tanh) * (
                    up * ((0.5 * GELU_C) + (1.5 * GELU_C * GELU_A) * square)
                )
                dup_o[rows, cols] = (da * slope).astype(BF16)
        away = nt(dup_o[pl.ds(pl.multiple_of((1 - place.core) * 256, 256), 256), :], wup[...])
        for p in range(4):
            send_o[pl.ds(p * 64, 64), :] = away[(p ^ 1) * 64 : (p ^ 1) * 64 + 64].astype(BF16)
        dsec_o[...] = nt(dup_o[pl.ds(pl.multiple_of(place.core * 256, 256), 256), :], wup[...])

    def feed_weights(sec, dup, act, dy, up_keep, up_send, down_keep, down_send, bias_o, turned, chosen):
        place = Place(inner)
        turned[...] = sec[...].T
        pick_rows(turned, chosen, place.y, place.x)
        for j in range(4):
            cols = pl.ds(j * 384, 384)
            put_slots(nn(chosen[...], dup[:, cols]).astype(BF16), up_keep, up_send, j * 144)
            bias_o[:, cols] = column_sum(dup[0:128, cols]) + column_sum(dup[256:384, cols])
        dy_half = dy[:, pl.ds(pl.multiple_of(place.y * 384, 128), 384)]
        for k, out in enumerate((down_keep, down_send)):
            for z in range(2):
                j = 2 * z + flip(place.z_low, k)
                units = pl.ds(pl.multiple_of(j * 384, 128), 384)
                product = tn(act[:, units], dy_half).astype(BF16)
                for h in range(2):
                    for t in range(3):
                        out[z, h, pl.ds(t * 192, 192), :] = product[
                            h * 192 : h * 192 + 192, t * 128 : t * 128 + 128
                        ]

    def attention_back(
        dsec_in, got, hid_core, d0, d1, d2, d3, vec, probs_in, mine, wout, up_sums,
        exa_o, exb_o, dhid_o, sums_o, heads_o,
        dh, datt,
    ):
        place = Place(inner)
        g = vec[5:6, :]
        sums = [jnp.zeros((1, 768), F32)] * 3
        for p, d in enumerate((d0, d1, d2, d3)):
            rows = pl.ds(p * 64, 64)
            xhat, rstd = standardize(hid_core[rows, :])
            grad = dsec_in[rows, :] + got[rows, :].astype(F32)
            dhid = d[place.core].astype(F32) + norm_back(xhat, rstd, grad * g)
            low = dhid.astype(BF16)
            dh[rows, :] = low
            if p < 2:
                sums = [a + column_sum(v) for a, v in zip(sums, (low, grad * xhat, grad))]
            if p == 0:
                dhid_o[...] = dhid
            if p == 1:
                exb_o[pl.ds(256, 64), :] = low
        for r in range(3):
            sums_o[r : r + 1, :] = sums[r]
        sums_o[3:4, :] = column_sum(d0[0]) + column_sum(d0[1])
        sums_o[4:8, :] = jnp.zeros((4, 768), F32)
        exb_o[0:256, 384:768] = dh[:, pl.ds(pl.multiple_of(place.y * 384, 128), 384)]
        datt[...] = nt(dh[...], wout[pl.ds(pl.multiple_of(place.y * 384, 128), 384), :]).astype(BF16)
        low, high = half_masks()
        for j in range(HEADS // 4):
            cols = pl.ds(j * 128, 128)
            q, k, v = (mine[:, pl.ds(n * 384 + j * 128, 128)] for n in range(3))
            da = datt[:, cols]
            dq = dk = dv = None
            for h, keep in enumerate((low, high)):
                qh, kh, dah = q * keep, k * keep, da * keep
                probs = probs_in[2 * j + h]
                dprobs = nt(dah, v)
                delta = jnp.sum(probs * dprobs, axis=-1, keepdims=True)
                ds = (probs * (dprobs - delta)).astype(BF16)
                parts = nn(ds, kh), tn(ds, qh), tn(probs.astype(BF16), dah)
                if dq is None:
                    dq, dk, dv = parts
                else:
                    dq, dk, dv = dq + parts[0], dk + parts[1], dv + parts[2]
            dq = (dq * 0.125).astype(BF16)
            dv = dv.astype(BF16)
            exa_o[:, cols] = dq
            exa_o[:, pl.ds(384 + j * 128, 128)] = dk.astype(BF16)
            exb_o[0:256, cols] = dv
            heads_o[0:1, cols] = column_sum(dq)
            heads_o[1:2, cols] = column_sum(dv)
        heads_o[2:8, :] = jnp.zeros((6, 384), F32)

    def turn(
        att_own, att_other, t0, t1, t2, t3, params, act, wdown, before,
        first_o, att_o, part_o, part_send,
        first, att, turned,
    ):
        place = Place(inner)
        both_cores(place.core, att_own, att_other, att)
        for s in range(2):
            for p, t in enumerate((t0, t1, t2, t3)):
                xhat, _ = standardize(t[s].astype(F32))
                first[s, pl.ds(p * 64, 64), :] = (xhat * params[0:1, :] + params[1:2, :]).astype(BF16)
        for source, chosen in ((first, first_o), (att, att_o)):
            for s in range(2):
                turned[:, pl.ds(s * 256, 256)] = source[s].T
            pick_rows(turned, chosen, place.core, place.x)
        for s in range(2):
            part = nn(act[pl.ds(s * 256, 128), :], wdown[...])
            part_o[s] = part[0:64]
            part_send[s] = part[64:128].astype(BF16)

    def attention_weights(
        owna, ownb, othera, otherb, first, att, t0, t2, params, sums, heads, up_sums, wqkv,
        keep, send, dfirst_own, dfirst_send,
        exa, exb, rows, vec,
    ):
        place = Place(inner)
        weights = [wqkv[:, pl.ds(pl.multiple_of(n * 768 + place.y * 384, 128), 384)] for n in range(3)]
        both_cores(place.core, owna, othera, exa)
        both_cores(place.core, ownb, otherb, exb)
        for chosen, source, lanes, offset in (
            (first, exa, slice(0, 768), 0),
            (first, exb, slice(0, 384), 288),
            (att, exb, slice(384, 768), 432),
        ):
            product = nn(chosen[:, 0:256], source[0, :, lanes]) + nn(chosen[:, 256:512], source[1, :, lanes])
            put_slots(product.astype(BF16), keep, send, offset)
        dgain = jnp.zeros((1, 768), F32)
        dshift = jnp.zeros((1, 768), F32)
        pieces = [(s, p, t) for s in range(2) for p, t in ((0, t0), (2, t2))]
        for i, (s, p, t) in enumerate(pieces):
            rows[pl.ds(i * 64, 64), 0:768] = exa[s, pl.ds(p * 64, 64), :]
            rows[pl.ds(i * 64, 64), 768:1152] = exb[s, pl.ds(p * 64, 64), 0:384]
        parts = sum(nt(rows[:, pl.ds(n * 384, 384)], weights[n]) for n in range(3))
        for i, (s, p, t) in enumerate(pieces):
            part = parts[i * 64 : i * 64 + 64]
            xhat, _ = standardize(t[s].astype(F32))
            dgain += column_sum(part * xhat)
            dshift += column_sum(part)
            if p == 0:
                dfirst_own[s] = part
            else:
                dfirst_send[s] = part.astype(BF16)
        vec[...] = jnp.zeros_like(vec)
        for s in range(SLOTS):
            k, z = flip(place.x, s % 2), s // 2
            lanes = slice(s * 96, s * 96 + 96)
            vec[k, z, 0:1, 0:96] = dgain[:, lanes]
            vec[k, z, 1:2, 0:96] = dshift[:, lanes]
            vec[k, z, 4:5, 0:96] = sums[0:1, lanes]
            vec[k, z, 5:6, 0:96] = sums[1:2, lanes]
            vec[k, z, 6:7, 0:96] = sums[2:3, lanes]
            vec[k, z, 11:12, 0:96] = sums[3:4, lanes]
        for h in range(2):
            for n in range(2):
                for r in range(2):
                    start = h * 192 + r * 96
                    vec[flip(place.x, h), 2 * n + place.y, 2 + r : 3 + r, 0:96] = heads[
                        n : n + 1, start : start + 96
                    ]
        for z in range(4):
            for r in range(4):
                start = z * 384 + r * 96
                vec[flip(place.x, place.core), z, 7 + r : 8 + r, 0:96] = up_sums[:, start : start + 96]
        for z in range(4):
            keep[z, pl.ds(576, 16), :] = vec[0, z].astype(BF16)
            send[z, pl.ds(576, 16), :] = vec[1, z].astype(BF16)

    def input_grad(
        tokens, dfirst, received, dhid, other, vec, hid_own, part, part_got, before,
        out, block_o, mark,
    ):
        mark[...] = jnp.zeros_like(mark)
        place = Place(inner)

        def write(s, residual):
            xhat, rstd = standardize(tokens[s].astype(F32))
            grad = dfirst[s] + received[s].astype(F32)
            out[s] = (residual + norm_back(xhat, rstd, grad * vec[0:1, :])).astype(BF16)

        write(place.core, dhid[...])
        write(1 - place.core, other[256:320, :].astype(F32))
        for s in range(2):
            added = part[s] + part_got[s].astype(F32) + vec[7:8, :]
            block_o[s] = (hid_own[pl.ds(s * 64, 64), :] + added).astype(BF16)

    def halve_z_low(keep, got, before, stay, leave):
        halve(Place(inner).z_low, keep, got, stay, leave)

    def halve_z_high(keep, got, before, stay, leave):
        halve(Place(inner).z_high, keep, got, stay, leave)

    def halve(bit, keep, got, stay, leave):
        for i in range(stay.shape[0]):
            for out, k in ((leave, 1), (stay, 0)):
                at = 2 * i + flip(bit, k)
                out[i] = (keep[at].astype(F32) + got[at].astype(F32)).astype(BF16)

    def add(a, b, before, out):
        out[...] = (a[...].astype(F32) + b[...].astype(F32)).astype(BF16)

    def add_split(a, b, before, kept, sent):
        core = Place(inner).core
        for out, k in ((sent, 1), (kept, 0)):
            at = flip(core, k)
            out[...] = (a[0, at].astype(F32) + b[0, at].astype(F32)).astype(BF16)

    def pick(kept, got, before, own, other):
        place = Place(inner)

        def write(mine, others):
            own[...] = mine[...]
            other[...] = others[...]

        @pl.when(place.core == place.x)
        def _():
            write(kept, got)

        @pl.when(place.core != place.x)
        def _():
            write(got, kept)

    def assemble_feed(a0, a1, a2, a3, b0, b1, b2, b3, up_o, down_o):
        place = Place(inner)
        for k, (up, down) in enumerate(((a0, b0), (a1, b1), (a2, b2), (a3, b3))):
            y, core = flip(place.y, k // 2), flip(place.core, k % 2)
            rows = pl.ds(pl.multiple_of(y * 48, 16), 48)
            for j in range(4):
                for t in range(3):
                    cols = pl.ds(pl.multiple_of((2 * j + core) * 384 + t * 128, 128), 128)
                    up_o[rows, cols] = up[0, pl.ds((3 * j + t) * 48, 48), :].astype(F32)
            rows = pl.ds(pl.multiple_of(core * 192, 64), 192)
            for t in range(3):
                cols = pl.ds(pl.multiple_of(y * 384 + t * 128, 128), 128)
                down_o[rows, cols] = down[pl.ds(t * 192, 192), :].astype(F32)

    def assemble_rest(p0, p1, p2, p3, out_o, qkv_o, gain1, shift1, qv, out_b, gain2, shift2, up_b, down_b):
        place = Place(inner)
        total = jnp.zeros((16, 128), F32)
        for k, piece in enumerate((p0, p1, p2, p3)):
            y, core = flip(place.y, k // 2), flip(place.core, k % 2)
            rows = pl.ds(pl.multiple_of(core * 48, 16), 48)
            for t in range(3):
                cols = pl.ds(pl.multiple_of(y * 384 + t * 128, 128), 128)
                out_o[rows, cols] = piece[0, pl.ds(432 + t * 48, 48), :].astype(F32)
                for n in range(3):
                    cols = pl.ds(pl.multiple_of(n * 768 + y * 384 + t * 128, 128), 128)
                    qkv_o[rows, cols] = piece[0, pl.ds((3 * n + t) * 48, 48), :].astype(F32)
            total += piece[0, pl.ds(576, 16), :].astype(F32)

        def lay(out, start, count):
            parts = [total[start + r : start + r + 1, 0:96] for r in range(count)]
            out[...] = jnp.concatenate(parts, axis=1).reshape(count * 96)

        for out, start, count in (
            (gain1, 0, 1), (shift1, 1, 1), (qv, 2, 2), (out_b, 4, 1), (gain2, 5, 1), (shift2, 6, 1),
            (up_b, 7, 4), (down_b, 11, 1),
        ):
            lay(out, start, count)

    return locals()


def build(seq_size, blk_size):
    inner = seq_size // SLOTS
    kernels = build_kernels(inner)

    def swap(x, axis, size, step):
        return lax.ppermute(x, axis, [(i, i ^ step) for i in range(size)])

    def core_swap(x):
        return swap(x, "blk", blk_size, 1)

    def y_swap(x):
        return swap(x, "blk", blk_size, 2)

    def seq_swap(x, step):
        return swap(x, "seq", seq_size, step * inner)

    def gather(x):
        across = y_swap(x)
        return x, core_swap(x), across, core_swap(across)

    def halve(name, keep, got, before):
        shape = ((keep.shape[0] // 2, *keep.shape[1:]), BF16)
        return call(kernels[name], (shape, shape), [VMEM, VMEM, ANY], (keep, got, before), us=STEP)

    def add(a, b, before, us):
        return call(kernels["add"], ((a.shape, BF16),), [VMEM, VMEM, ANY], (a, b, before), us=us)[0]

    def on_device(
        tokens, ln1_gain, ln1_bias, wqkv, bias_qv, wout, output_bias, ln2_gain, ln2_bias,
        wup, up_bias, wdown, down_bias, segment_ids, dy,
    ):
        t1 = core_swap(tokens)
        t2 = y_swap(tokens)
        hbm = in_hbm(
            dy, tokens, segment_ids, ln1_gain, ln1_bias, bias_qv, output_bias, ln2_gain, ln2_bias, down_bias,
            up_bias, wqkv, wout, wup, wdown,
        )
        near_qkv, mask, vec, up_row, t0, d0, wqkv, wout, wup, wdown = call(
            kernels["near"],
            (
                ((128, 2304), BF16), ((256, 256), F32), ((8, 768), F32), ((1, 1536), F32), ((2, 64, 768), BF16), ((2, 64, 768), BF16),
                ((768, 2304), BF16), ((768, 768), BF16), ((768, 1536), BF16), ((1536, 768), BF16),
            ),
            [VMEM] + [HBM] * 15,
            (t1, *hbm),
            [pltpu.VMEM((128, 768), BF16), pltpu.VMEM((2, 256), jnp.int32)]
            + [pltpu.VMEM((n,), BF16) for n in (768, 768, 1536, 768, 768, 768, 768, 3072)]
            + [pltpu.SemaphoreType.DMA((23,))],
            us=3.0,
        )
        near_qkv, t2 = lax.optimization_barrier((near_qkv, t2))
        rows = ((64, 768), BF16)
        t2_core, t2_away = call(kernels["split_sequences"], (rows, rows), [VMEM], (t2,), us=US)
        t3_core, t3_away = core_swap(t2_away), core_swap(t2_core)
        d_pieces = gather(d0)
        atta, attb, mine, probs = call(
            kernels["attention"],
            (((256, 384), BF16), ((256, 384), BF16), ((256, 1152), BF16), ((6, 256, 256), F32)),
            [VMEM] * 6 + [ANY],
            (near_qkv, mask, vec, t2, t3_core, wqkv, t3_away),
            [pltpu.VMEM((128, 768), BF16), pltpu.VMEM((128, 2304), BF16), pltpu.VMEM((256, 2304), BF16)],
            us=US,
        )
        chunk, half = ((4, 576, 128), BF16), ((2, 2, 576, 128), BF16)
        own = (2, 64, 768)
        att, att_other, sec, hid_core, hid_own, t3 = call(
            kernels["residual"],
            (
                ((256, 768), BF16), ((256, 768), BF16), ((512, 768), BF16), ((256, 768), F32),
                ((128, 768), F32), (own, BF16),
            ),
            [VMEM] * 11,
            (atta, attb, core_swap(atta), core_swap(attb), t0, t1, t2, t3_core, t3_away, vec, wout),
            [pltpu.VMEM((2, 256, 768), BF16), pltpu.VMEM((2, 256, 768), F32)],
            us=US,
        )
        t_pieces = t0, t1, t2, t3
        dup, act, partial, dsec, dy_rows = call(
            kernels["feed"],
            (
                ((512, 1536), BF16), ((512, 1536), BF16), ((256, 768), BF16), ((256, 768), F32),
                ((512, 768), BF16),
            ),
            [VMEM] * 8,
            (sec, up_row, *d_pieces, wup, wdown),
            us=US,
        )
        arrived = core_swap(partial)
        up_keep, up_send, down_keep, down_send, up_sums = call(
            kernels["feed_weights"],
            (chunk, chunk, half, half, ((1, 1536), F32)),
            [VMEM] * 4,
            (sec, dup, act, dy_rows),
            [pltpu.VMEM((768, 512), BF16), pltpu.VMEM((384, 512), BF16)],
            us=FILL,
        )
        exa, exb, dhid, sums, heads = call(
            kernels["attention_back"],
            (((256, 768), BF16), ((320, 768), BF16), ((64, 768), F32), ((8, 768), F32), ((8, 384), F32)),
            [VMEM] * 12,
            (dsec, arrived, hid_core, *d_pieces, vec, probs, mine, wout, up_sums),
            [pltpu.VMEM((256, 768), BF16), pltpu.VMEM((256, 384), BF16)],
            us=US,
        )
        exa_other, exb_other = core_swap(exa), core_swap(exb)
        rest = ((4, 592, 128), BF16)
        first_t, att_t, part, part_send = call(
            kernels["turn"],
            (((384, 512), BF16), ((384, 512), BF16), (own, F32), (own, BF16)),
            [VMEM] * 9 + [ANY],
            (att, att_other, *t_pieces, vec, act, wdown, sums),
            [pltpu.VMEM((2, 256, 768), BF16), pltpu.VMEM((2, 256, 768), BF16), pltpu.VMEM((768, 512), BF16)],
            us=FILL,
        )
        rest_keep, rest_send, dfirst_own, dfirst_send = call(
            kernels["attention_weights"],
            (rest, rest, (own, F32), (own, BF16)),
            [VMEM] * 13,
            (exa, exb, exa_other, exb_other, first_t, att_t, t0, t2, vec, sums, heads, up_sums, wqkv),
            [
                pltpu.VMEM((2, 256, 768), BF16), pltpu.VMEM((2, 256, 768), BF16),
                pltpu.VMEM((256, 1152), BF16), pltpu.VMEM((2, 4, 16, 128), F32),
            ],
            us=US,
        )
        down_stay, down_leave = halve("halve_z_high", down_keep, seq_swap(down_send, 2), rest_keep)
        up_stay, up_leave = halve("halve_z_low", up_keep, seq_swap(up_send, 1), down_stay)
        rest_stay, rest_leave = halve("halve_z_low", rest_keep, seq_swap(rest_send, 1), up_stay)
        in_grad, block_out, mark = call(
            kernels["input_grad"],
            ((own, BF16), (own, BF16), ((8, 128), F32)),
            [VMEM] * 9 + [ANY],
            (
                t0, dfirst_own, y_swap(dfirst_send), dhid, exb_other, vec, hid_own, part,
                core_swap(part_send), rest_stay,
            ),
            us=US,
        )
        piece = ((576, 128), BF16)
        down_kept, down_sent = call(
            kernels["add_split"],
            (piece, piece),
            [VMEM, VMEM, ANY],
            (down_stay, seq_swap(down_leave, 4), mark),
            us=STEP,
        )
        up_stay, up_leave = halve("halve_z_high", up_stay, seq_swap(up_leave, 2), down_kept)
        down_own, down_other = call(
            kernels["pick"], (piece, piece), [VMEM, VMEM, ANY], (down_kept, core_swap(down_sent), up_stay), us=STEP
        )
        rest_stay, rest_leave = halve("halve_z_high", rest_stay, seq_swap(rest_leave, 2), down_own)
        up_sum = add(up_stay, seq_swap(up_leave, 4), rest_stay, STEP)
        down_sum = add(down_own, seq_swap(down_other, 1), up_sum, STEP)
        rest_sum = add(rest_stay, seq_swap(rest_leave, 4), down_sum, FILL)
        up_pieces, down_pieces, rest_across = gather(up_sum), gather(down_sum), y_swap(rest_sum)
        up_o, down_o = call(
            kernels["assemble_feed"],
            (((96, 3072), F32), ((384, 768), F32)),
            [VMEM] * 8,
            (*up_pieces, *down_pieces),
            us=US,
        )
        rest_across, up_o, down_o = lax.optimization_barrier((rest_across, up_o, down_o))
        small = [96, 96, 192, 96, 96, 96, 384, 96]
        out_o, qkv_o, *vectors = call(
            kernels["assemble_rest"],
            (((96, 768), F32), ((96, 2304), F32)) + tuple(((n,), F32) for n in small),
            [VMEM] * 4,
            (rest_sum, core_swap(rest_sum), rest_across, core_swap(rest_across)),
            us=US,
        )
        gain1, shift1, qv, out_b, gain2, shift2, up_b, down_b = vectors
        outs = [gain1, shift1, qkv_o, qv, out_o, out_b, gain2, shift2, up_o, up_b, down_o, down_b]
        if inner > 1:
            groups = [list(range(g * inner, g * inner + inner)) for g in range(SLOTS)]
            outs = [
                lax.psum_scatter(o, "seq", scatter_dimension=0, axis_index_groups=groups, tiled=True)
                for o in outs
            ]
        return (block_out, in_grad, *outs)

    return on_device


def solution(mesh):
    data, vector, matrix = P("seq", "blk", None), P("seq"), P("seq", None)
    return jax.shard_map(
        build(mesh.shape["seq"], mesh.shape["blk"]),
        mesh=mesh,
        in_specs=(data,) + (P(),) * 12 + (matrix, data),
        out_specs=(
            data, data, vector, vector, matrix, vector, matrix, vector, vector, vector,
            matrix, vector, matrix, vector,
        ),
        check_vma=False,
    )
```

```python
import jax
import jax.numpy as jnp
from jax import lax
from jax.experimental import pallas as pl
from jax.experimental.pallas import tpu as pltpu
from jax.sharding import PartitionSpec as P

HEADS = 12
EPS = 1e-06
SLOTS = 8
F32 = jnp.float32
BF16 = jnp.bfloat16
GELU_C = 0.7978845608028654
GELU_A = 0.044715
US = 0.01
FILL = 20.0
STEP = 0.2
VMEM = pl.BlockSpec(memory_space=pltpu.VMEM)
HBM = pl.BlockSpec(memory_space=pltpu.HBM)
ANY = pl.BlockSpec(memory_space=pl.ANY)


def nn(a, b):
    return lax.dot_general(a, b, (((1,), (0,)), ((), ())), preferred_element_type=F32)


def nt(a, b):
    return lax.dot_general(a, b, (((1,), (1,)), ((), ())), preferred_element_type=F32)


def tn(a, b):
    return lax.dot_general(a, b, (((0,), (0,)), ((), ())), preferred_element_type=F32)


def standardize(x):
    centered = x - jnp.mean(x, axis=-1, keepdims=True)
    rstd = lax.rsqrt(jnp.mean(centered * centered, axis=-1, keepdims=True) + EPS)
    return centered * rstd, rstd


def norm_back(xhat, rstd, g):
    return rstd * (
        g
        - jnp.mean(g, axis=-1, keepdims=True)
        - xhat * jnp.mean(g * xhat, axis=-1, keepdims=True)
    )


def row(ref):
    return ref[...].astype(F32).reshape(1, -1)


def half_masks():
    lane = lax.broadcasted_iota(jnp.int32, (1, 128), 1)
    low = jnp.where(lane < 64, 1.0, 0.0)
    return low.astype(BF16), (1.0 - low).astype(BF16)


def flip(bit, k):
    return lax.rem(bit + k, 2)


def softmax_parts(scores, mask):
    scores = scores + mask
    e = jnp.exp(scores - jnp.max(scores, axis=-1, keepdims=True))
    return e, 1.0 / jnp.sum(e, axis=-1, keepdims=True)


def column_sum(x):
    return jnp.sum(x.astype(F32), axis=0, keepdims=True)


def call(kernel, outs, ins, args, scratch=(), limit=24, us=2.0):
    return pl.pallas_call(
        kernel,
        out_shape=tuple(jax.ShapeDtypeStruct(s, d) for s, d in outs),
        in_specs=ins,
        out_specs=tuple(VMEM for _ in outs),
        scratch_shapes=list(scratch),
        compiler_params=pltpu.CompilerParams(vmem_limit_bytes=limit * 1024 * 1024),
        cost_estimate=pl.CostEstimate(
            flops=int(us * 1e9), bytes_accessed=int(us * 1e5), transcendentals=0
        ),
        name=kernel.__name__,
    )(*args)


def in_hbm(*arrays):
    return tuple(pltpu.with_memory_space_constraint(a, pltpu.HBM) for a in arrays)


class Place:
    def __init__(self, inner):
        b = lax.axis_index("blk")
        slot = lax.axis_index("seq") // inner
        self.y, self.core = b // 2, lax.rem(b, 2)
        self.x, self.z_low, self.z_high = lax.rem(slot, 2), lax.rem(slot // 2, 2), slot // 4


def crop_mask(place, seg):
    ids = jnp.broadcast_to(seg[pl.ds(place.core, 1), :], (256, 256))
    first, second = ids[:, 0:128], ids[:, 128:256]
    tiles = jnp.where(place.y == 1, second, first), jnp.where(place.y == 1, first, second)
    tiles = [jnp.where(place.core == 1, pltpu.roll(t, 64, 1), t) for t in tiles]
    wide = jnp.concatenate(tiles, axis=1)
    return jnp.where(wide == wide.T, 0.0, -1e9)


def pick_rows(transposed, chosen, part, x_bit):
    for k in range(2):
        for z in range(4):
            start = pl.multiple_of((2 * z + flip(x_bit, k)) * 96 + part * 48, 16)
            chosen[pl.ds((4 * k + z) * 48, 48), :] = transposed[pl.ds(start, 48), :]


def put_slots(product, keep, send, offset):
    for t in range(product.shape[1] // 128):
        for z in range(4):
            tile = product[:, t * 128 : t * 128 + 128]
            keep[z, pl.ds(offset + t * 48, 48), :] = tile[z * 48 : z * 48 + 48]
            send[z, pl.ds(offset + t * 48, 48), :] = tile[192 + z * 48 : 240 + z * 48]


def gather_rows(pieces, out):
    for s in range(2):
        for p, piece in enumerate(pieces):
            out[pl.ds(s * 256 + p * 64, 64), :] = piece[s]


def both_cores(core, own, other, out):
    for p in range(4):
        out[core, pl.ds(p * 64, 64), :] = own[pl.ds(p * 64, 64), :]
        out[1 - core, pl.ds(p * 64, 64), :] = other[pl.ds((p ^ 1) * 64, 64), :]


def build_kernels(inner):
    def near(
        t1, dy_hbm, tokens_hbm, seg_hbm, g1_hbm, s1_hbm, qv_hbm, ob_hbm, g2_hbm, s2_hbm, db_hbm, ub_hbm,
        wqkv_hbm, wout_hbm, wup_hbm, wdown_hbm,
        near_o, same_o, vec_o, up_bias_o, t0, d0, wqkv, wout, wup, wdown,
        first, seg, g1, s1, qv, ob, g2, s2, db, ub, sem,
    ):
        place = Place(inner)
        pairs = [
            (g1_hbm, g1), (s1_hbm, s1), (qv_hbm, qv), (ob_hbm, ob), (g2_hbm, g2), (s2_hbm, s2),
            (db_hbm, db), (ub_hbm, ub), (seg_hbm, seg), (tokens_hbm, t0), (dy_hbm, d0),
        ]
        small = len(pairs)
        pairs += [(wqkv_hbm.at[:, pl.ds(n * 768, 768)], wqkv.at[:, pl.ds(n * 768, 768)]) for n in range(3)]
        pairs.append((wout_hbm, wout))
        for j in range(4):
            units = pl.ds(pl.multiple_of((2 * j + place.core) * 384, 128), 384)
            mine = pl.ds(j * 384, 384)
            pairs += [(wup_hbm.at[:, units], wup.at[:, mine]), (wdown_hbm.at[units, :], wdown.at[mine, :])]
        loads = [pltpu.make_async_copy(a, b, sem.at[i]) for i, (a, b) in enumerate(pairs)]
        for load in loads:
            load.start()
        for load in loads[:small]:
            load.wait()
        both = row(qv)
        for r, value in enumerate(
            (row(g1), row(s1), both[:, 0:768], both[:, 768:1536], row(ob), row(g2), row(s2), row(db))
        ):
            vec_o[r : r + 1, :] = value
        flat = row(ub)
        for j in range(4):
            start = 2 * j * 384
            up_bias_o[:, pl.ds(j * 384, 384)] = jnp.where(
                place.core == 1, flat[:, start + 384 : start + 768], flat[:, start : start + 384]
            )
        same_o[...] = crop_mask(place, seg)
        for p, t in enumerate((t0, t1)):
            xhat, _ = standardize(t[place.core].astype(F32))
            first[pl.ds(p * 64, 64), :] = (xhat * vec_o[0:1, :] + vec_o[1:2, :]).astype(BF16)
        for n in range(3):
            loads[small + n].wait()
            project(n, first[...], wqkv, vec_o, near_o)
        for load in loads[small + 3 :]:
            load.wait()

    def project(n, first, wqkv, vec, out):
        cols = pl.ds(n * 768, 768)
        value = nn(first, wqkv[:, cols])
        if n != 1:
            value = value + vec[2 + n // 2 : 3 + n // 2, :]
        value = value.astype(BF16)
        out[:, cols] = value * BF16(0.125) if n == 0 else value

    def split_sequences(tokens, mine, away):
        core = Place(inner).core
        mine[...] = tokens[core]
        away[...] = tokens[1 - core]

    def attention(near_in, mask, vec, t2, t3, wqkv, before, atta_o, attb_o, mine_o, probs_o, first, far, qkv):
        place = Place(inner)
        for p, t in enumerate((t2[place.core], t3[...])):
            xhat, _ = standardize(t.astype(F32))
            first[pl.ds(p * 64, 64), :] = (xhat * vec[0:1, :] + vec[1:2, :]).astype(BF16)
        for n in range(3):
            project(n, first[...], wqkv, vec, far)
        qkv[0:128, :] = near_in[...]
        qkv[128:256, :] = far[...]
        low, high = half_masks()
        for half in range(2):
            for j in range(HEADS // 4):
                start = flip(place.y, half) * 384 + j * 128
                cols = [pl.ds(pl.multiple_of(n * 768 + start, 128), 128) for n in range(3)]
                q, k, v = (qkv[:, c] for c in cols)
                out = None
                for h, keep in enumerate((low, high)):
                    e, scale = softmax_parts(nt(q * keep, k), mask[...])
                    if half == 0:
                        probs = e * scale
                        probs_o[2 * j + h] = probs
                        part = nn(probs.astype(BF16), v * keep)
                    else:
                        part = nn(e.astype(BF16), v * keep) * scale
                    out = part if out is None else out + part
                (atta_o, attb_o)[half][:, pl.ds(j * 128, 128)] = out.astype(BF16)
                if half == 0:
                    for n, value in enumerate((q, k, v)):
                        mine_o[:, pl.ds(n * 384 + j * 128, 128)] = value

    def residual(
        atta, attb, othera, otherb, t0, t1, t2, t3_core, t3_away, vec, wout,
        att_own_o, att_other_o, sec_o, hid_core_o, hid_own_o, t3_o,
        att, hid,
    ):
        place = Place(inner)
        for out, halves in ((att_own_o, (atta, attb)), (att_other_o, (othera, otherb))):
            for n, part in enumerate(halves):
                cols = pl.ds(pl.multiple_of(flip(place.y, n) * 384, 128), 384)
                out[:, cols] = part[...]
        both_cores(place.core, att_own_o, att_other_o, att)
        t3_o[place.core] = t3_core[...]
        t3_o[1 - place.core] = t3_away[...]
        g, b, ob = vec[5:6, :], vec[6:7, :], vec[4:5, :]
        for s in range(2):
            added = nn(att[s], wout[...]) + ob
            for p, t in enumerate((t0, t1, t2, t3_o)):
                h = t[s].astype(F32) + added[p * 64 : p * 64 + 64]
                hid[s, pl.ds(p * 64, 64), :] = h
                xhat, _ = standardize(h)
                sec_o[pl.ds(s * 256 + p * 64, 64), :] = (xhat * g + b).astype(BF16)
            hid_own_o[pl.ds(s * 64, 64), :] = hid[s, 0:64, :]
        hid_core_o[...] = hid[place.core]

    def feed(sec_o, up_bias, d0, d1, d2, d3, wup, wdown, dup_o, act_o, send_o, dsec_o, dy_o):
        place = Place(inner)
        gather_rows((d0, d1, d2, d3), dy_o)
        for j in range(6):
            cols = pl.ds(j * 256, 256)
            for s in range(2):
                rows = pl.ds(s * 256, 256)
                up = nn(sec_o[rows, :], wup[:, cols]) + up_bias[:, cols]
                da = nt(dy_o[rows, :], wdown[cols, :])
                square = up * up
                tanh = jnp.tanh(up * (GELU_C + (GELU_C * GELU_A) * square))
                cdf = 0.5 + 0.5 * tanh
                act_o[rows, cols] = (up * cdf).astype(BF16)
                slope = cdf + (1.0 - tanh * tanh) * (
                    up * ((0.5 * GELU_C) + (1.5 * GELU_C * GELU_A) * square)
                )
                dup_o[rows, cols] = (da * slope).astype(BF16)
        away = nt(dup_o[pl.ds(pl.multiple_of((1 - place.core) * 256, 256), 256), :], wup[...])
        for p in range(4):
            send_o[pl.ds(p * 64, 64), :] = away[(p ^ 1) * 64 : (p ^ 1) * 64 + 64].astype(BF16)
        dsec_o[...] = nt(dup_o[pl.ds(pl.multiple_of(place.core * 256, 256), 256), :], wup[...])

    def feed_weights(sec, dup, act, dy, up_keep, up_send, down_keep, down_send, bias_o, turned, chosen):
        place = Place(inner)
        turned[...] = sec[...].T
        pick_rows(turned, chosen, place.y, place.x)
        for j in range(2):
            cols = pl.ds(j * 768, 768)
            put_slots(nn(chosen[...], dup[:, cols]).astype(BF16), up_keep, up_send, j * 288)
            bias_o[:, cols] = column_sum(dup[0:128, cols]) + column_sum(dup[256:384, cols])
        dy_half = dy[:, pl.ds(pl.multiple_of(place.y * 384, 128), 384)]
        for k, out in enumerate((down_keep, down_send)):
            for z in range(2):
                j = 2 * z + flip(place.z_low, k)
                units = pl.ds(pl.multiple_of(j * 384, 128), 384)
                product = tn(act[:, units], dy_half).astype(BF16)
                for h in range(2):
                    for t in range(3):
                        out[z, h, pl.ds(t * 192, 192), :] = product[
                            h * 192 : h * 192 + 192, t * 128 : t * 128 + 128
                        ]

    def attention_back(
        dsec_in, got, hid_core, d0, d1, d2, d3, vec, probs_in, mine, wout, up_sums,
        exa_o, exb_o, dhid_o, sums_o, heads_o,
        dh, datt,
    ):
        place = Place(inner)
        g = vec[5:6, :]
        sums = [jnp.zeros((1, 768), F32)] * 3
        for p, d in enumerate((d0, d1, d2, d3)):
            rows = pl.ds(p * 64, 64)
            xhat, rstd = standardize(hid_core[rows, :])
            grad = dsec_in[rows, :] + got[rows, :].astype(F32)
            dhid = d[place.core].astype(F32) + norm_back(xhat, rstd, grad * g)
            low = dhid.astype(BF16)
            dh[rows, :] = low
            if p < 2:
                sums = [a + column_sum(v) for a, v in zip(sums, (low, grad * xhat, grad))]
            if p == 0:
                dhid_o[...] = dhid
            if p == 1:
                exb_o[pl.ds(256, 64), :] = low
        for r in range(3):
            sums_o[r : r + 1, :] = sums[r]
        sums_o[3:4, :] = column_sum(d0[0]) + column_sum(d0[1])
        sums_o[4:8, :] = jnp.zeros((4, 768), F32)
        exb_o[0:256, 384:768] = dh[:, pl.ds(pl.multiple_of(place.y * 384, 128), 384)]
        datt[...] = nt(dh[...], wout[pl.ds(pl.multiple_of(place.y * 384, 128), 384), :]).astype(BF16)
        low, high = half_masks()
        for j in range(HEADS // 4):
            cols = pl.ds(j * 128, 128)
            q, k, v = (mine[:, pl.ds(n * 384 + j * 128, 128)] for n in range(3))
            da = datt[:, cols]
            dq = dk = dv = None
            for h, keep in enumerate((low, high)):
                qh, kh, dah = q * keep, k * keep, da * keep
                probs = probs_in[2 * j + h]
                dprobs = nt(dah, v)
                delta = jnp.sum(probs * dprobs, axis=-1, keepdims=True)
                ds = (probs * (dprobs - delta)).astype(BF16)
                parts = nn(ds, kh), tn(ds, qh), tn(probs.astype(BF16), dah)
                if dq is None:
                    dq, dk, dv = parts
                else:
                    dq, dk, dv = dq + parts[0], dk + parts[1], dv + parts[2]
            dq = (dq * 0.125).astype(BF16)
            dv = dv.astype(BF16)
            exa_o[:, cols] = dq
            exa_o[:, pl.ds(384 + j * 128, 128)] = dk.astype(BF16)
            exb_o[0:256, cols] = dv
            heads_o[0:1, cols] = column_sum(dq)
            heads_o[1:2, cols] = column_sum(dv)
        heads_o[2:8, :] = jnp.zeros((6, 384), F32)

    def turn(
        att_own, att_other, t0, t1, t2, t3, params, act, wdown, before,
        first_o, att_o, part_o, part_send,
        first, att, turned,
    ):
        place = Place(inner)
        both_cores(place.core, att_own, att_other, att)
        for s in range(2):
            for p, t in enumerate((t0, t1, t2, t3)):
                xhat, _ = standardize(t[s].astype(F32))
                first[s, pl.ds(p * 64, 64), :] = (xhat * params[0:1, :] + params[1:2, :]).astype(BF16)
        for source, chosen in ((first, first_o), (att, att_o)):
            for s in range(2):
                turned[:, pl.ds(s * 256, 256)] = source[s].T
            pick_rows(turned, chosen, place.core, place.x)
        for s in range(2):
            part = nn(act[pl.ds(s * 256, 128), :], wdown[...])
            part_o[s] = part[0:64]
            part_send[s] = part[64:128].astype(BF16)

    def attention_weights(
        owna, ownb, othera, otherb, first, att, t0, t2, params, sums, heads, up_sums, wqkv,
        keep, send, dfirst_own, dfirst_send,
        exa, exb, rows, vec,
    ):
        place = Place(inner)
        weights = [wqkv[:, pl.ds(pl.multiple_of(n * 768 + place.y * 384, 128), 384)] for n in range(3)]
        both_cores(place.core, owna, othera, exa)
        both_cores(place.core, ownb, otherb, exb)
        for chosen, source, lanes, offset in (
            (first, exa, slice(0, 768), 0),
            (first, exb, slice(0, 384), 288),
            (att, exb, slice(384, 768), 432),
        ):
            product = nn(chosen[:, 0:256], source[0, :, lanes]) + nn(chosen[:, 256:512], source[1, :, lanes])
            put_slots(product.astype(BF16), keep, send, offset)
        dgain = jnp.zeros((1, 768), F32)
        dshift = jnp.zeros((1, 768), F32)
        pieces = [(s, p, t) for s in range(2) for p, t in ((0, t0), (2, t2))]
        for i, (s, p, t) in enumerate(pieces):
            rows[pl.ds(i * 64, 64), 0:768] = exa[s, pl.ds(p * 64, 64), :]
            rows[pl.ds(i * 64, 64), 768:1152] = exb[s, pl.ds(p * 64, 64), 0:384]
        parts = sum(nt(rows[:, pl.ds(n * 384, 384)], weights[n]) for n in range(3))
        for i, (s, p, t) in enumerate(pieces):
            part = parts[i * 64 : i * 64 + 64]
            xhat, _ = standardize(t[s].astype(F32))
            dgain += column_sum(part * xhat)
            dshift += column_sum(part)
            if p == 0:
                dfirst_own[s] = part
            else:
                dfirst_send[s] = part.astype(BF16)
        vec[...] = jnp.zeros_like(vec)
        for s in range(SLOTS):
            k, z = flip(place.x, s % 2), s // 2
            lanes = slice(s * 96, s * 96 + 96)
            vec[k, z, 0:1, 0:96] = dgain[:, lanes]
            vec[k, z, 1:2, 0:96] = dshift[:, lanes]
            vec[k, z, 4:5, 0:96] = sums[0:1, lanes]
            vec[k, z, 5:6, 0:96] = sums[1:2, lanes]
            vec[k, z, 6:7, 0:96] = sums[2:3, lanes]
            vec[k, z, 11:12, 0:96] = sums[3:4, lanes]
        for h in range(2):
            for n in range(2):
                for r in range(2):
                    start = h * 192 + r * 96
                    vec[flip(place.x, h), 2 * n + place.y, 2 + r : 3 + r, 0:96] = heads[
                        n : n + 1, start : start + 96
                    ]
        for z in range(4):
            for r in range(4):
                start = z * 384 + r * 96
                vec[flip(place.x, place.core), z, 7 + r : 8 + r, 0:96] = up_sums[:, start : start + 96]
        for z in range(4):
            keep[z, pl.ds(576, 16), :] = vec[0, z].astype(BF16)
            send[z, pl.ds(576, 16), :] = vec[1, z].astype(BF16)

    def input_grad(
        tokens, dfirst, received, dhid, other, vec, hid_own, part, part_got, before,
        out, block_o, mark,
    ):
        mark[...] = jnp.zeros_like(mark)
        place = Place(inner)

        def write(s, residual):
            xhat, rstd = standardize(tokens[s].astype(F32))
            grad = dfirst[s] + received[s].astype(F32)
            out[s] = (residual + norm_back(xhat, rstd, grad * vec[0:1, :])).astype(BF16)

        write(place.core, dhid[...])
        write(1 - place.core, other[256:320, :].astype(F32))
        for s in range(2):
            added = part[s] + part_got[s].astype(F32) + vec[7:8, :]
            block_o[s] = (hid_own[pl.ds(s * 64, 64), :] + added).astype(BF16)

    def halve_z_low(keep, got, before, stay, leave):
        halve(Place(inner).z_low, keep, got, stay, leave)

    def halve_z_high(keep, got, before, stay, leave):
        halve(Place(inner).z_high, keep, got, stay, leave)

    def halve(bit, keep, got, stay, leave):
        for i in range(stay.shape[0]):
            for out, k in ((leave, 1), (stay, 0)):
                at = 2 * i + flip(bit, k)
                out[i] = (keep[at].astype(F32) + got[at].astype(F32)).astype(BF16)

    def add(a, b, before, out):
        out[...] = (a[...].astype(F32) + b[...].astype(F32)).astype(BF16)

    def add_wide(a, b, before, out):
        rows = a.shape[1]
        out[:, 0:rows, :] = (a[...].astype(F32) + b[...].astype(F32)).astype(BF16)
        out[:, rows : out.shape[1], :] = jnp.zeros((1, out.shape[1] - rows, 128), BF16)

    def add_split(a, b, before, kept, sent):
        core = Place(inner).core
        for out, k in ((sent, 1), (kept, 0)):
            at = flip(core, k)
            out[...] = (a[0, at].astype(F32) + b[0, at].astype(F32)).astype(BF16)

    def pick(kept, got, before, own, other):
        place = Place(inner)

        def write(mine, others):
            own[...] = mine[...]
            other[...] = others[...]

        @pl.when(place.core == place.x)
        def _():
            write(kept, got)

        @pl.when(place.core != place.x)
        def _():
            write(got, kept)

    def assemble_down(p0, p1, p2, p3, out):
        place = Place(inner)
        for k, piece in enumerate((p0, p1, p2, p3)):
            y, core = flip(place.y, k // 2), flip(place.core, k % 2)
            rows = pl.ds(pl.multiple_of(core * 192, 64), 192)
            for t in range(3):
                cols = pl.ds(pl.multiple_of(y * 384 + t * 128, 128), 128)
                out[rows, cols] = piece[pl.ds(t * 192, 192), :].astype(F32)

    def assemble_last(
        a0, a1, a2, a3, p0, p1, p2, p3,
        up_o, out_o, qkv_o, gain1, shift1, qv, out_b, gain2, shift2, up_b, down_b,
    ):
        place = Place(inner)
        for k, piece in enumerate((a0, a1, a2, a3)):
            y, core = flip(place.y, k // 2), flip(place.core, k % 2)
            rows = pl.ds(pl.multiple_of(y * 48, 16), 48)
            for j in range(4):
                for t in range(3):
                    cols = pl.ds(pl.multiple_of((2 * j + core) * 384 + t * 128, 128), 128)
                    up_o[rows, cols] = piece[0, pl.ds((3 * j + t) * 48, 48), :].astype(F32)
        total = jnp.zeros((16, 128), F32)
        for k, piece in enumerate((p0, p1, p2, p3)):
            y, core = flip(place.y, k // 2), flip(place.core, k % 2)
            rows = pl.ds(pl.multiple_of(core * 48, 16), 48)
            for t in range(3):
                cols = pl.ds(pl.multiple_of(y * 384 + t * 128, 128), 128)
                out_o[rows, cols] = piece[0, pl.ds(432 + t * 48, 48), :].astype(F32)
                for n in range(3):
                    cols = pl.ds(pl.multiple_of(n * 768 + y * 384 + t * 128, 128), 128)
                    qkv_o[rows, cols] = piece[0, pl.ds((3 * n + t) * 48, 48), :].astype(F32)
            total += piece[0, pl.ds(576, 16), :].astype(F32)

        def lay(out, start, count):
            parts = [total[start + r : start + r + 1, 0:96] for r in range(count)]
            out[...] = jnp.concatenate(parts, axis=1).reshape(count * 96)

        for out, start, count in (
            (gain1, 0, 1), (shift1, 1, 1), (qv, 2, 2), (out_b, 4, 1), (gain2, 5, 1), (shift2, 6, 1),
            (up_b, 7, 4), (down_b, 11, 1),
        ):
            lay(out, start, count)

    return locals()


def build(seq_size, blk_size):
    inner = seq_size // SLOTS
    kernels = build_kernels(inner)

    def swap(x, axis, size, step):
        return lax.ppermute(x, axis, [(i, i ^ step) for i in range(size)])

    def core_swap(x):
        return swap(x, "blk", blk_size, 1)

    def y_swap(x):
        return swap(x, "blk", blk_size, 2)

    def seq_swap(x, step):
        return swap(x, "seq", seq_size, step * inner)

    def gather(x):
        across = y_swap(x)
        return x, core_swap(x), across, core_swap(across)

    def halve(name, keep, got, before, us=STEP):
        shape = ((keep.shape[0] // 2, *keep.shape[1:]), BF16)
        return call(kernels[name], (shape, shape), [VMEM, VMEM, ANY], (keep, got, before), us=us)

    def add(a, b, before, us):
        return call(kernels["add"], ((a.shape, BF16),), [VMEM, VMEM, ANY], (a, b, before), us=us)[0]

    def on_device(
        tokens, ln1_gain, ln1_bias, wqkv, bias_qv, wout, output_bias, ln2_gain, ln2_bias,
        wup, up_bias, wdown, down_bias, segment_ids, dy,
    ):
        t1 = core_swap(tokens)
        t2 = y_swap(tokens)
        hbm = in_hbm(
            dy, tokens, segment_ids, ln1_gain, ln1_bias, bias_qv, output_bias, ln2_gain, ln2_bias, down_bias,
            up_bias, wqkv, wout, wup, wdown,
        )
        near_qkv, mask, vec, up_row, t0, d0, wqkv, wout, wup, wdown = call(
            kernels["near"],
            (
                ((128, 2304), BF16), ((256, 256), F32), ((8, 768), F32), ((1, 1536), F32), ((2, 64, 768), BF16), ((2, 64, 768), BF16),
                ((768, 2304), BF16), ((768, 768), BF16), ((768, 1536), BF16), ((1536, 768), BF16),
            ),
            [VMEM] + [HBM] * 15,
            (t1, *hbm),
            [pltpu.VMEM((128, 768), BF16), pltpu.VMEM((2, 256), jnp.int32)]
            + [pltpu.VMEM((n,), BF16) for n in (768, 768, 1536, 768, 768, 768, 768, 3072)]
            + [pltpu.SemaphoreType.DMA((23,))],
            us=3.0,
        )
        near_qkv, t2 = lax.optimization_barrier((near_qkv, t2))
        rows = ((64, 768), BF16)
        t2_core, t2_away = call(kernels["split_sequences"], (rows, rows), [VMEM], (t2,), us=US)
        t3_core, t3_away = core_swap(t2_away), core_swap(t2_core)
        d_pieces = gather(d0)
        atta, attb, mine, probs = call(
            kernels["attention"],
            (((256, 384), BF16), ((256, 384), BF16), ((256, 1152), BF16), ((6, 256, 256), F32)),
            [VMEM] * 6 + [ANY],
            (near_qkv, mask, vec, t2, t3_core, wqkv, t3_away),
            [pltpu.VMEM((128, 768), BF16), pltpu.VMEM((128, 2304), BF16), pltpu.VMEM((256, 2304), BF16)],
            us=US,
        )
        chunk, half = ((4, 576, 128), BF16), ((2, 2, 576, 128), BF16)
        own = (2, 64, 768)
        att, att_other, sec, hid_core, hid_own, t3 = call(
            kernels["residual"],
            (
                ((256, 768), BF16), ((256, 768), BF16), ((512, 768), BF16), ((256, 768), F32),
                ((128, 768), F32), (own, BF16),
            ),
            [VMEM] * 11,
            (atta, attb, core_swap(atta), core_swap(attb), t0, t1, t2, t3_core, t3_away, vec, wout),
            [pltpu.VMEM((2, 256, 768), BF16), pltpu.VMEM((2, 256, 768), F32)],
            us=US,
        )
        t_pieces = t0, t1, t2, t3
        dup, act, partial, dsec, dy_rows = call(
            kernels["feed"],
            (
                ((512, 1536), BF16), ((512, 1536), BF16), ((256, 768), BF16), ((256, 768), F32),
                ((512, 768), BF16),
            ),
            [VMEM] * 8,
            (sec, up_row, *d_pieces, wup, wdown),
            us=US,
        )
        arrived = core_swap(partial)
        up_keep, up_send, down_keep, down_send, up_sums = call(
            kernels["feed_weights"],
            (chunk, chunk, half, half, ((1, 1536), F32)),
            [VMEM] * 4,
            (sec, dup, act, dy_rows),
            [pltpu.VMEM((768, 512), BF16), pltpu.VMEM((384, 512), BF16)],
            us=FILL,
        )
        exa, exb, dhid, sums, heads = call(
            kernels["attention_back"],
            (((256, 768), BF16), ((320, 768), BF16), ((64, 768), F32), ((8, 768), F32), ((8, 384), F32)),
            [VMEM] * 12,
            (dsec, arrived, hid_core, *d_pieces, vec, probs, mine, wout, up_sums),
            [pltpu.VMEM((256, 768), BF16), pltpu.VMEM((256, 384), BF16)],
            us=US,
        )
        exa_other, exb_other = core_swap(exa), core_swap(exb)
        rest = ((4, 592, 128), BF16)
        first_t, att_t, part, part_send = call(
            kernels["turn"],
            (((384, 512), BF16), ((384, 512), BF16), (own, F32), (own, BF16)),
            [VMEM] * 9 + [ANY],
            (att, att_other, *t_pieces, vec, act, wdown, sums),
            [pltpu.VMEM((2, 256, 768), BF16), pltpu.VMEM((2, 256, 768), BF16), pltpu.VMEM((768, 512), BF16)],
            us=FILL,
        )
        rest_keep, rest_send, dfirst_own, dfirst_send = call(
            kernels["attention_weights"],
            (rest, rest, (own, F32), (own, BF16)),
            [VMEM] * 13,
            (exa, exb, exa_other, exb_other, first_t, att_t, t0, t2, vec, sums, heads, up_sums, wqkv),
            [
                pltpu.VMEM((2, 256, 768), BF16), pltpu.VMEM((2, 256, 768), BF16),
                pltpu.VMEM((256, 1152), BF16), pltpu.VMEM((2, 4, 16, 128), F32),
            ],
            us=US,
        )
        down_stay, down_leave = halve("halve_z_high", down_keep, seq_swap(down_send, 2), rest_keep)
        up_stay, up_leave = halve("halve_z_low", up_keep, seq_swap(up_send, 1), down_stay)
        rest_stay, rest_leave = halve("halve_z_low", rest_keep, seq_swap(rest_send, 1), up_stay, FILL)
        up_stay, up_leave = halve("halve_z_high", up_stay, seq_swap(up_leave, 2), rest_stay)
        in_grad, block_out, mark = call(
            kernels["input_grad"],
            ((own, BF16), (own, BF16), ((8, 128), F32)),
            [VMEM] * 9 + [ANY],
            (
                t0, dfirst_own, y_swap(dfirst_send), dhid, exb_other, vec, hid_own, part,
                core_swap(part_send), up_stay,
            ),
            us=US,
        )
        piece = ((576, 128), BF16)
        down_kept, down_sent = call(
            kernels["add_split"],
            (piece, piece),
            [VMEM, VMEM, ANY],
            (down_stay, seq_swap(down_leave, 4), mark),
            us=STEP,
        )
        down_own, down_other = call(
            kernels["pick"], (piece, piece), [VMEM, VMEM, ANY], (down_kept, core_swap(down_sent), mark), us=STEP
        )
        rest_stay, rest_leave = halve("halve_z_high", rest_stay, seq_swap(rest_leave, 2), down_own)
        down_sum = add(down_own, seq_swap(down_other, 1), rest_stay, 0.001)
        (up_sum,) = call(
            kernels["add_wide"],
            (((1, 592, 128), BF16),),
            [VMEM, VMEM, ANY],
            (up_stay, seq_swap(up_leave, 4), down_sum),
            us=STEP,
        )
        rest_sum = add(rest_stay, seq_swap(rest_leave, 4), up_sum, FILL)
        up_across, down_pieces, rest_across = y_swap(up_sum), gather(down_sum), y_swap(rest_sum)
        (down_o,) = call(kernels["assemble_down"], (((384, 768), F32),), [VMEM] * 4, down_pieces, us=US)
        up_across, rest_across, down_o = lax.optimization_barrier((up_across, rest_across, down_o))
        small = [96, 96, 192, 96, 96, 96, 384, 96]
        up_o, out_o, qkv_o, *vectors = call(
            kernels["assemble_last"],
            (((96, 3072), F32), ((96, 768), F32), ((96, 2304), F32)) + tuple(((n,), F32) for n in small),
            [VMEM] * 8,
            (
                up_sum, core_swap(up_sum), up_across, core_swap(up_across),
                rest_sum, core_swap(rest_sum), rest_across, core_swap(rest_across),
            ),
            us=US,
        )
        gain1, shift1, qv, out_b, gain2, shift2, up_b, down_b = vectors
        outs = [gain1, shift1, qkv_o, qv, out_o, out_b, gain2, shift2, up_o, up_b, down_o, down_b]
        if inner > 1:
            groups = [list(range(g * inner, g * inner + inner)) for g in range(SLOTS)]
            outs = [
                lax.psum_scatter(o, "seq", scatter_dimension=0, axis_index_groups=groups, tiled=True)
                for o in outs
            ]
        return (block_out, in_grad, *outs)

    return on_device


def solution(mesh):
    data, vector, matrix = P("seq", "blk", None), P("seq"), P("seq", None)
    return jax.shard_map(
        build(mesh.shape["seq"], mesh.shape["blk"]),
        mesh=mesh,
        in_specs=(data,) + (P(),) * 12 + (matrix, data),
        out_specs=(
            data, data, vector, vector, matrix, vector, matrix, vector, vector, vector,
            matrix, vector, matrix, vector,
        ),
        check_vma=False,
    )
```

```python
import jax
import jax.numpy as jnp
from jax import lax
from jax.experimental import pallas as pl
from jax.experimental.pallas import tpu as pltpu
from jax.sharding import PartitionSpec as P

HEADS = 12
EPS = 1e-06
SLOTS = 8
F32 = jnp.float32
BF16 = jnp.bfloat16
GELU_C = 0.7978845608028654
GELU_A = 0.044715
US = 0.01
FILL = 20.0
STEP = 0.2
VMEM = pl.BlockSpec(memory_space=pltpu.VMEM)
HBM = pl.BlockSpec(memory_space=pltpu.HBM)
ANY = pl.BlockSpec(memory_space=pl.ANY)


def nn(a, b):
    return lax.dot_general(a, b, (((1,), (0,)), ((), ())), preferred_element_type=F32)


def nt(a, b):
    return lax.dot_general(a, b, (((1,), (1,)), ((), ())), preferred_element_type=F32)


def tn(a, b):
    return lax.dot_general(a, b, (((0,), (0,)), ((), ())), preferred_element_type=F32)


def standardize(x):
    centered = x - jnp.mean(x, axis=-1, keepdims=True)
    rstd = lax.rsqrt(jnp.mean(centered * centered, axis=-1, keepdims=True) + EPS)
    return centered * rstd, rstd


def norm_back(xhat, rstd, g):
    return rstd * (
        g
        - jnp.mean(g, axis=-1, keepdims=True)
        - xhat * jnp.mean(g * xhat, axis=-1, keepdims=True)
    )


def row(ref):
    return ref[...].astype(F32).reshape(1, -1)


def half_masks():
    lane = lax.broadcasted_iota(jnp.int32, (1, 128), 1)
    low = jnp.where(lane < 64, 1.0, 0.0)
    return low.astype(BF16), (1.0 - low).astype(BF16)


def flip(bit, k):
    return lax.rem(bit + k, 2)


def softmax_parts(scores, mask):
    scores = scores + mask
    e = jnp.exp(scores - jnp.max(scores, axis=-1, keepdims=True))
    return e, 1.0 / jnp.sum(e, axis=-1, keepdims=True)


def column_sum(x):
    return jnp.sum(x.astype(F32), axis=0, keepdims=True)


def call(kernel, outs, ins, args, scratch=(), limit=24, us=2.0):
    return pl.pallas_call(
        kernel,
        out_shape=tuple(jax.ShapeDtypeStruct(s, d) for s, d in outs),
        in_specs=ins,
        out_specs=tuple(VMEM for _ in outs),
        scratch_shapes=list(scratch),
        compiler_params=pltpu.CompilerParams(vmem_limit_bytes=limit * 1024 * 1024),
        cost_estimate=pl.CostEstimate(
            flops=int(us * 1e9), bytes_accessed=int(us * 1e5), transcendentals=0
        ),
        name=kernel.__name__,
    )(*args)


def in_hbm(*arrays):
    return tuple(pltpu.with_memory_space_constraint(a, pltpu.HBM) for a in arrays)


class Place:
    def __init__(self, inner):
        b = lax.axis_index("blk")
        slot = lax.axis_index("seq") // inner
        self.y, self.core = b // 2, lax.rem(b, 2)
        self.x, self.z_low, self.z_high = lax.rem(slot, 2), lax.rem(slot // 2, 2), slot // 4


def crop_mask(place, seg):
    ids = jnp.broadcast_to(seg[pl.ds(place.core, 1), :], (256, 256))
    first, second = ids[:, 0:128], ids[:, 128:256]
    tiles = jnp.where(place.y == 1, second, first), jnp.where(place.y == 1, first, second)
    tiles = [jnp.where(place.core == 1, pltpu.roll(t, 64, 1), t) for t in tiles]
    wide = jnp.concatenate(tiles, axis=1)
    return jnp.where(wide == wide.T, 0.0, -1e9)


def pick_rows(transposed, chosen, part, x_bit):
    for k in range(2):
        for z in range(4):
            start = pl.multiple_of((2 * z + flip(x_bit, k)) * 96 + part * 48, 16)
            chosen[pl.ds((4 * k + z) * 48, 48), :] = transposed[pl.ds(start, 48), :]


def put_slots(product, keep, send, offset):
    for t in range(product.shape[1] // 128):
        for z in range(4):
            tile = product[:, t * 128 : t * 128 + 128]
            keep[z, pl.ds(offset + t * 48, 48), :] = tile[z * 48 : z * 48 + 48]
            send[z, pl.ds(offset + t * 48, 48), :] = tile[192 + z * 48 : 240 + z * 48]


def gather_rows(pieces, out):
    for s in range(2):
        for p, piece in enumerate(pieces):
            out[pl.ds(s * 256 + p * 64, 64), :] = piece[s]


def both_cores(core, own, other, out):
    for p in range(4):
        out[core, pl.ds(p * 64, 64), :] = own[pl.ds(p * 64, 64), :]
        out[1 - core, pl.ds(p * 64, 64), :] = other[pl.ds((p ^ 1) * 64, 64), :]


def build_kernels(inner):
    def near(
        t1, dy_hbm, tokens_hbm, seg_hbm, g1_hbm, s1_hbm, qv_hbm, ob_hbm, g2_hbm, s2_hbm, db_hbm, ub_hbm,
        wqkv_hbm, wout_hbm, wup_hbm, wdown_hbm,
        near_o, same_o, vec_o, up_bias_o, t0, d0, wqkv, wout, wup, wdown,
        first, seg, g1, s1, qv, ob, g2, s2, db, ub, sem,
    ):
        place = Place(inner)
        pairs = [
            (g1_hbm, g1), (s1_hbm, s1), (qv_hbm, qv), (ob_hbm, ob), (g2_hbm, g2), (s2_hbm, s2),
            (db_hbm, db), (ub_hbm, ub), (seg_hbm, seg), (tokens_hbm, t0), (dy_hbm, d0),
        ]
        small = len(pairs)
        pairs += [(wqkv_hbm.at[:, pl.ds(n * 768, 768)], wqkv.at[:, pl.ds(n * 768, 768)]) for n in range(3)]
        pairs.append((wout_hbm, wout))
        for j in range(4):
            units = pl.ds(pl.multiple_of((2 * j + place.core) * 384, 128), 384)
            mine = pl.ds(j * 384, 384)
            pairs += [(wup_hbm.at[:, units], wup.at[:, mine]), (wdown_hbm.at[units, :], wdown.at[mine, :])]
        loads = [pltpu.make_async_copy(a, b, sem.at[i]) for i, (a, b) in enumerate(pairs)]
        for load in loads:
            load.start()
        for load in loads[:small]:
            load.wait()
        both = row(qv)
        for r, value in enumerate(
            (row(g1), row(s1), both[:, 0:768], both[:, 768:1536], row(ob), row(g2), row(s2), row(db))
        ):
            vec_o[r : r + 1, :] = value
        flat = row(ub)
        for j in range(4):
            start = 2 * j * 384
            up_bias_o[:, pl.ds(j * 384, 384)] = jnp.where(
                place.core == 1, flat[:, start + 384 : start + 768], flat[:, start : start + 384]
            )
        same_o[...] = crop_mask(place, seg)
        for p, t in enumerate((t0, t1)):
            xhat, _ = standardize(t[place.core].astype(F32))
            first[pl.ds(p * 64, 64), :] = (xhat * vec_o[0:1, :] + vec_o[1:2, :]).astype(BF16)
        for n in range(3):
            loads[small + n].wait()
            project(n, first[...], wqkv, vec_o, near_o)
        for load in loads[small + 3 :]:
            load.wait()

    def project(n, first, wqkv, vec, out):
        cols = pl.ds(n * 768, 768)
        value = nn(first, wqkv[:, cols])
        if n != 1:
            value = value + vec[2 + n // 2 : 3 + n // 2, :]
        value = value.astype(BF16)
        out[:, cols] = value * BF16(0.125) if n == 0 else value

    def split_sequences(tokens, mine, away):
        core = Place(inner).core
        mine[...] = tokens[core]
        away[...] = tokens[1 - core]

    def attention(near_in, mask, vec, t2, t3, wqkv, before, atta_o, attb_o, mine_o, probs_o, first, far, qkv):
        place = Place(inner)
        for p, t in enumerate((t2[place.core], t3[...])):
            xhat, _ = standardize(t.astype(F32))
            first[pl.ds(p * 64, 64), :] = (xhat * vec[0:1, :] + vec[1:2, :]).astype(BF16)
        for n in range(3):
            project(n, first[...], wqkv, vec, far)
        qkv[0:128, :] = near_in[...]
        qkv[128:256, :] = far[...]
        low, high = half_masks()
        for half in range(2):
            for j in range(HEADS // 4):
                start = flip(place.y, half) * 384 + j * 128
                cols = [pl.ds(pl.multiple_of(n * 768 + start, 128), 128) for n in range(3)]
                q, k, v = (qkv[:, c] for c in cols)
                out = None
                for h, keep in enumerate((low, high)):
                    e, scale = softmax_parts(nt(q * keep, k), mask[...])
                    if half == 0:
                        probs = e * scale
                        probs_o[2 * j + h] = probs
                        part = nn(probs.astype(BF16), v * keep)
                    else:
                        part = nn(e.astype(BF16), v * keep) * scale
                    out = part if out is None else out + part
                (atta_o, attb_o)[half][:, pl.ds(j * 128, 128)] = out.astype(BF16)
                if half == 0:
                    for n, value in enumerate((q, k, v)):
                        mine_o[:, pl.ds(n * 384 + j * 128, 128)] = value

    def residual(
        atta, attb, othera, otherb, t0, t1, t2, t3_core, t3_away, vec, wout,
        att, sec_o, hid, t3_o,
    ):
        place = Place(inner)
        for n in range(2):
            cols = pl.ds(pl.multiple_of(flip(place.y, n) * 384, 128), 384)
            att[place.core, :, cols] = (atta, attb)[n][...]
            for p in range(4):
                rows = pl.ds((p ^ 1) * 64, 64)
                att[1 - place.core, pl.ds(p * 64, 64), cols] = (othera, otherb)[n][rows, :]
        t3_o[place.core] = t3_core[...]
        t3_o[1 - place.core] = t3_away[...]
        g, b, ob = vec[5:6, :], vec[6:7, :], vec[4:5, :]
        for s in range(2):
            added = nn(att[s], wout[...]) + ob
            for p, t in enumerate((t0, t1, t2, t3_o)):
                h = t[s].astype(F32) + added[p * 64 : p * 64 + 64]
                hid[s, pl.ds(p * 64, 64), :] = h
                xhat, _ = standardize(h)
                sec_o[pl.ds(s * 256 + p * 64, 64), :] = (xhat * g + b).astype(BF16)

    def feed(sec_o, up_bias, d0, d1, d2, d3, wup, wdown, dup_o, act_o, send_o, dsec_o, dy_o, chosen_o, turned):
        place = Place(inner)
        gather_rows((d0, d1, d2, d3), dy_o)
        turned[...] = sec_o[...].T
        pick_rows(turned, chosen_o, place.y, place.x)
        for j in range(6):
            cols = pl.ds(j * 256, 256)
            for s in range(2):
                rows = pl.ds(s * 256, 256)
                up = nn(sec_o[rows, :], wup[:, cols]) + up_bias[:, cols]
                da = nt(dy_o[rows, :], wdown[cols, :])
                square = up * up
                tanh = jnp.tanh(up * (GELU_C + (GELU_C * GELU_A) * square))
                cdf = 0.5 + 0.5 * tanh
                act_o[rows, cols] = (up * cdf).astype(BF16)
                slope = cdf + (1.0 - tanh * tanh) * (
                    up * ((0.5 * GELU_C) + (1.5 * GELU_C * GELU_A) * square)
                )
                dup_o[rows, cols] = (da * slope).astype(BF16)
        away = nt(dup_o[pl.ds(pl.multiple_of((1 - place.core) * 256, 256), 256), :], wup[...])
        for p in range(4):
            send_o[pl.ds(p * 64, 64), :] = away[(p ^ 1) * 64 : (p ^ 1) * 64 + 64].astype(BF16)
        dsec_o[...] = nt(dup_o[pl.ds(pl.multiple_of(place.core * 256, 256), 256), :], wup[...])

    def feed_weights(chosen, dup, act, dy, up_keep, up_send, down_keep, down_send):
        place = Place(inner)
        for j in range(2):
            cols = pl.ds(j * 768, 768)
            put_slots(nn(chosen[...], dup[:, cols]).astype(BF16), up_keep, up_send, j * 288)
        dy_half = dy[:, pl.ds(pl.multiple_of(place.y * 384, 128), 384)]
        for k, out in enumerate((down_keep, down_send)):
            for z in range(2):
                j = 2 * z + flip(place.z_low, k)
                units = pl.ds(pl.multiple_of(j * 384, 128), 384)
                product = tn(act[:, units], dy_half).astype(BF16)
                for h in range(2):
                    for t in range(3):
                        out[z, h, pl.ds(t * 192, 192), :] = product[
                            h * 192 : h * 192 + 192, t * 128 : t * 128 + 128
                        ]

    def attention_back(
        dsec_in, got, hid_core, d0, d1, d2, d3, vec, probs_in, mine, wout, before,
        exa_o, exb_o, dhid_o, sums_o, heads_o,
        dh, datt,
    ):
        place = Place(inner)
        g = vec[5:6, :]
        sums = [jnp.zeros((1, 768), F32)] * 3
        for p, d in enumerate((d0, d1, d2, d3)):
            rows = pl.ds(p * 64, 64)
            xhat, rstd = standardize(hid_core[place.core, rows, :])
            grad = dsec_in[rows, :] + got[rows, :].astype(F32)
            dhid = d[place.core].astype(F32) + norm_back(xhat, rstd, grad * g)
            low = dhid.astype(BF16)
            dh[rows, :] = low
            if p < 2:
                sums = [a + column_sum(v) for a, v in zip(sums, (low, grad * xhat, grad))]
            if p == 0:
                dhid_o[...] = dhid
            if p == 1:
                exb_o[pl.ds(256, 64), :] = low
        for r in range(3):
            sums_o[r : r + 1, :] = sums[r]
        sums_o[3:4, :] = column_sum(d0[0]) + column_sum(d0[1])
        sums_o[4:8, :] = jnp.zeros((4, 768), F32)
        exb_o[0:256, 384:768] = dh[:, pl.ds(pl.multiple_of(place.y * 384, 128), 384)]
        datt[...] = nt(dh[...], wout[pl.ds(pl.multiple_of(place.y * 384, 128), 384), :]).astype(BF16)
        low, high = half_masks()
        for j in range(HEADS // 4):
            cols = pl.ds(j * 128, 128)
            q, k, v = (mine[:, pl.ds(n * 384 + j * 128, 128)] for n in range(3))
            da = datt[:, cols]
            dq = dk = dv = None
            for h, keep in enumerate((low, high)):
                qh, kh, dah = q * keep, k * keep, da * keep
                probs = probs_in[2 * j + h]
                dprobs = nt(dah, v)
                delta = jnp.sum(probs * dprobs, axis=-1, keepdims=True)
                ds = (probs * (dprobs - delta)).astype(BF16)
                parts = nn(ds, kh), tn(ds, qh), tn(probs.astype(BF16), dah)
                if dq is None:
                    dq, dk, dv = parts
                else:
                    dq, dk, dv = dq + parts[0], dk + parts[1], dv + parts[2]
            dq = (dq * 0.125).astype(BF16)
            dv = dv.astype(BF16)
            exa_o[:, cols] = dq
            exa_o[:, pl.ds(384 + j * 128, 128)] = dk.astype(BF16)
            exb_o[0:256, cols] = dv
            heads_o[0:1, cols] = column_sum(dq)
            heads_o[1:2, cols] = column_sum(dv)
        heads_o[2:8, :] = jnp.zeros((6, 384), F32)

    def turn(
        att, t0, t1, t2, t3, params, act, wdown, dup, before,
        first_o, att_o, part_o, part_send, bias_o,
        first, turned,
    ):
        place = Place(inner)
        bias_o[...] = column_sum(dup[0:128, :]) + column_sum(dup[256:384, :])
        for s in range(2):
            for p, t in enumerate((t0, t1, t2, t3)):
                xhat, _ = standardize(t[s].astype(F32))
                first[s, pl.ds(p * 64, 64), :] = (xhat * params[0:1, :] + params[1:2, :]).astype(BF16)
        for source, chosen in ((first, first_o), (att, att_o)):
            for s in range(2):
                turned[:, pl.ds(s * 256, 256)] = source[s].T
            pick_rows(turned, chosen, place.core, place.x)
        for s in range(2):
            part = nn(act[pl.ds(s * 256, 128), :], wdown[...])
            part_o[s] = part[0:64]
            part_send[s] = part[64:128].astype(BF16)

    def attention_weights(
        owna, ownb, othera, otherb, first, att, t0, t2, params, sums, heads, up_sums, wqkv,
        keep, send, dfirst_own, dfirst_send,
        exa, exb, rows, vec,
    ):
        place = Place(inner)
        weights = [wqkv[:, pl.ds(pl.multiple_of(n * 768 + place.y * 384, 128), 384)] for n in range(3)]
        both_cores(place.core, owna, othera, exa)
        both_cores(place.core, ownb, otherb, exb)
        for chosen, source, lanes, offset in (
            (first, exa, slice(0, 768), 0),
            (first, exb, slice(0, 384), 288),
            (att, exb, slice(384, 768), 432),
        ):
            product = nn(chosen[:, 0:256], source[0, :, lanes]) + nn(chosen[:, 256:512], source[1, :, lanes])
            put_slots(product.astype(BF16), keep, send, offset)
        dgain = jnp.zeros((1, 768), F32)
        dshift = jnp.zeros((1, 768), F32)
        pieces = [(s, p, t) for s in range(2) for p, t in ((0, t0), (2, t2))]
        for i, (s, p, t) in enumerate(pieces):
            rows[pl.ds(i * 64, 64), 0:768] = exa[s, pl.ds(p * 64, 64), :]
            rows[pl.ds(i * 64, 64), 768:1152] = exb[s, pl.ds(p * 64, 64), 0:384]
        parts = sum(nt(rows[:, pl.ds(n * 384, 384)], weights[n]) for n in range(3))
        for i, (s, p, t) in enumerate(pieces):
            part = parts[i * 64 : i * 64 + 64]
            xhat, _ = standardize(t[s].astype(F32))
            dgain += column_sum(part * xhat)
            dshift += column_sum(part)
            if p == 0:
                dfirst_own[s] = part
            else:
                dfirst_send[s] = part.astype(BF16)
        vec[...] = jnp.zeros_like(vec)
        for s in range(SLOTS):
            k, z = flip(place.x, s % 2), s // 2
            lanes = slice(s * 96, s * 96 + 96)
            vec[k, z, 0:1, 0:96] = dgain[:, lanes]
            vec[k, z, 1:2, 0:96] = dshift[:, lanes]
            vec[k, z, 4:5, 0:96] = sums[0:1, lanes]
            vec[k, z, 5:6, 0:96] = sums[1:2, lanes]
            vec[k, z, 6:7, 0:96] = sums[2:3, lanes]
            vec[k, z, 11:12, 0:96] = sums[3:4, lanes]
        for h in range(2):
            for n in range(2):
                for r in range(2):
                    start = h * 192 + r * 96
                    vec[flip(place.x, h), 2 * n + place.y, 2 + r : 3 + r, 0:96] = heads[
                        n : n + 1, start : start + 96
                    ]
        for z in range(4):
            for r in range(4):
                start = z * 384 + r * 96
                vec[flip(place.x, place.core), z, 7 + r : 8 + r, 0:96] = up_sums[:, start : start + 96]
        for z in range(4):
            keep[z, pl.ds(576, 16), :] = vec[0, z].astype(BF16)
            send[z, pl.ds(576, 16), :] = vec[1, z].astype(BF16)

    def hold(received, part_got, before, mark):
        mark[...] = jnp.zeros_like(mark)

    def input_grad(
        tokens, dfirst, received, dhid, other, vec, hid_own, part, part_got, before,
        out, block_o, mark,
    ):
        mark[...] = jnp.zeros_like(mark)
        place = Place(inner)

        def write(s, residual):
            xhat, rstd = standardize(tokens[s].astype(F32))
            grad = dfirst[s] + received[s].astype(F32)
            out[s] = (residual + norm_back(xhat, rstd, grad * vec[0:1, :])).astype(BF16)

        write(place.core, dhid[...])
        write(1 - place.core, other[256:320, :].astype(F32))
        for s in range(2):
            added = part[s] + part_got[s].astype(F32) + vec[7:8, :]
            block_o[s] = (hid_own[s, 0:64, :] + added).astype(BF16)

    def halve_z_low(keep, got, before, stay, leave):
        halve(Place(inner).z_low, keep, got, stay, leave)

    def halve_z_high(keep, got, before, stay, leave):
        halve(Place(inner).z_high, keep, got, stay, leave)

    def halve(bit, keep, got, stay, leave):
        for i in range(stay.shape[0]):
            for out, k in ((leave, 1), (stay, 0)):
                at = 2 * i + flip(bit, k)
                out[i] = (keep[at].astype(F32) + got[at].astype(F32)).astype(BF16)

    def add(a, b, before, out):
        out[...] = (a[...].astype(F32) + b[...].astype(F32)).astype(BF16)

    def add_wide(a, b, before, out):
        rows = a.shape[1]
        out[:, 0:rows, :] = (a[...].astype(F32) + b[...].astype(F32)).astype(BF16)
        out[:, rows : out.shape[1], :] = jnp.zeros((1, out.shape[1] - rows, 128), BF16)

    def add_split(a, b, before, kept, sent):
        core = Place(inner).core
        for out, k in ((sent, 1), (kept, 0)):
            at = flip(core, k)
            out[...] = (a[0, at].astype(F32) + b[0, at].astype(F32)).astype(BF16)

    def pick(kept, got, before, own, other):
        place = Place(inner)

        def write(mine, others):
            own[...] = mine[...]
            other[...] = others[...]

        @pl.when(place.core == place.x)
        def _():
            write(kept, got)

        @pl.when(place.core != place.x)
        def _():
            write(got, kept)

    def assemble_down(p0, p1, p2, p3, out):
        place = Place(inner)
        for k, piece in enumerate((p0, p1, p2, p3)):
            y, core = flip(place.y, k // 2), flip(place.core, k % 2)
            rows = pl.ds(pl.multiple_of(core * 192, 64), 192)
            for t in range(3):
                cols = pl.ds(pl.multiple_of(y * 384 + t * 128, 128), 128)
                out[rows, cols] = piece[pl.ds(t * 192, 192), :].astype(F32)

    def assemble_last(
        a0, a1, a2, a3, p0, p1, p2, p3,
        up_o, out_o, qkv_o, gain1, shift1, qv, out_b, gain2, shift2, up_b, down_b,
    ):
        place = Place(inner)
        for k, piece in enumerate((a0, a1, a2, a3)):
            y, core = flip(place.y, k // 2), flip(place.core, k % 2)
            rows = pl.ds(pl.multiple_of(y * 48, 16), 48)
            for j in range(4):
                for t in range(3):
                    cols = pl.ds(pl.multiple_of((2 * j + core) * 384 + t * 128, 128), 128)
                    up_o[rows, cols] = piece[0, pl.ds((3 * j + t) * 48, 48), :].astype(F32)
        total = jnp.zeros((16, 128), F32)
        for k, piece in enumerate((p0, p1, p2, p3)):
            y, core = flip(place.y, k // 2), flip(place.core, k % 2)
            rows = pl.ds(pl.multiple_of(core * 48, 16), 48)
            for t in range(3):
                cols = pl.ds(pl.multiple_of(y * 384 + t * 128, 128), 128)
                out_o[rows, cols] = piece[0, pl.ds(432 + t * 48, 48), :].astype(F32)
                for n in range(3):
                    cols = pl.ds(pl.multiple_of(n * 768 + y * 384 + t * 128, 128), 128)
                    qkv_o[rows, cols] = piece[0, pl.ds((3 * n + t) * 48, 48), :].astype(F32)
            total += piece[0, pl.ds(576, 16), :].astype(F32)

        def lay(out, start, count):
            parts = [total[start + r : start + r + 1, 0:96] for r in range(count)]
            out[...] = jnp.concatenate(parts, axis=1).reshape(count * 96)

        for out, start, count in (
            (gain1, 0, 1), (shift1, 1, 1), (qv, 2, 2), (out_b, 4, 1), (gain2, 5, 1), (shift2, 6, 1),
            (up_b, 7, 4), (down_b, 11, 1),
        ):
            lay(out, start, count)

    return locals()


def build(seq_size, blk_size):
    inner = seq_size // SLOTS
    kernels = build_kernels(inner)

    def swap(x, axis, size, step):
        return lax.ppermute(x, axis, [(i, i ^ step) for i in range(size)])

    def core_swap(x):
        return swap(x, "blk", blk_size, 1)

    def y_swap(x):
        return swap(x, "blk", blk_size, 2)

    def seq_swap(x, step):
        return swap(x, "seq", seq_size, step * inner)

    def gather(x):
        across = y_swap(x)
        return x, core_swap(x), across, core_swap(across)

    def halve(name, keep, got, before, us=STEP):
        shape = ((keep.shape[0] // 2, *keep.shape[1:]), BF16)
        return call(kernels[name], (shape, shape), [VMEM, VMEM, ANY], (keep, got, before), us=us)

    def add(a, b, before, us):
        return call(kernels["add"], ((a.shape, BF16),), [VMEM, VMEM, ANY], (a, b, before), us=us)[0]

    def on_device(
        tokens, ln1_gain, ln1_bias, wqkv, bias_qv, wout, output_bias, ln2_gain, ln2_bias,
        wup, up_bias, wdown, down_bias, segment_ids, dy,
    ):
        t1 = core_swap(tokens)
        t2 = y_swap(tokens)
        hbm = in_hbm(
            dy, tokens, segment_ids, ln1_gain, ln1_bias, bias_qv, output_bias, ln2_gain, ln2_bias, down_bias,
            up_bias, wqkv, wout, wup, wdown,
        )
        near_qkv, mask, vec, up_row, t0, d0, wqkv, wout, wup, wdown = call(
            kernels["near"],
            (
                ((128, 2304), BF16), ((256, 256), F32), ((8, 768), F32), ((1, 1536), F32), ((2, 64, 768), BF16), ((2, 64, 768), BF16),
                ((768, 2304), BF16), ((768, 768), BF16), ((768, 1536), BF16), ((1536, 768), BF16),
            ),
            [VMEM] + [HBM] * 15,
            (t1, *hbm),
            [pltpu.VMEM((128, 768), BF16), pltpu.VMEM((2, 256), jnp.int32)]
            + [pltpu.VMEM((n,), BF16) for n in (768, 768, 1536, 768, 768, 768, 768, 3072)]
            + [pltpu.SemaphoreType.DMA((23,))],
            us=3.0,
        )
        near_qkv, t2 = lax.optimization_barrier((near_qkv, t2))
        rows = ((64, 768), BF16)
        t2_core, t2_away = call(kernels["split_sequences"], (rows, rows), [VMEM], (t2,), us=US)
        t3_core, t3_away = core_swap(t2_away), core_swap(t2_core)
        d_pieces = gather(d0)
        atta, attb, mine, probs = call(
            kernels["attention"],
            (((256, 384), BF16), ((256, 384), BF16), ((256, 1152), BF16), ((6, 256, 256), F32)),
            [VMEM] * 6 + [ANY],
            (near_qkv, mask, vec, t2, t3_core, wqkv, t3_away),
            [pltpu.VMEM((128, 768), BF16), pltpu.VMEM((128, 2304), BF16), pltpu.VMEM((256, 2304), BF16)],
            us=US,
        )
        chunk, half = ((4, 576, 128), BF16), ((2, 2, 576, 128), BF16)
        own = (2, 64, 768)
        att, sec, hid, t3 = call(
            kernels["residual"],
            (((2, 256, 768), BF16), ((512, 768), BF16), ((2, 256, 768), F32), (own, BF16)),
            [VMEM] * 11,
            (atta, attb, core_swap(atta), core_swap(attb), t0, t1, t2, t3_core, t3_away, vec, wout),
            us=US,
        )
        t_pieces = t0, t1, t2, t3
        dup, act, partial, dsec, dy_rows, second_t = call(
            kernels["feed"],
            (
                ((512, 1536), BF16), ((512, 1536), BF16), ((256, 768), BF16), ((256, 768), F32),
                ((512, 768), BF16), ((384, 512), BF16),
            ),
            [VMEM] * 8,
            (sec, up_row, *d_pieces, wup, wdown),
            [pltpu.VMEM((768, 512), BF16)],
            us=US,
        )
        arrived = core_swap(partial)
        up_keep, up_send, down_keep, down_send = call(
            kernels["feed_weights"],
            (chunk, chunk, half, half),
            [VMEM] * 4,
            (second_t, dup, act, dy_rows),
            us=FILL,
        )
        exa, exb, dhid, sums, heads = call(
            kernels["attention_back"],
            (((256, 768), BF16), ((320, 768), BF16), ((64, 768), F32), ((8, 768), F32), ((8, 384), F32)),
            [VMEM] * 11 + [ANY],
            (dsec, arrived, hid, *d_pieces, vec, probs, mine, wout, down_keep),
            [pltpu.VMEM((256, 768), BF16), pltpu.VMEM((256, 384), BF16)],
            us=US,
        )
        exa_other, exb_other = core_swap(exa), core_swap(exb)
        rest = ((4, 592, 128), BF16)
        first_t, att_t, part, part_send, up_sums = call(
            kernels["turn"],
            (((384, 512), BF16), ((384, 512), BF16), (own, F32), (own, BF16), ((1, 1536), F32)),
            [VMEM] * 9 + [ANY],
            (att, *t_pieces, vec, act, wdown, dup, sums),
            [pltpu.VMEM((2, 256, 768), BF16), pltpu.VMEM((768, 512), BF16)],
            us=FILL,
        )
        rest_keep, rest_send, dfirst_own, dfirst_send = call(
            kernels["attention_weights"],
            (rest, rest, (own, F32), (own, BF16)),
            [VMEM] * 13,
            (exa, exb, exa_other, exb_other, first_t, att_t, t0, t2, vec, sums, heads, up_sums, wqkv),
            [
                pltpu.VMEM((2, 256, 768), BF16), pltpu.VMEM((2, 256, 768), BF16),
                pltpu.VMEM((256, 1152), BF16), pltpu.VMEM((2, 4, 16, 128), F32),
            ],
            us=US,
        )
        down_stay, down_leave = halve("halve_z_high", down_keep, seq_swap(down_send, 2), rest_keep)
        up_stay, up_leave = halve("halve_z_low", up_keep, seq_swap(up_send, 1), down_stay)
        rest_stay, rest_leave = halve("halve_z_low", rest_keep, seq_swap(rest_send, 1), up_stay, FILL)
        up_stay, up_leave = halve("halve_z_high", up_stay, seq_swap(up_leave, 2), rest_stay)
        received, part_got = y_swap(dfirst_send), core_swap(part_send)
        (mark,) = call(
            kernels["hold"], (((8, 128), F32),), [ANY] * 3, (received, part_got, up_stay), us=US
        )
        piece = ((576, 128), BF16)
        down_kept, down_sent = call(
            kernels["add_split"],
            (piece, piece),
            [VMEM, VMEM, ANY],
            (down_stay, seq_swap(down_leave, 4), mark),
            us=STEP,
        )
        down_own, down_other = call(
            kernels["pick"], (piece, piece), [VMEM, VMEM, ANY], (down_kept, core_swap(down_sent), mark), us=STEP
        )
        rest_stay, rest_leave = halve("halve_z_high", rest_stay, seq_swap(rest_leave, 2), down_own)
        down_sum = add(down_own, seq_swap(down_other, 1), rest_stay, 0.001)
        in_grad, block_out, late = call(
            kernels["input_grad"],
            ((own, BF16), (own, BF16), ((8, 128), F32)),
            [VMEM] * 9 + [ANY],
            (t0, dfirst_own, received, dhid, exb_other, vec, hid, part, part_got, down_sum),
            us=US,
        )
        (up_sum,) = call(
            kernels["add_wide"],
            (((1, 592, 128), BF16),),
            [VMEM, VMEM, ANY],
            (up_stay, seq_swap(up_leave, 4), late),
            us=STEP,
        )
        rest_sum = add(rest_stay, seq_swap(rest_leave, 4), up_sum, FILL)
        up_across, down_pieces, rest_across = y_swap(up_sum), gather(down_sum), y_swap(rest_sum)
        (down_o,) = call(kernels["assemble_down"], (((384, 768), F32),), [VMEM] * 4, down_pieces, us=US)
        up_across, rest_across, down_o = lax.optimization_barrier((up_across, rest_across, down_o))
        small = [96, 96, 192, 96, 96, 96, 384, 96]
        up_o, out_o, qkv_o, *vectors = call(
            kernels["assemble_last"],
            (((96, 3072), F32), ((96, 768), F32), ((96, 2304), F32)) + tuple(((n,), F32) for n in small),
            [VMEM] * 8,
            (
                up_sum, core_swap(up_sum), up_across, core_swap(up_across),
                rest_sum, core_swap(rest_sum), rest_across, core_swap(rest_across),
            ),
            us=US,
        )
        gain1, shift1, qv, out_b, gain2, shift2, up_b, down_b = vectors
        outs = [gain1, shift1, qkv_o, qv, out_o, out_b, gain2, shift2, up_o, up_b, down_o, down_b]
        if inner > 1:
            groups = [list(range(g * inner, g * inner + inner)) for g in range(SLOTS)]
            outs = [
                lax.psum_scatter(o, "seq", scatter_dimension=0, axis_index_groups=groups, tiled=True)
                for o in outs
            ]
        return (block_out, in_grad, *outs)

    return on_device


def solution(mesh):
    data, vector, matrix = P("seq", "blk", None), P("seq"), P("seq", None)
    return jax.shard_map(
        build(mesh.shape["seq"], mesh.shape["blk"]),
        mesh=mesh,
        in_specs=(data,) + (P(),) * 12 + (matrix, data),
        out_specs=(
            data, data, vector, vector, matrix, vector, matrix, vector, vector, vector,
            matrix, vector, matrix, vector,
        ),
        check_vma=False,
    )
```
